32 devices in a mesh: edge: 8 (over z, y), grp: 4 (over x, core).
Axes of the slice: x: 2, y: 2, z: 4, core: 2. Of those that a mesh axis runs over, the one named last changes fastest.
Arguments:
- atoms: bfloat16 [8192, 9, 128], P(('edge', 'grp')), may hold values from -4 to 4
- neighbours: int32 [8192, 64], P(('edge', 'grp')), may hold values from 0 to 8191, as said below
- live_mask: int32 [8192, 64], P(('edge', 'grp')), may hold values from 0 to 1, as said below
- distances: float32 [8192, 64], P(('edge', 'grp')), may hold values from 0.8 to 4.8
- w_iso1: bfloat16 [128, 128], replicated, may hold values from -0.5 to 0.5
- w_anti1: bfloat16 [128, 128], replicated, may hold values from -0.5 to 0.5
- w_sym1: bfloat16 [128, 128], replicated, may hold values from -0.5 to 0.5
- w_rad1: bfloat16 [32, 128], replicated, may hold values from -2 to 2
- b_rad1: bfloat16 [128], replicated, may hold values from -3 to 3
- w_rad2: bfloat16 [128, 256], replicated, may hold values from -0.75 to 0.75
- b_rad2: bfloat16 [256], replicated, may hold values from -3 to 3
- w_rad3: bfloat16 [256, 384], replicated, may hold values from -0.5 to 0.5
- b_rad3: bfloat16 [384], replicated, may hold values from -3 to 3
- w_iso2: bfloat16 [128, 128], replicated, may hold values from -1.5 to 1.5
- w_anti2: bfloat16 [128, 128], replicated, may hold values from -1.5 to 1.5
- w_sym2: bfloat16 [128, 128], replicated, may hold values from -1.5 to 1.5
- out_grad: bfloat16 [8192, 9, 128], P(('edge', 'grp')), may hold values from -6 to 6
Outputs:
- updated: bfloat16 [8192, 9, 128], P(('edge', 'grp'))
- grad_atoms: float32 [8192, 9, 128], P(('edge', 'grp'))
- grad_w_iso1: float32 [128, 128], replicated
- grad_w_anti1: float32 [128, 128], replicated
- grad_w_sym1: float32 [128, 128], replicated
- grad_w_rad1: float32 [32, 128], replicated
- grad_b_rad1: float32 [128], replicated
- grad_w_rad2: float32 [128, 256], replicated
- grad_b_rad2: float32 [256], replicated
- grad_w_rad3: float32 [256, 384], replicated
- grad_b_rad3: float32 [384], replicated
- grad_w_iso2: float32 [128, 128], replicated
- grad_w_anti2: float32 [128, 128], replicated
- grad_w_sym2: float32 [128, 128], replicated
The draws below stay inside these ranges and needn't reach their ends.
Inputs may be any that keep to these rules, and one draw needn't show every extreme that they name: neighbours[i, s] is an atom of the molecule of atom i; molecules are runs of consecutive atoms of at most 256, so the difference of neighbours[i, s] and i is under 256 in size, and 255 occurs; a slot with live_mask 0 holds i itself. `live_mask`: in each row the live slots come first, at least one.
All inputs are finite; a program needn't handle non-finite values.
Results may differ from the reference program's by a relative error of at most 0.012.
Values may be sent and summed in bfloat16 or wider, within the bound.
No kernel may reach another device: no remote copies, remote signals or barrier semaphores. Data moves between devices by JAX's collectives and lax.ppermute only.
A program may use at most 192 MiB of HBM per device.

```python
import math
import jax
import jax.numpy as jnp
from jax import lax

CHAN = 128
BASIS = 32
SLOTS = 64
ATOM_DEV = 256
MOL_MOST = 256
ATOMS = 8192


def neighbour_plan(key):
    folded = jax.random.fold_in(key, 17)
    key_sizes, key_pick, key_offset, key_live = jax.random.split(folded, 4)
    smallest = min(10, MOL_MOST // 2)
    number = ATOMS // smallest + 1
    mol_sizes = jax.random.randint(key_sizes, (number,), smallest, MOL_MOST + 1)
    chosen = jax.random.randint(key_pick, (), 0, ATOMS // MOL_MOST)
    mol_sizes = jnp.where(jnp.arange(number) == chosen, MOL_MOST, mol_sizes)
    mol_ends = jnp.cumsum(mol_sizes)
    mol_starts = mol_ends - mol_sizes
    positions = jnp.arange(ATOMS)
    molecule = jnp.searchsorted(mol_ends, positions, side='right').astype(jnp.int32)
    first_atom = jnp.take(mol_starts, molecule)
    past_end = jnp.minimum(jnp.take(mol_ends, molecule), ATOMS)
    mol_span = past_end - first_atom
    offsets = jax.random.randint(key_offset, (ATOMS, SLOTS), 0, 1 << 20)
    partner = first_atom[:, None] + offsets % jnp.maximum(mol_span - 1, 1)[:, None]
    partner = jnp.where(partner >= positions[:, None], partner + 1, partner)
    partner = jnp.minimum(partner, past_end[:, None] - 1)
    counts = jax.random.randint(key_live, (ATOMS,), max(SLOTS // 3, 1), SLOTS + 1)
    slot_index = jnp.arange(SLOTS)
    is_live = slot_index[None, :] < counts[:, None]
    partners = jnp.where(is_live, partner, positions[:, None])
    head_atom = jnp.take(mol_starts, chosen)
    partners = partners.at[head_atom, 0].set(head_atom + MOL_MOST - 1)
    return (partners.astype(jnp.int32), is_live.astype(jnp.int32))


def draw_neighbours(key, part):
    partners, is_live = neighbour_plan(key)
    return partners


def draw_live_mask(key, part):
    partners, is_live = neighbour_plan(key)
    return is_live


def block_scale(key, shape, cuts, low, top_value):
    gain, own = 1.0, jax.random.fold_in(key, 6)
    for axis_at, parts in cuts:
        heights = jnp.exp(jax.random.uniform(jax.random.fold_in(own, axis_at), (parts,), jnp.float32, low / len(cuts), top_value / len(cuts)))
        gain = gain * jnp.repeat(heights, shape[axis_at] // parts).reshape([-1 if axis == axis_at else 1 for axis in range(len(shape))])
    return gain


def gaussian(key, shape, deviation, reach, shards=(), kind=jnp.bfloat16):
    values = deviation * jax.random.normal(key, shape, jnp.float32)
    if shards:
        values = values * block_scale(key, shape, shards, -0.22, 0.18)
    return jnp.clip(values, -reach, reach).astype(kind)


def setup_inputs(seed: int = 0) -> dict:
    keys = jax.random.split(jax.random.key(seed), 18)
    atoms = gaussian(keys[0], (ATOMS, 9, CHAN), 0.5, 4.0, ((0, 32),))
    neighbours = draw_neighbours(jax.random.fold_in(keys[17], 71), 0)
    live_mask = draw_live_mask(jax.random.fold_in(keys[17], 71), 0)
    distances = jnp.clip(0.8 + 4 * jax.random.uniform(keys[3], (ATOMS, SLOTS), jnp.float32) ** block_scale(keys[3], (ATOMS, SLOTS), ((0, 32),), -0.2, 0.2), 0.8, 4.8)
    w_iso1 = gaussian(keys[4], (CHAN, CHAN), CHAN ** -0.5, 0.5)
    w_anti1 = gaussian(keys[5], (CHAN, CHAN), CHAN ** -0.5, 0.5)
    w_sym1 = gaussian(keys[6], (CHAN, CHAN), CHAN ** -0.5, 0.5)
    w_rad1 = gaussian(keys[7], (BASIS, CHAN), (BASIS // 4) ** -0.5, 2.0)
    b_rad1 = gaussian(keys[8], (CHAN,), 0.5, 3.0)
    w_rad2 = gaussian(keys[9], (CHAN, 2 * CHAN), (CHAN // 2) ** -0.5, 0.75)
    b_rad2 = gaussian(keys[10], (2 * CHAN,), 0.5, 3.0)
    w_rad3 = gaussian(keys[11], (2 * CHAN, 3 * CHAN), CHAN ** -0.5, 0.5)
    b_rad3 = gaussian(keys[12], (3 * CHAN,), 0.5, 3.0)
    w_iso2 = gaussian(keys[13], (CHAN, CHAN), (CHAN // 8) ** -0.5, 1.5)
    w_anti2 = gaussian(keys[14], (CHAN, CHAN), (CHAN // 8) ** -0.5, 1.5)
    w_sym2 = gaussian(keys[15], (CHAN, CHAN), (CHAN // 8) ** -0.5, 1.5)
    out_grad = gaussian(keys[16], (ATOMS, 9, CHAN), 1.0, 6.0, ((0, 32),))
    return dict(atoms=atoms, neighbours=neighbours, live_mask=live_mask, distances=distances, w_iso1=w_iso1, w_anti1=w_anti1, w_sym1=w_sym1, w_rad1=w_rad1, b_rad1=b_rad1, w_rad2=w_rad2, b_rad2=b_rad2, w_rad3=w_rad3, b_rad3=b_rad3, w_iso2=w_iso2, w_anti2=w_anti2, w_sym2=w_sym2, out_grad=out_grad)


@jax.custom_vjp
def low(v):
    return lax.optimization_barrier(v.astype(jnp.bfloat16)).astype(jnp.float32)

@jax.custom_vjp
def low_back(v):
    return v

def low_keep(v):
    return (low(v), None)

def low_pass(kept, grad):
    return (grad,)

def back_keep(v):
    return (v, None)

def back_low(kept, grad):
    return (low(grad),)
low.defvjp(low_keep, low_pass)
low_back.defvjp(back_keep, back_low)
CUTOFF = 5.0
PRECISE = lax.Precision.HIGHEST

def flip_pairs(tensor):
    leading = tensor.shape[0]
    return jnp.swapaxes(tensor.reshape(leading, 3, 3, -1), 1, 2).reshape(leading, 9, -1)

def split_parts(tensor):
    unit_diag = jnp.eye(3, dtype=jnp.float32).reshape(1, 9, 1)
    thirds = (tensor[:, 0] + tensor[:, 4] + tensor[:, 8]) / 3.0
    isotropic = thirds[:, None, :] * unit_diag
    flipped = flip_pairs(tensor)
    antisym = 0.5 * (tensor - flipped)
    symmetric = 0.5 * (tensor + flipped) - isotropic
    return (isotropic, antisym, symmetric)

def tensor_product(left_mat, right_mat):
    leading = left_mat.shape[0]
    left_view = left_mat.reshape(leading, 3, 3, 1, -1)
    right_view = right_mat.reshape(leading, 1, 3, 3, -1)
    return lax.optimization_barrier(jnp.sum(left_view * right_view, axis=2)).reshape(leading, 9, -1)

def channel_mix(tensor_parts, weight):
    return jnp.einsum('nmc,cd->nmd', tensor_parts, weight, precision=PRECISE)

def radial_basis(lengths, basis_count):
    centres = jnp.arange(basis_count, dtype=jnp.float32) * (CUTOFF / (basis_count - 1))
    sharpness = 0.5 * ((basis_count - 1) / CUTOFF) ** 2
    return jnp.exp(-sharpness * (lengths[..., None] - centres) ** 2)

def smooth_cut(lengths):
    return 0.5 * (jnp.cos(math.pi * lengths / CUTOFF) + 1.0)

def forward(atoms_float, params, neighbours, live_float, distances):
    w_iso1, w_anti1, w_sym1, w_rad1, b_rad1, w_rad2, b_rad2, w_rad3, b_rad3, w_iso2, w_anti2, w_sym2 = params
    scale_in = lax.optimization_barrier(jnp.sum(atoms_float * atoms_float, axis=1, keepdims=True)) + 1.0
    normed = atoms_float / scale_in
    iso_in, anti_in, sym_in = split_parts(normed)
    mixed_rows = channel_mix(low(iso_in), w_iso1) + channel_mix(low(anti_in), w_anti1) + channel_mix(low(sym_in), w_sym1)
    mixed_rows = low(low_back(mixed_rows))
    channels = mixed_rows.shape[2]
    block_count = ATOMS // ATOM_DEV

    def block_messages(block_args):
        block_links, block_live, block_dist = block_args
        basis_vals = low(radial_basis(block_dist, BASIS))
        hidden1 = low_back(jnp.einsum('akr,rc->akc', basis_vals, w_rad1, precision=PRECISE) + b_rad1)
        active1 = low(jax.nn.silu(hidden1))
        hidden2 = low_back(jnp.einsum('akc,cd->akd', active1, w_rad2, precision=PRECISE) + b_rad2)
        active2 = low(jax.nn.silu(hidden2))
        hidden3 = low_back(jnp.einsum('akc,cd->akd', active2, w_rad3, precision=PRECISE) + b_rad3)
        factors = jax.nn.silu(hidden3) * (smooth_cut(block_dist) * block_live)[..., None]
        sources = jnp.take(mixed_rows, block_links.reshape(-1), axis=0)
        iso_src, anti_src, sym_src = split_parts(sources)
        block_shape = (block_links.shape[0], block_links.shape[1], 9, channels)
        summed = factors[:, :, None, :channels] * iso_src.reshape(block_shape)
        summed = summed + factors[:, :, None, channels:2 * channels] * anti_src.reshape(block_shape)
        summed = summed + factors[:, :, None, 2 * channels:] * sym_src.reshape(block_shape)
        return lax.optimization_barrier(jnp.sum(summed, axis=1))
    block_args = (neighbours.reshape(block_count, ATOM_DEV, SLOTS), live_float.reshape(block_count, ATOM_DEV, SLOTS), distances.reshape(block_count, ATOM_DEV, SLOTS))
    messages = lax.map(jax.checkpoint(block_messages), block_args).reshape(ATOMS, 9, channels)
    messages = low_back(messages)
    paired = tensor_product(mixed_rows, messages) + tensor_product(messages, mixed_rows)
    scale_mid = lax.optimization_barrier(jnp.sum(paired * paired, axis=1, keepdims=True)) + 1.0
    iso_mid, anti_mid, sym_mid = split_parts(paired)
    update = channel_mix(low(iso_mid / scale_mid), w_iso2) + channel_mix(low(anti_mid / scale_mid), w_anti2) + channel_mix(low(sym_mid / scale_mid), w_sym2)
    update = low_back(update)
    return normed + update + tensor_product(update, update)

def reference(atoms, neighbours, live_mask, distances, w_iso1, w_anti1, w_sym1, w_rad1, b_rad1, w_rad2, b_rad2, w_rad3, b_rad3, w_iso2, w_anti2, w_sym2, out_grad):
    params = (w_iso1.astype(jnp.float32), w_anti1.astype(jnp.float32), w_sym1.astype(jnp.float32), w_rad1.astype(jnp.float32), b_rad1.astype(jnp.float32), w_rad2.astype(jnp.float32), b_rad2.astype(jnp.float32), w_rad3.astype(jnp.float32), b_rad3.astype(jnp.float32), w_iso2.astype(jnp.float32), w_anti2.astype(jnp.float32), w_sym2.astype(jnp.float32))
    live_float = live_mask.astype(jnp.float32)

    def wrapped(atoms_float, weights):
        return forward(atoms_float, weights, neighbours, live_float, distances)
    result, pullback = jax.vjp(wrapped, atoms.astype(jnp.float32), params)
    grad_atoms, grad_params = pullback(out_grad.astype(jnp.float32))
    return (result.astype(jnp.bfloat16), grad_atoms, grad_params[0], grad_params[1], grad_params[2], grad_params[3], grad_params[4], grad_params[5], grad_params[6], grad_params[7], grad_params[8], grad_params[9], grad_params[10], grad_params[11])
```

```python
import functools
import math

import jax
import jax.numpy as jnp
from jax import lax
from jax.experimental import pallas as pl
from jax.experimental.pallas import tpu as pltpu
from jax.sharding import PartitionSpec as P

MOL_MOST = 256
CUTOFF = 5.0
LANES = 128
GROUP = 8
WINDOW = 256
KIND = (0, 1, 1, 1, 2, 2, 2, 2, 2)
AXES = ("edge", "grp")
F32 = jnp.float32
BF16 = jnp.bfloat16


def col(c):
    return slice(c * LANES, (c + 1) * LANES)


def to_matrix(coords):
    t, a01, a02, a12, s01, s02, s12, s00, s11 = coords
    return [
        [t + s00, s01 + a01, s02 + a02],
        [s01 - a01, t + s11, s12 + a12],
        [s02 - a02, s12 - a12, t - s00 - s11],
    ]


def primal(m):
    t = (m[0][0] + m[1][1] + m[2][2]) * (1.0 / 3.0)
    return [
        t,
        0.5 * (m[0][1] - m[1][0]),
        0.5 * (m[0][2] - m[2][0]),
        0.5 * (m[1][2] - m[2][1]),
        0.5 * (m[0][1] + m[1][0]),
        0.5 * (m[0][2] + m[2][0]),
        0.5 * (m[1][2] + m[2][1]),
        m[0][0] - t,
        m[1][1] - t,
    ]


def dual(m):
    return [
        m[0][0] + m[1][1] + m[2][2],
        m[0][1] - m[1][0],
        m[0][2] - m[2][0],
        m[1][2] - m[2][1],
        m[0][1] + m[1][0],
        m[0][2] + m[2][0],
        m[1][2] + m[2][1],
        m[0][0] - m[2][2],
        m[1][1] - m[2][2],
    ]


def dual_of_primal(c):
    return [3.0 * c[0]] + [2.0 * v for v in c[1:7]] + [2.0 * c[7] + c[8], 2.0 * c[8] + c[7]]


def primal_of_dual(d):
    third = 1.0 / 3.0
    return (
        [d[0] * third]
        + [0.5 * v for v in d[1:7]]
        + [(2.0 * d[7] - d[8]) * third, (2.0 * d[8] - d[7]) * third]
    )


def product(a, b):
    return [
        [a[p][0] * b[0][q] + a[p][1] * b[1][q] + a[p][2] * b[2][q] for q in range(3)]
        for p in range(3)
    ]


def add(a, b):
    return [[a[p][q] + b[p][q] for q in range(3)] for p in range(3)]


def both_ways(a, b):
    return add(product(a, b), product(b, a))


def flip(m):
    return [[m[q][p] for q in range(3)] for p in range(3)]


def flat(m):
    return [m[p][q] for p in range(3) for q in range(3)]


def square(parts):
    return [list(parts[0:3]), list(parts[3:6]), list(parts[6:9])]


def total(values):
    out = values[0]
    for v in values[1:]:
        out = out + v
    return out


def dot(a, b):
    return jnp.dot(a, b, preferred_element_type=F32)


def dot_first(a, b):
    return lax.dot_general(a, b, (((0,), (0,)), ((), ())), preferred_element_type=F32)


def dot_last(a, b):
    return lax.dot_general(a, b, (((1,), (1,)), ((), ())), preferred_element_type=F32)


def by_kind(coords, weights, multiply):
    rows = coords[0].shape[0]
    out = []
    for kind, (lo, hi) in enumerate(((0, 1), (1, 4), (4, 9))):
        stacked = jnp.concatenate([v.astype(BF16) for v in coords[lo:hi]], axis=0)
        result = multiply(stacked, weights[kind])
        out += [result[n * rows : (n + 1) * rows] for n in range(hi - lo)]
    return out


def kind_grads(parts, gradients):
    out = []
    for lo, hi in ((0, 1), (1, 4), (4, 9)):
        left = jnp.concatenate([v.astype(BF16) for v in parts[lo:hi]], axis=0)
        right = jnp.concatenate([v.astype(BF16) for v in gradients[lo:hi]], axis=0)
        out.append(dot_first(left, right))
    return out


def half_silu(u):
    t = jnp.tanh(u)
    v = u * t
    return u + v, (1.0 + t) * (1.0 + u - v)


def parts_kernel(atoms_ref, out_ref):
    values = [atoms_ref[:, col(c)].astype(F32) for c in range(9)]
    scale = 1.0 / (1.0 + total([v * v for v in values]))
    coords = primal(square([v * scale for v in values]))
    for c in range(9):
        out_ref[:, col(c)] = coords[c].astype(BF16)


def main_kernel(
    win_ref, low_ref, own_ref, high_ref, atoms_ref, outgrad_ref, rows_ref,
    w1_ref, w2_ref, b2_ref, w3_ref, b3_ref,
    iso1_ref, anti1_ref, sym1_ref, iso2_ref, anti2_ref, sym2_ref,
    upd_ref, f_ref, gmp_ref, gfp_ref, d3_ref, d2_ref, d1_ref, dw2_ref,
    table, x_s, basis_s, a1_s, l1_s, a2_s, l2_s, l3_s, msg_s, gmd_s,
):
    step = pl.program_id(0)
    chunks, _, edges = rows_ref.shape
    halo = low_ref.shape[0]
    own = own_ref.shape[0]
    atoms = upd_ref.shape[0]
    pairs = edges // 16

    @pl.when(step == 0)
    def _():
        weights = (iso1_ref[...], anti1_ref[...], sym1_ref[...])
        place = 0
        for ref in (low_ref, own_ref, high_ref):
            for c in range(9):
                table[place : place + ref.shape[0], col(c)] = dot(
                    ref[:, col(c)], weights[KIND[c]]
                ).astype(BF16)
            place += ref.shape[0]
        table[place:, :] = jnp.zeros((table.shape[0] - place, table.shape[1]), BF16)
        d3_ref[...] = jnp.zeros_like(d3_ref)
        d2_ref[...] = jnp.zeros_like(d2_ref)
        d1_ref[...] = jnp.zeros_like(d1_ref)
        dw2_ref[...] = jnp.zeros_like(dw2_ref)

    def forward_chunk(j, carry):
        base = pl.multiple_of(j * edges, edges)
        here = pl.ds(base, edges)
        cols = jnp.transpose(rows_ref[j])
        dist, gate, link = cols[:, 0:1], cols[:, 1:2], cols[:, 2:3]
        first = win_ref[step * chunks + j, 0]
        count = win_ref[step * chunks + j, 1]
        near = lax.broadcasted_iota(jnp.int32, (edges, WINDOW), 1).astype(F32)

        def picked(w, accumulate):
            start = pl.multiple_of(first + w * WINDOW, 16)
            hot = (link - start.astype(F32) == near).astype(BF16)
            for lo in range(0, 9 * LANES, 2 * LANES):
                hi = min(lo + 2 * LANES, 9 * LANES)
                got = dot(hot, table[pl.ds(start, WINDOW), lo:hi]).astype(BF16)
                if accumulate:
                    got = x_s[here, lo:hi] + got
                x_s[here, lo:hi] = got

        picked(0, False)

        @pl.loop(1, count)
        def _(w):
            picked(w, True)

        lane = lax.broadcasted_iota(jnp.int32, (edges, LANES), 1)
        off = dist - lane.astype(F32) * (CUTOFF / 31.0)
        basis = jnp.exp(off * off * (-0.5 * (31.0 / CUTOFF) ** 2))
        basis = jnp.where(lane < 32, basis, jnp.where(lane == 32, 1.0, 0.0)).astype(BF16)
        basis_s[here, :] = basis
        act, slope = half_silu(dot(basis, w1_ref[...]))
        act1 = act.astype(BF16)
        a1_s[here, :] = act1
        l1_s[here, :] = slope.astype(BF16)
        act, slope = half_silu(dot(act1, w2_ref[...]) + b2_ref[...])
        act2 = act.astype(BF16)
        a2_s[here, :] = act2
        l2_s[here, :] = slope.astype(BF16)
        act, slope = half_silu(dot(act2, w3_ref[...]) + b3_ref[...])
        factors = act * gate
        f_ref[here, :] = factors.astype(BF16)
        l3_s[here, :] = (slope * (0.5 * gate)).astype(BF16)
        for c in range(9):
            terms = factors[:, col(KIND[c])] * x_s[here, col(c)].astype(F32)
            msg_s[pl.ds(pl.multiple_of(j * GROUP, GROUP), GROUP), col(c)] = jnp.sum(
                terms.reshape(edges // GROUP, GROUP, LANES), axis=0
            )
        return carry

    lax.fori_loop(0, chunks, forward_chunk, 0)

    weights2 = (iso2_ref[...], anti2_ref[...], sym2_ref[...])
    at = pl.ds(pl.multiple_of(halo + step * atoms, 16), atoms)
    mixed = to_matrix([table[at, col(c)].astype(F32) for c in range(9)])
    messages = to_matrix([msg_s[:, col(c)] for c in range(9)])
    paired = both_ways(mixed, messages)
    inverse = 1.0 / (1.0 + total([v * v for v in flat(paired)]))
    pair_coords = primal(paired)
    mid = [v * inverse for v in pair_coords]
    update = to_matrix(by_kind(mid, weights2, dot))
    values = [atoms_ref[:, col(c)].astype(F32) for c in range(9)]
    inverse_in = 1.0 / (1.0 + total([v * v for v in values]))
    squared = flat(product(update, update))
    for c, (v, u, s) in enumerate(zip(values, flat(update), squared)):
        upd_ref[:, col(c)] = (v * inverse_in + u + s).astype(BF16)
    out_grad = square([outgrad_ref[:, col(c)].astype(F32) for c in range(9)])
    grad_update = add(out_grad, both_ways(out_grad, flip(update)))
    grad_dual = [v.astype(BF16) for v in dual(grad_update)]
    for kind, grad in enumerate(kind_grads(mid, grad_dual)):
        dw2_ref[kind * LANES : (kind + 1) * LANES, :] += grad
    mid_dual = by_kind(grad_dual, weights2, dot_last)
    projected = total([a * b for a, b in zip(mid_dual, pair_coords)]) * (2.0 * inverse * inverse)
    grad_paired = to_matrix([v * inverse for v in primal_of_dual(mid_dual)])
    grad_paired = [
        [grad_paired[p][q] - paired[p][q] * projected for q in range(3)] for p in range(3)
    ]
    grad_messages = both_ways(flip(mixed), grad_paired)
    from_pair = primal(both_ways(grad_paired, flip(messages)))
    for c in range(9):
        gfp_ref[:, col(c)] = from_pair[c]
    for c, (a, b) in enumerate(zip(dual(grad_messages), primal(grad_messages))):
        for ref, v in ((gmd_s, a), (gmp_ref, b)):
            twice = v.reshape(chunks, 1, GROUP, LANES)
            twice = jnp.concatenate([twice, twice], axis=1).reshape(2 * atoms, LANES)
            ref[:, col(c)] = twice.astype(BF16)

    def backward_chunk(j, carry):
        base = pl.multiple_of(j * edges, edges)
        here = pl.ds(base, edges)
        two = pl.ds(pl.multiple_of(j * 2 * GROUP, 2 * GROUP), 2 * GROUP)
        terms = [
            x_s[here, col(c)].reshape(pairs, 16, LANES) * gmd_s[two, col(c)][None]
            for c in range(9)
        ]
        grads = [terms[0], total(terms[1:4]), total(terms[4:9])]
        grad3 = jnp.concatenate([g.reshape(edges, LANES) for g in grads], axis=1) * l3_s[here, :]
        ones = jnp.ones((16, edges), BF16)
        act2 = jnp.concatenate([jnp.transpose(a2_s[here, :]), ones], axis=0)
        d3_ref[...] += dot(act2, grad3)
        grad2 = dot_last(grad3, w3_ref[...]).astype(BF16) * l2_s[here, :]
        act1 = jnp.concatenate([jnp.transpose(a1_s[here, :]), ones], axis=0)
        d2_ref[...] += dot(act1, grad2)
        grad1 = dot_last(grad2, w2_ref[...]).astype(BF16) * l1_s[here, :]
        d1_ref[...] += dot(jnp.transpose(basis_s[here, :]), grad1)
        return carry

    lax.fori_loop(0, chunks, backward_chunk, 0)


def scatter_kernel(
    win_ref, low_ref, own_ref, high_ref, rows_ref, f_ref, gmp_ref, gfp_ref,
    rim_low_ref, own_out_ref, rim_high_ref, dw1_ref,
    spread,
):
    step = pl.program_id(0)
    chunks, _, edges = rows_ref.shape
    halo = low_ref.shape[0]
    own = own_ref.shape[0]
    pairs = edges // 16

    @pl.when(step == 0)
    def _():
        spread[...] = jnp.zeros_like(spread)
        spread[halo : halo + own, :] = gfp_ref[...]

    def chunk(j, carry):
        here = pl.ds(pl.multiple_of(j * edges, edges), edges)
        two = pl.ds(pl.multiple_of(j * 2 * GROUP, 2 * GROUP), 2 * GROUP)
        link = rows_ref[j][2:3, :]
        first = win_ref[step * chunks + j, 0]
        count = win_ref[step * chunks + j, 1]
        factors = [f_ref[here, col(k)].reshape(pairs, 16, LANES) for k in range(3)]
        values = jnp.concatenate(
            [
                (factors[KIND[c]] * gmp_ref[two, col(c)][None]).reshape(edges, LANES)
                for c in range(9)
            ],
            axis=1,
        )
        near = lax.broadcasted_iota(jnp.int32, (WINDOW, edges), 0).astype(F32)

        @pl.loop(0, count)
        def _(w):
            start = pl.multiple_of(first + w * WINDOW, 16)
            hot = (link - start.astype(F32) == near).astype(BF16)
            spread[pl.ds(start, WINDOW), :] += dot(hot, values)

        return carry

    lax.fori_loop(0, chunks, chunk, 0)

    @pl.when(step == pl.num_programs(0) - 1)
    def _():
        grads = [None] * 3
        place = 0
        for ref, out in ((low_ref, rim_low_ref), (own_ref, own_out_ref), (high_ref, rim_high_ref)):
            rows = ref.shape[0]
            coords = [spread[place : place + rows, col(c)] for c in range(9)]
            for c in range(9):
                out[:, col(c)] = coords[c].astype(out.dtype)
            fresh = kind_grads([ref[:, col(c)] for c in range(9)], dual_of_primal(coords))
            grads = [n if o is None else o + n for o, n in zip(grads, fresh)]
            place += rows
        for kind in range(3):
            dw1_ref[kind * LANES : (kind + 1) * LANES, :] = grads[kind]


def final_kernel(
    own_ref, above_ref, below_ref, atoms_ref, outgrad_ref, iso1_ref, anti1_ref, sym1_ref, out_ref
):
    weights = (iso1_ref[...], anti1_ref[...], sym1_ref[...])
    grad_mixed = [
        own_ref[:, col(c)] + above_ref[:, col(c)].astype(F32) + below_ref[:, col(c)].astype(F32)
        for c in range(9)
    ]
    back = flat(to_matrix(by_kind(grad_mixed, weights, dot_last)))
    values = [atoms_ref[:, col(c)].astype(F32) for c in range(9)]
    inverse = 1.0 / (1.0 + total([v * v for v in values]))
    grad = [outgrad_ref[:, col(c)].astype(F32) + back[c] for c in range(9)]
    along = total([g * v for g, v in zip(grad, values)]) * (2.0 * inverse)
    for c in range(9):
        out_ref[:, col(c)] = (grad[c] - values[c] * along) * inverse


def whole(shape):
    return pl.BlockSpec(shape, lambda *_: (0,) * len(shape))


def block(shape):
    return pl.BlockSpec(shape, lambda i, *_: (i,) + (0,) * (len(shape) - 1))


def shape_of(shape, kind):
    return jax.ShapeDtypeStruct(shape, kind)


def reduce_everywhere(value, axes):
    peers = math.prod(lax.axis_size(a) for a in axes)
    rows = value.shape[0]
    share = -(-rows // (peers * 8)) * 8
    padded = jnp.pad(value, ((0, share * peers - rows), (0, 0))).astype(BF16)
    mine = lax.all_to_all(padded.reshape(peers, share, -1), axes, 0, 0, tiled=True)
    summed = jnp.sum(mine.astype(F32), axis=0).astype(BF16)
    copies = jnp.broadcast_to(summed[None], (peers,) + summed.shape)
    back = lax.all_to_all(copies, axes, 0, 0, tiled=True)
    return back.reshape(share * peers, -1)[:rows].astype(F32)


def local(
    atoms, neighbours, live_mask, distances,
    w_iso1, w_anti1, w_sym1, w_rad1, b_rad1, w_rad2, b_rad2, w_rad3, b_rad3,
    w_iso2, w_anti2, w_sym2, out_grad,
):
    rows, _, channels = atoms.shape
    slots = neighbours.shape[1]
    halo = MOL_MOST
    wide = 9 * channels
    ext = rows + 2 * halo
    edges = GROUP * slots
    chunk_count = rows // GROUP
    steps = 4
    chunks = chunk_count // steps
    block_atoms = rows // steps
    block_edges = block_atoms * slots
    vmem = 56 * 1024 * 1024
    me = lax.axis_index(AXES)
    peers = math.prod(lax.axis_size(a) for a in AXES)
    up = [(i, i + 1) for i in range(peers - 1)]
    down = [(i + 1, i) for i in range(peers - 1)]

    atoms_flat = atoms.reshape(rows, wide)
    out_grad_flat = out_grad.reshape(rows, wide)
    own = pl.pallas_call(
        parts_kernel,
        out_shape=shape_of((rows, wide), BF16),
        compiler_params=pltpu.CompilerParams(vmem_limit_bytes=vmem),
        name="parts",
    )(atoms_flat)
    low = lax.ppermute(own, AXES, up)
    high = lax.ppermute(own, AXES, down)

    links = neighbours - (me * rows - halo)
    gating = 0.5 * (jnp.cos(math.pi * distances / CUTOFF) + 1.0) * live_mask.astype(F32)

    def as_rows(v):
        return jnp.swapaxes(v.reshape(chunk_count, GROUP, slots), 1, 2).reshape(
            chunk_count, 1, edges
        )

    edge_rows = jnp.concatenate(
        [as_rows(distances), as_rows(gating), as_rows(links.astype(F32))]
        + [jnp.zeros((chunk_count, 5, edges), F32)],
        axis=1,
    )
    grouped = links.reshape(chunk_count, edges)
    first = jnp.min(grouped, axis=1) // 16 * 16
    count = (jnp.max(grouped, axis=1) - first) // WINDOW + 1
    windows = jnp.stack([first, count], axis=1)

    w1_ext = jnp.zeros((LANES, channels), F32)
    w1_ext = w1_ext.at[: w_rad1.shape[0]].set(0.5 * w_rad1.astype(F32))
    w1_ext = w1_ext.at[w_rad1.shape[0]].set(0.5 * b_rad1.astype(F32)).astype(BF16)
    w2_half = (0.5 * w_rad2.astype(F32)).astype(BF16)
    w3_half = (0.5 * w_rad3.astype(F32)).astype(BF16)
    b2_half = 0.5 * b_rad2.astype(F32)[None]
    b3_half = 0.5 * b_rad3.astype(F32)[None]

    mid_width, last_width = w_rad2.shape[1], w_rad3.shape[1]
    small = whole((channels, channels))
    smem = pl.BlockSpec(memory_space=pltpu.SMEM)
    updated, factors, gmp, gfp, d3, d2, d1, dw2 = pl.pallas_call(
        main_kernel,
        grid=(steps,),
        in_specs=[
            smem, whole((halo, wide)), whole((rows, wide)), whole((halo, wide)),
            block((block_atoms, wide)), block((block_atoms, wide)), block((chunks, 8, edges)),
            whole((LANES, channels)), whole((channels, mid_width)), whole((1, mid_width)),
            whole((mid_width, last_width)), whole((1, last_width)),
            small, small, small, small, small, small,
        ],
        out_specs=[
            block((block_atoms, wide)), block((block_edges, last_width)),
            block((2 * block_atoms, wide)), block((block_atoms, wide)),
            whole((mid_width + 16, last_width)), whole((channels + 16, mid_width)),
            whole((LANES, channels)), whole((3 * channels, channels)),
        ],
        out_shape=[
            shape_of((rows, wide), BF16), shape_of((rows * slots, last_width), BF16),
            shape_of((2 * rows, wide), BF16), shape_of((rows, wide), F32),
            shape_of((mid_width + 16, last_width), F32), shape_of((channels + 16, mid_width), F32),
            shape_of((LANES, channels), F32), shape_of((3 * channels, channels), F32),
        ],
        scratch_shapes=[
            pltpu.VMEM((ext + WINDOW, wide), BF16),
            pltpu.VMEM((block_edges, wide), BF16),
            pltpu.VMEM((block_edges, LANES), BF16),
            pltpu.VMEM((block_edges, channels), BF16),
            pltpu.VMEM((block_edges, channels), BF16),
            pltpu.VMEM((block_edges, mid_width), BF16),
            pltpu.VMEM((block_edges, mid_width), BF16),
            pltpu.VMEM((block_edges, last_width), BF16),
            pltpu.VMEM((block_atoms, wide), F32),
            pltpu.VMEM((2 * block_atoms, wide), BF16),
        ],
        compiler_params=pltpu.CompilerParams(vmem_limit_bytes=vmem),
        name="main",
    )(
        windows, low, own, high, atoms_flat, out_grad_flat, edge_rows,
        w1_ext, w2_half, b2_half, w3_half, b3_half,
        w_iso1, w_anti1, w_sym1, w_iso2, w_anti2, w_sym2,
    )

    rim_low, own_grad, rim_high, dw1 = pl.pallas_call(
        scatter_kernel,
        grid=(steps,),
        in_specs=[
            smem, whole((halo, wide)), whole((rows, wide)), whole((halo, wide)),
            block((chunks, 8, edges)), block((block_edges, last_width)),
            block((2 * block_atoms, wide)), whole((rows, wide)),
        ],
        out_specs=[
            whole((halo, wide)), whole((rows, wide)), whole((halo, wide)),
            whole((3 * channels, channels)),
        ],
        out_shape=[
            shape_of((halo, wide), BF16), shape_of((rows, wide), F32),
            shape_of((halo, wide), BF16), shape_of((3 * channels, channels), F32),
        ],
        scratch_shapes=[pltpu.VMEM((ext + WINDOW, wide), F32)],
        compiler_params=pltpu.CompilerParams(vmem_limit_bytes=vmem),
        name="scatter",
    )(windows, low, own, high, edge_rows, factors, gmp, gfp)

    above = lax.ppermute(rim_low, AXES, down)
    below = lax.ppermute(rim_high, AXES, up)

    grad_atoms = pl.pallas_call(
        final_kernel,
        out_shape=shape_of((rows, wide), F32),
        compiler_params=pltpu.CompilerParams(vmem_limit_bytes=vmem),
        name="final",
    )(own_grad, above, below, atoms_flat, out_grad_flat, w_iso1, w_anti1, w_sym1)

    basis_count = w_rad1.shape[0]
    pieces = [dw1, dw2, d1[:basis_count], d1[basis_count : basis_count + 1]]
    pieces += [d2[:channels, col(n)] for n in range(mid_width // LANES)]
    pieces += [d2[channels : channels + 1, col(n)] for n in range(mid_width // LANES)]
    pieces += [d3[:mid_width, col(n)] for n in range(last_width // LANES)]
    pieces += [d3[mid_width : mid_width + 1, col(n)] for n in range(last_width // LANES)]
    summed = reduce_everywhere(jnp.concatenate(pieces, axis=0), AXES)
    place = 0

    def take(count, lanes):
        nonlocal place
        got = []
        for _ in range(lanes // LANES):
            got.append(summed[place : place + count])
            place += count
        return jnp.concatenate(got, axis=1) if len(got) > 1 else got[0]

    small_grads = [take(channels, LANES) for _ in range(6)]
    g_w1 = take(basis_count, LANES)
    g_b1 = take(1, LANES)[0]
    g_w2 = take(channels, mid_width)
    g_b2 = take(1, mid_width)[0]
    g_w3 = take(mid_width, last_width)
    g_b3 = take(1, last_width)[0]
    return (
        updated.reshape(atoms.shape),
        grad_atoms.reshape(atoms.shape),
        *small_grads[:3],
        g_w1, g_b1, g_w2, g_b2, g_w3, g_b3,
        *small_grads[3:],
    )


def solution(mesh):
    split3 = P(AXES, None, None)
    split2 = P(AXES, None)
    return jax.shard_map(
        local,
        mesh=mesh,
        in_specs=(split3, split2, split2, split2) + (P(),) * 12 + (split3,),
        out_specs=(split3, split3) + (P(),) * 12,
        check_vma=False,
    )
```

```python
import functools
import math

import jax
import jax.numpy as jnp
from jax import lax
from jax.experimental import pallas as pl
from jax.experimental.pallas import tpu as pltpu
from jax.sharding import PartitionSpec as P

MOL_MOST = 256
CUTOFF = 5.0
LANES = 128
GROUP = 8
BASES = 32
UNROLL = 2
PAIRS = ((0, 1), (2, 3), (4, 5), (6, 7), (8,))
SCHEDULE = "".join(n + s for n in "01" for s in "HaTDb0G1cWd2E3eF4xVyUz")
WINDOW = 256
KIND = (0, 1, 1, 1, 2, 2, 2, 2, 2)
AXES = ("edge", "grp")
F32 = jnp.float32
BF16 = jnp.bfloat16


def col(c):
    return slice(c * LANES, (c + 1) * LANES)


def to_matrix(coords):
    t, a01, a02, a12, s01, s02, s12, s00, s11 = coords
    return [
        [t + s00, s01 + a01, s02 + a02],
        [s01 - a01, t + s11, s12 + a12],
        [s02 - a02, s12 - a12, t - s00 - s11],
    ]


def primal(m):
    t = (m[0][0] + m[1][1] + m[2][2]) * (1.0 / 3.0)
    return [
        t,
        0.5 * (m[0][1] - m[1][0]),
        0.5 * (m[0][2] - m[2][0]),
        0.5 * (m[1][2] - m[2][1]),
        0.5 * (m[0][1] + m[1][0]),
        0.5 * (m[0][2] + m[2][0]),
        0.5 * (m[1][2] + m[2][1]),
        m[0][0] - t,
        m[1][1] - t,
    ]


def dual(m):
    return [
        m[0][0] + m[1][1] + m[2][2],
        m[0][1] - m[1][0],
        m[0][2] - m[2][0],
        m[1][2] - m[2][1],
        m[0][1] + m[1][0],
        m[0][2] + m[2][0],
        m[1][2] + m[2][1],
        m[0][0] - m[2][2],
        m[1][1] - m[2][2],
    ]


def primal_of_dual(d):
    third = 1.0 / 3.0
    return (
        [d[0] * third]
        + [0.5 * v for v in d[1:7]]
        + [(2.0 * d[7] - d[8]) * third, (2.0 * d[8] - d[7]) * third]
    )


def product(a, b):
    return [
        [a[p][0] * b[0][q] + a[p][1] * b[1][q] + a[p][2] * b[2][q] for q in range(3)]
        for p in range(3)
    ]


def add(a, b):
    return [[a[p][q] + b[p][q] for q in range(3)] for p in range(3)]


def both_ways(a, b):
    return add(product(a, b), product(b, a))


def flip(m):
    return [[m[q][p] for q in range(3)] for p in range(3)]


def flat(m):
    return [m[p][q] for p in range(3) for q in range(3)]


def square(parts):
    return [list(parts[0:3]), list(parts[3:6]), list(parts[6:9])]


def total(values):
    out = values[0]
    for v in values[1:]:
        out = out + v
    return out


def dot(a, b):
    return jnp.dot(a, b, preferred_element_type=F32)


def dot_first(a, b):
    return lax.dot_general(a, b, (((0,), (0,)), ((), ())), preferred_element_type=F32)


def dot_last(a, b):
    return lax.dot_general(a, b, (((1,), (1,)), ((), ())), preferred_element_type=F32)


def stack(values):
    return jnp.concatenate([v.astype(BF16) for v in values], axis=0)


def pieces_of(value, rows):
    return [value[n * rows : (n + 1) * rows] for n in range(value.shape[0] // rows)]


def rounded_parts(m):
    coords = primal(m)
    return [v.astype(BF16) for v in coords + [-coords[7] - coords[8]]]


def parts_in(atoms_ref, at):
    values = [atoms_ref[c, at : at + 64, :].astype(F32) for c in range(9)]
    scale = 1.0 / (1.0 + total([v * v for v in values]))
    return rounded_parts(square([v * scale for v in values]))


def mix_parts(parts, weights):
    rows = parts[0].shape[0]
    t, a01, a02, a12, s01, s02, s12, s00, s11, s22 = (
        pieces_of(dot(parts[0], weights[0]), rows)
        + pieces_of(dot(stack(parts[1:4]), weights[1]), rows)
        + pieces_of(dot(stack(parts[4:10]), weights[2]), rows)
    )
    return [
        [t + s00, s01 + a01, s02 + a02],
        [s01 - a01, t + s11, s12 + a12],
        [s02 - a02, s12 - a12, t + s22],
    ]


def seen_by_kind(grad):
    diagonal = [grad[0][0], grad[1][1], grad[2][2]]
    skew = [grad[0][1], grad[1][0], grad[0][2], grad[2][0], grad[1][2], grad[2][1]]
    return [stack(v) for v in (diagonal, skew, skew + diagonal)]


def back_parts(grad, weights):
    rows = grad[0][0].shape[0]
    seen = seen_by_kind(grad)
    iso, anti, sym = (pieces_of(dot_last(v, w), rows) for v, w in zip(seen, weights))
    coords = [
        iso[0] + iso[1] + iso[2],
        anti[0] - anti[1], anti[2] - anti[3], anti[4] - anti[5],
        sym[0] + sym[1], sym[2] + sym[3], sym[4] + sym[5],
        sym[6] - sym[8], sym[7] - sym[8],
    ]
    return seen, coords


def weight_grads(parts, seen):
    p = parts
    lefts = (
        [p[0]] * 3,
        [p[1], -p[1], p[2], -p[2], p[3], -p[3]],
        [p[4], p[4], p[5], p[5], p[6], p[6], p[7], p[8], p[9]],
    )
    return [dot_first(stack(left), right) for left, right in zip(lefts, seen)]


def half_silu(u):
    t = jnp.tanh(u)
    p = 1.0 + t
    act = u * p
    return act, p + act * (1.0 - t)


SLOPE3, ACT2, SLOPE2 = slice(0, 384), slice(384, 640), slice(640, 896)
ACT1, SLOPE1 = slice(896, 1024), slice(1024, 1152)
KEPT = 1152
HALF = 64
AHEAD = 6

ORDER = ((0, 1), (1, 0), (0, 2), (2, 0), (1, 2), (2, 1), (0, 0), (1, 1), (2, 2))


class Network:
    def __init__(self, rows, out, factors, basis, at, refs):
        self.rows, self.out, self.factors, self.basis, self.refs = rows, out, factors, basis, refs
        edges = rows.shape[1]
        self.here = pl.ds(pl.multiple_of(at * edges, edges), edges)
        self.half = pl.ds(pl.multiple_of(at * (edges // 2), edges // 2), edges // 2)

    def run(self):
        self.layer1()
        self.active1()
        self.layer2()
        self.active2()
        self.layer3()
        for kind in range(3):
            self.active3(kind)

    def layer1(self):
        cols = jnp.transpose(self.rows)
        self.gate = cols[:, 1:2]
        deep = cols.shape[0] // 2
        lane = lax.broadcasted_iota(jnp.int32, (deep, LANES), 1)
        dist = jnp.where(lane < HALF, cols[:deep, 0:1], cols[deep:, 0:1])
        lane = lane % HALF
        off = dist - lane.astype(F32) * (CUTOFF / 31.0)
        basis = jnp.exp(off * off * (-0.5 * (31.0 / CUTOFF) ** 2))
        last = jnp.where(lane == BASES, 1.0, 0.0)
        basis = jnp.where(lane < BASES, basis, last).astype(BF16)
        self.basis[self.half, :] = basis
        inner = dot(basis, self.refs[0][...])
        self.inner = jnp.concatenate([inner[:, :LANES], inner[:, LANES:]], axis=0)

    def active1(self):
        act, slope = half_silu(self.inner)
        self.act = act.astype(BF16)
        self.out[self.here, ACT1] = self.act
        self.out[self.here, SLOPE1] = slope.astype(BF16)

    def layer2(self):
        one = lax.broadcasted_iota(jnp.int32, self.act.shape, 1) == 0
        one = jnp.where(one, 1.0, 0.0).astype(BF16)
        self.inner = dot(jnp.concatenate([self.act, one], axis=1), self.refs[1][...])

    def active2(self):
        act, slope = half_silu(self.inner)
        self.act = act.astype(BF16)
        self.out[self.here, ACT2] = self.act
        self.out[self.here, SLOPE2] = slope.astype(BF16)

    def layer3(self):
        self.inner = dot(self.act, self.refs[2][...])

    def active3(self, kind):
        act, slope = half_silu(self.inner[:, col(kind)] + self.refs[3][:, col(kind)])
        self.factors[self.here, col(kind)] = act * self.gate
        self.out[self.here, col(kind)] = (slope * (0.5 * self.gate)).astype(BF16)


def halve_weights(w1_ref, w2_ref, w3_ref, bias_ref, w1_s, w2_s, w3_s, b3_s):
    half = 0.5 * bias_ref[...].astype(F32)

    def biased(weights, bias, rows):
        below = lax.broadcasted_iota(jnp.int32, (rows - weights.shape[0], bias.shape[1]), 0)
        bias = jnp.where(below == 0, bias, 0.0)
        return jnp.concatenate([0.5 * weights.astype(F32), bias], axis=0).astype(BF16)

    w1_s[...] = jnp.zeros_like(w1_s)
    first = biased(w1_ref[...], half[0:1], HALF)
    w1_s[:HALF, :LANES] = first
    w1_s[HALF:, LANES:] = first
    wide2 = jnp.concatenate([half[1:2], half[2:3]], axis=1)
    w2_s[...] = biased(w2_ref[...], wide2, w2_s.shape[0])
    w3_s[...] = (0.5 * w3_ref[...].astype(F32)).astype(BF16)
    b3_s[...] = jnp.concatenate([half[3:4], half[4:5], half[5:6]], axis=1)


def network_kernel(
    rows_ref, w1_raw, w2_raw, w3_raw, bias_ref, out_ref, fac_ref, basis_ref, w1_s, w2_s, w3_s, b3_s
):
    net_refs = (w1_s, w2_s, w3_s, b3_s)

    @pl.when(pl.program_id(0) == 0)
    def _():
        halve_weights(w1_raw, w2_raw, w3_raw, bias_ref, *net_refs)

    Network(rows_ref[0], out_ref, fac_ref, basis_ref, 0, net_refs).run()


def window_key(link, first, w):
    start = first + w * WINDOW
    base = pl.multiple_of(first // 16 * 16 + w * WINDOW, 16)
    off = first % 16
    rel = link - start.astype(F32)
    key = rel + off.astype(F32)
    key = jnp.where(key >= WINDOW, key - WINDOW, key)
    key = jnp.where(jnp.logical_and(rel >= 0, rel < WINDOW), key, -1.0)
    return key, base, off


def main_kernel(
    win_ref, low_ref, own_ref, high_ref, outgrad_ref, rows_ref,
    w1_raw, w2_raw, w3_raw, bias_ref,
    iso1_ref, anti1_ref, sym1_ref, iso2_ref, anti2_ref, sym2_ref, net_first, fac_first, basis_first,
    upd_ref, rim_low_ref, own_out_ref, rim_high_ref, grads_ref,
    table, net_a, net_b, fac_a, fac_b, basis_a, basis_b, x_s, msg_s, gm_s, spread,
    d3_ref, d2_ref, d1_ref, dw2_ref, w1_ref, w2_ref, w3_ref, b3_ref, sems,
):
    step = pl.program_id(0)
    steps = pl.num_programs(0)
    edges = rows_ref.shape[2]
    halo = low_ref.shape[1]
    atoms = upd_ref.shape[1]
    chunks = atoms // GROUP
    slots = edges // GROUP
    pairs = edges // 16
    wide = 9 * LANES
    radial = (w1_ref, w2_ref, w3_ref, b3_ref)

    def fetches(j):
        here = pl.ds(pl.multiple_of(j * edges, edges), edges)
        half = pl.ds(pl.multiple_of(j * (edges // 2), edges // 2), edges // 2)
        return (
            pltpu.make_async_copy(net_first.at[here], net_a.at[here], sems.at[j, 0]),
            pltpu.make_async_copy(fac_first.at[here], fac_a.at[here], sems.at[j, 1]),
            pltpu.make_async_copy(basis_first.at[half], basis_a.at[half], sems.at[j, 2]),
        )

    @pl.when(step == 0)
    def _():
        for j in range(AHEAD):
            for copy in fetches(j):
                copy.start()
        halve_weights(w1_raw, w2_raw, w3_raw, bias_ref, *radial)
        weights = (iso1_ref[...], anti1_ref[...], sym1_ref[...])
        place = 0
        for ref in (low_ref, own_ref, high_ref):
            for at in range(0, ref.shape[1], 64):
                here = slice(place + at, place + at + 64)
                mixed = mix_parts(parts_in(ref, at), weights)
                for n, (p, q) in enumerate(ORDER):
                    table[here, col(n)] = mixed[p][q].astype(BF16)
            place += ref.shape[1]
        table[place:, :] = jnp.zeros((table.shape[0] - place, wide), BF16)
        d3_ref[...] = jnp.zeros_like(d3_ref)
        d2_ref[...] = jnp.zeros_like(d2_ref)
        d1_ref[...] = jnp.zeros_like(d1_ref)
        dw2_ref[...] = jnp.zeros_like(dw2_ref)
        spread[...] = jnp.zeros_like(spread)

        @pl.loop(AHEAD, chunks)
        def _(j):
            Network(rows_ref[j], net_a, fac_a, basis_a, j, radial).run()

    def gather(fac, j, w, more):
        here = pl.ds(pl.multiple_of(j * edges, edges), edges)
        index = step * chunks + j
        key, base, off = window_key(rows_ref[index][2:3, :], win_ref[index, 0], w)
        key = jnp.transpose(jnp.broadcast_to(key, (8, edges)))[:, 0:1]
        near = lax.broadcasted_iota(jnp.int32, (edges, WINDOW), 1).astype(F32)
        hot = (key == near).astype(BF16)
        kept = lax.broadcasted_iota(jnp.int32, (16, LANES), 0) >= off
        kept = jnp.where(kept, 1.0, 0.0).astype(BF16)[:, 0:1]
        factors = [fac[here, col(k)] for k in range(3)]
        to = pl.ds(pl.multiple_of(j * GROUP, GROUP), GROUP)

        def rows_of(lanes):
            top = table[pl.ds(base, 16), lanes] * kept
            top += table[pl.ds(base + WINDOW, 16), lanes] * (1.0 - kept)
            rest = table[pl.ds(base + 16, WINDOW - 16), lanes]
            got = dot(hot, jnp.concatenate([top, rest], axis=0))
            return [got[:, col(n)] for n in range(got.shape[1] // LANES)]

        def use(c, x):
            rounded = x.astype(BF16)
            message = factors[KIND[c]] * x
            message = jnp.sum(message.reshape(slots, GROUP, LANES), axis=0)
            x_s[here, col(c)] = x_s[here, col(c)] + rounded if more else rounded
            msg_s[to, col(c)] = msg_s[to, col(c)] + message if more else message

        for n in range(3):
            one, other = rows_of(slice(2 * n * LANES, 2 * (n + 1) * LANES))
            use(1 + n, one - other)
            use(4 + n, one + other)
        x00, x11 = rows_of(slice(6 * LANES, 8 * LANES))
        (x22,) = rows_of(slice(8 * LANES, 9 * LANES))
        trace = x00 + x11 + x22
        third = trace * (1.0 / 3.0)
        use(0, trace)
        use(7, x00 - third)
        use(8, x11 - third)

    even = step % 2 == 0

    def collect(fac):
        @pl.loop(0, chunks // UNROLL)
        def _(pair):
            if fac is fac_a:

                @pl.when(jnp.logical_and(step == 0, pair < AHEAD // UNROLL))
                def _():
                    for n in range(UNROLL):
                        for copy in fetches(pair * UNROLL + n):
                            copy.wait()

            for n in range(UNROLL):
                gather(fac, pair * UNROLL + n, 0, False)

        @pl.loop(0, chunks)
        def _(j):
            @pl.loop(1, win_ref[step * chunks + j, 1])
            def _(w):
                gather(fac, j, w, True)

    @pl.when(even)
    def _():
        collect(fac_a)

    @pl.when(jnp.logical_not(even))
    def _():
        collect(fac_b)

    weights2 = (iso2_ref[...], anti2_ref[...], sym2_ref[...])
    put = pl.ds(pl.multiple_of(halo + step * atoms, 16), atoms)
    mixed = [[None] * 3 for _ in range(3)]
    for n, (p, q) in enumerate(ORDER):
        mixed[p][q] = table[put, col(n)].astype(F32)
    sums = [msg_s[:, col(c)] for c in range(9)]
    messages = to_matrix([sums[0] * (1.0 / 3.0)] + [0.5 * v for v in sums[1:7]] + sums[7:])
    paired = both_ways(mixed, messages)
    inverse = 1.0 / (1.0 + total([v * v for v in flat(paired)]))
    pair_coords = primal(paired)
    mid = [(v * inverse).astype(BF16) for v in pair_coords]
    mid.append(((-pair_coords[7] - pair_coords[8]) * inverse).astype(BF16))
    update = mix_parts(mid, weights2)
    at = pl.ds(pl.multiple_of(step * atoms, 16), atoms)
    values = [own_ref[c, at, :].astype(F32) for c in range(9)]
    inverse_in = 1.0 / (1.0 + total([v * v for v in values]))
    squared = flat(product(update, update))
    for c, (v, u, s) in enumerate(zip(values, flat(update), squared)):
        upd_ref[c] = (v * inverse_in + u + s).astype(BF16)
    out_grad = square([outgrad_ref[c].astype(F32) for c in range(9)])
    grad_update = add(out_grad, both_ways(out_grad, flip(update)))
    seen, mid_dual = back_parts(grad_update, weights2)
    for kind, grad in enumerate(weight_grads(mid, seen)):
        dw2_ref[kind * LANES : (kind + 1) * LANES, :] += grad
    projected = total([a * b for a, b in zip(mid_dual, pair_coords)]) * (2.0 * inverse * inverse)
    grad_paired = to_matrix([v * inverse for v in primal_of_dual(mid_dual)])
    grad_paired = [
        [grad_paired[p][q] - paired[p][q] * projected for q in range(3)] for p in range(3)
    ]
    from_pair = primal(both_ways(grad_paired, flip(messages)))
    for c in range(9):
        spread[put, col(c)] += from_pair[c]
    grad_messages = [
        [v.astype(BF16).astype(F32) for v in row] for row in both_ways(flip(mixed), grad_paired)
    ]
    for c, v in enumerate(primal(grad_messages) + dual(grad_messages)[7:]):
        twice = v.reshape(chunks, 1, GROUP, LANES)
        twice = jnp.concatenate([twice, twice], axis=1).reshape(2 * atoms, LANES)
        gm_s[:, col(c)] = twice.astype(BF16)

    def chunk_places(j):
        here = pl.ds(pl.multiple_of(j * edges, edges), edges)
        two = pl.ds(pl.multiple_of(j * 2 * GROUP, 2 * GROUP), 2 * GROUP)
        return here, two

    def scatter_hot(j, w):
        index = step * chunks + j
        key, base, off = window_key(rows_ref[index][2:3, :], win_ref[index, 0], w)
        near = lax.broadcasted_iota(jnp.int32, (WINDOW, edges), 0).astype(F32)
        kept = lax.broadcasted_iota(jnp.int32, (16, LANES), 0) >= off
        return (key == near).astype(BF16), base, kept

    def scatter(fac, j, hot_base_kept, cs):
        here, two = chunk_places(j)
        hot, base, kept = hot_base_kept
        terms = [
            (fac[here, col(KIND[c])].astype(BF16).reshape(pairs, 16, LANES) * gm_s[two, col(c)]).reshape(
                edges, LANES
            )
            for c in cs
        ]
        sums = dot(hot, jnp.concatenate(terms, axis=1))
        for n, c in enumerate(cs):
            top = sums[:16, col(n)]
            spread[pl.ds(base, 16), col(c)] += jnp.where(kept, top, 0.0)
            spread[pl.ds(base + WINDOW, 16), col(c)] += jnp.where(kept, 0.0, top)
            spread[pl.ds(base + 16, WINDOW - 16), col(c)] += sums[16:, col(n)]

    class Backward:
        def __init__(self, j, now, after):
            self.j, self.now = j, now
            self.net, self.fac, self.basis = now
            self.here, self.two = chunk_places(j)
            self.half = pl.ds(pl.multiple_of(j * (edges // 2), edges // 2), edges // 2)
            self.ahead = None
            if after is not None:
                self.ahead = Network(rows_ref[(step + 1) * chunks + j], *after, j, radial)

        def hot(self):
            self.key = scatter_hot(self.j, 0)

        def spread(self, n):
            scatter(self.fac, self.j, self.key, PAIRS[n])

        def terms(self):
            here, two = self.here, self.two
            terms = [
                x_s[here, col(c)].reshape(pairs, 16, LANES) * gm_s[two, col(c if c < 7 else c + 2)]
                for c in range(9)
            ]
            grads = [terms[0], total(terms[1:4]), total(terms[4:9])]
            grad3 = jnp.concatenate([v.reshape(edges, LANES) for v in grads], axis=1)
            self.grad3 = grad3 * self.net[here, SLOPE3]

        def back3(self):
            self.inner2 = dot_last(self.grad3, w3_ref[...])

        def grads2(self):
            slope = self.net[self.here, SLOPE2].astype(F32)
            self.grad2 = (self.inner2 * slope).astype(BF16)

        def back2(self):
            self.inner1 = dot_last(self.grad2, w2_ref[:LANES, :])

        def grads1(self):
            slope = self.net[self.here, SLOPE1].astype(F32)
            grad1 = (self.inner1 * slope).astype(BF16)
            self.grad1 = jnp.concatenate([grad1[: edges // 2], grad1[edges // 2 :]], axis=1)

        def weights3(self):
            ones = jnp.ones((16, edges), BF16)
            act2 = jnp.concatenate([jnp.transpose(self.net[self.here, ACT2]), ones], axis=0)
            d3_ref[...] += dot(act2, self.grad3)

        def weights2(self):
            ones = jnp.ones((16, edges), BF16)
            act1 = jnp.concatenate([jnp.transpose(self.net[self.here, ACT1]), ones], axis=0)
            d2_ref[...] += dot(act1, self.grad2)

        def weights1(self):
            d1_ref[...] += dot(jnp.transpose(self.basis[self.half, :]), self.grad1)

    def sweep(now, after):
        steps_of = {
            "H": lambda b: b.hot(), "T": lambda b: b.terms(),
            "0": lambda b: b.spread(0), "1": lambda b: b.spread(1), "2": lambda b: b.spread(2),
            "3": lambda b: b.spread(3), "4": lambda b: b.spread(4),
            "D": lambda b: b.back3(), "G": lambda b: b.grads2(),
            "E": lambda b: b.back2(), "F": lambda b: b.grads1(),
            "W": lambda b: b.weights3(), "V": lambda b: b.weights2(), "U": lambda b: b.weights1(),
            "a": lambda b: b.ahead.layer1(), "b": lambda b: b.ahead.active1(),
            "c": lambda b: b.ahead.layer2(), "d": lambda b: b.ahead.active2(),
            "e": lambda b: b.ahead.layer3(), "x": lambda b: b.ahead.active3(0),
            "y": lambda b: b.ahead.active3(1), "z": lambda b: b.ahead.active3(2),
        }

        @pl.loop(0, chunks // UNROLL)
        def _(pair):
            both = [Backward(pair * UNROLL + n, now, after) for n in range(UNROLL)]
            for which, name in zip(SCHEDULE[::2], SCHEDULE[1::2]):
                if after is not None or not name.islower():
                    steps_of[name](both[int(which)])

        @pl.loop(0, chunks)
        def _(j):
            @pl.loop(1, win_ref[step * chunks + j, 1])
            def _(w):
                more = scatter_hot(j, w)
                for cs in PAIRS:
                    scatter(now[1], j, more, cs)

    last = step == steps - 1

    @pl.when(jnp.logical_and(even, jnp.logical_not(last)))
    def _():
        sweep((net_a, fac_a, basis_a), (net_b, fac_b, basis_b))

    @pl.when(jnp.logical_not(jnp.logical_or(even, last)))
    def _():
        sweep((net_b, fac_b, basis_b), (net_a, fac_a, basis_a))

    @pl.when(last)
    def _():
        sweep((net_b, fac_b, basis_b), None)
        grads = [None] * 3
        place = 0
        for ref, out in ((low_ref, rim_low_ref), (own_ref, own_out_ref), (high_ref, rim_high_ref)):
            for at in range(0, out.shape[0], 64):
                here = slice(place + at, place + at + 64)
                coords = [spread[here, col(c)] for c in range(9)]
                for c in range(9):
                    out[at : at + 64, col(c)] = coords[c].astype(out.dtype)
                seen = seen_by_kind(to_matrix(coords))
                fresh = weight_grads(parts_in(ref, at), seen)
                grads = [n if o is None else o + n for o, n in zip(grads, fresh)]
            place += out.shape[0]
        first = d1_ref[:HALF, :LANES] + d1_ref[HALF:, LANES:]
        place = 0
        for value in (*grads, dw2_ref[...], first[:BASES]):
            grads_ref[place : place + value.shape[0], :] = value.astype(BF16)
            place += value.shape[0]
        biases = [first[BASES : BASES + 1]]
        for ref in (d2_ref, d3_ref):
            deep = ref.shape[0] - 16
            for n in range(ref.shape[1] // LANES):
                grads_ref[place : place + deep, :] = ref[:deep, col(n)].astype(BF16)
                biases.append(ref[deep : deep + 1, col(n)])
                place += deep
        biases.append(jnp.zeros((grads_ref.shape[0] - place - len(biases), LANES), F32))
        grads_ref[place:, :] = jnp.concatenate(biases, axis=0).astype(BF16)


def unpack_kernel(grads_ref, *out_refs):
    small, g_w1, g_w2, g_w3 = out_refs[:6], out_refs[6], out_refs[8], out_refs[10]
    place = 0
    for ref in (*small, g_w1):
        ref[...] = grads_ref[place : place + ref.shape[0], :].astype(F32)
        place += ref.shape[0]
    for ref in (g_w2, g_w3):
        for n in range(ref.shape[1] // LANES):
            ref[:, col(n)] = grads_ref[place : place + ref.shape[0], :].astype(F32)
            place += ref.shape[0]
    biases = grads_ref[place : place + 16, :].astype(F32)
    row = 0
    for ref in (out_refs[7], out_refs[9], out_refs[11]):
        for n in range(ref.shape[1] // LANES):
            ref[:, col(n)] = biases[row : row + 1, :]
            row += 1


def final_kernel(
    own_ref, above_ref, below_ref, atoms_ref, outgrad_ref, iso1_ref, anti1_ref, sym1_ref, out_ref
):
    weights = (iso1_ref[...], anti1_ref[...], sym1_ref[...])
    grad_mixed = [
        own_ref[:, col(c)] + above_ref[:, col(c)].astype(F32) + below_ref[:, col(c)].astype(F32)
        for c in range(9)
    ]
    back = flat(to_matrix(primal_of_dual(back_parts(to_matrix(grad_mixed), weights)[1])))
    values = [atoms_ref[c].astype(F32) for c in range(9)]
    inverse = 1.0 / (1.0 + total([v * v for v in values]))
    grad = [outgrad_ref[c].astype(F32) + back[c] for c in range(9)]
    along = total([g * v for g, v in zip(grad, values)]) * (2.0 * inverse)
    for c in range(9):
        out_ref[c] = (grad[c] - values[c] * along) * inverse


def whole(shape):
    return pl.BlockSpec(shape, lambda *_: (0,) * len(shape), pipeline_mode=pl.Buffered(1))


def block(shape):
    return pl.BlockSpec(shape, lambda i, *_: (i,) + (0,) * (len(shape) - 1))


def shape_of(shape, kind):
    return jax.ShapeDtypeStruct(shape, kind)


def part(value, index):
    return lax.dynamic_index_in_dim(value, index, 0, keepdims=False)


def reduce_everywhere(value, axes, beside):
    beside = list(beside)

    def between(v):
        return lax.optimization_barrier((v, beside.pop(0)()))[0] if beside else v

    peers = math.prod(lax.axis_size(a) for a in axes)
    me = lax.axis_index(axes)
    runs, at = [], 1
    while at < peers:
        size = min(2 if at == 1 else 4, peers // at)
        runs.append((at, size))
        at *= size

    def swapped(v, by):
        return lax.ppermute(v, axes, [(i, i ^ by) for i in range(peers)])

    for at, size in runs[:-1]:
        shares = value.reshape(size, value.shape[0] // size, value.shape[1])
        mine = me // at % size
        kept = part(shares, mine).astype(F32)
        for k in range(1, size):
            kept = kept + swapped(part(shares, mine ^ k), k * at).astype(F32)
        value = between(kept.astype(BF16))
    at, size = runs[-1]
    kept = value.astype(F32)
    for k in range(1, size):
        kept = kept + swapped(value, k * at).astype(F32)
    value = between(kept.astype(BF16))
    for at, size in runs[-2::-1]:
        mine = me // at % size
        full = jnp.zeros((size,) + value.shape, value.dtype)
        full = lax.dynamic_update_index_in_dim(full, value, mine, 0)
        for k in range(1, size):
            full = lax.dynamic_update_index_in_dim(full, swapped(value, k * at), mine ^ k, 0)
        value = full.reshape(size * value.shape[0], value.shape[1])
    return value


def local(
    atoms, neighbours, live_mask, distances,
    w_iso1, w_anti1, w_sym1, w_rad1, b_rad1, w_rad2, b_rad2, w_rad3, b_rad3,
    w_iso2, w_anti2, w_sym2, out_grad,
):
    rows, _, channels = atoms.shape
    slots = neighbours.shape[1]
    halo = MOL_MOST
    wide = 9 * channels
    ext = rows + 2 * halo
    edges = GROUP * slots
    chunk_count = rows // GROUP
    steps = 4
    chunks = chunk_count // steps
    block_atoms = rows // steps
    block_edges = block_atoms * slots
    vmem = 62 * 1024 * 1024
    me = lax.axis_index(AXES)
    peers = math.prod(lax.axis_size(a) for a in AXES)
    up = [(i, i + 1) for i in range(peers - 1)]
    down = [(i + 1, i) for i in range(peers - 1)]

    by_component = jnp.swapaxes(atoms, 0, 1)
    out_grad_by_component = jnp.swapaxes(out_grad, 0, 1)
    low = lax.ppermute(by_component, AXES, up)
    high = lax.ppermute(by_component, AXES, down)

    links = neighbours - (me * rows - halo)
    gating = 0.5 * (jnp.cos(math.pi * distances / CUTOFF) + 1.0) * live_mask.astype(F32)

    def as_rows(v):
        return jnp.swapaxes(v.reshape(chunk_count, GROUP, slots), 1, 2).reshape(
            chunk_count, 1, edges
        )

    edge_rows = jnp.concatenate(
        [as_rows(distances), as_rows(gating), as_rows(links.astype(F32))]
        + [jnp.zeros((chunk_count, 5, edges), F32)],
        axis=1,
    )
    grouped = links.reshape(chunk_count, edges)
    first = jnp.min(grouped, axis=1)
    count = (jnp.max(grouped, axis=1) - first) // WINDOW + 1
    windows = jnp.stack([first, count], axis=1)

    biases = jnp.concatenate([b_rad1, b_rad2, b_rad3]).reshape(-1, LANES)
    mid_width, last_width = w_rad2.shape[1], w_rad3.shape[1]
    small = whole((channels, channels))
    components = pl.BlockSpec((9, block_atoms, channels), lambda i: (0, i, 0))
    smem = pl.BlockSpec(memory_space=pltpu.SMEM)
    net_args = (w_rad1, w_rad2, w_rad3, biases)
    net_specs = [whole(v.shape) for v in net_args]
    net_scratch = [
        pltpu.VMEM((LANES, 2 * channels), BF16),
        pltpu.VMEM((2 * channels, mid_width), BF16),
        pltpu.VMEM((mid_width, last_width), BF16), pltpu.VMEM((1, last_width), F32),
    ]
    net0 = pl.pallas_call(
        network_kernel,
        grid=(AHEAD,),
        in_specs=[block((1, 8, edges))] + net_specs,
        out_specs=[
            block((edges, KEPT)), block((edges, last_width)), block((edges // 2, LANES))
        ],
        out_shape=[
            shape_of((AHEAD * edges, KEPT), BF16), shape_of((AHEAD * edges, last_width), F32),
            shape_of((AHEAD * edges // 2, LANES), BF16),
        ],
        scratch_shapes=net_scratch,
        compiler_params=pltpu.CompilerParams(vmem_limit_bytes=vmem),
        cost_estimate=pl.CostEstimate(
            flops=2 * block_edges * 135168, bytes_accessed=block_edges * KEPT * 2, transcendentals=0
        ),
        name="network",
    )(edge_rows, *net_args)

    grad_rows = 6 * channels + BASES + mid_width // LANES * channels
    grad_rows += last_width // LANES * mid_width + 16
    grad_rows = -(-grad_rows // 128) * 128
    updated, rim_low, own_grad, rim_high, grads = pl.pallas_call(
        main_kernel,
        grid=(steps,),
        in_specs=[
            smem, whole(low.shape), whole(by_component.shape), whole(high.shape),
            components, whole((chunk_count, 8, edges)), *net_specs,
            small, small, small, small, small, small,
            *[pl.BlockSpec(memory_space=pl.ANY)] * 3,
        ],
        out_specs=[
            components, whole((halo, wide)), whole((rows, wide)), whole((halo, wide)),
            whole((grad_rows, channels)),
        ],
        out_shape=[
            shape_of((9, rows, channels), BF16),
            shape_of((halo, wide), BF16), shape_of((rows, wide), F32),
            shape_of((halo, wide), BF16), shape_of((grad_rows, channels), BF16),
        ],
        scratch_shapes=[
            pltpu.VMEM((ext + WINDOW, wide), BF16),
            pltpu.VMEM((block_edges, KEPT), BF16),
            pltpu.VMEM((block_edges, KEPT), BF16),
            pltpu.VMEM((block_edges, last_width), F32),
            pltpu.VMEM((block_edges, last_width), F32),
            pltpu.VMEM((block_edges // 2, LANES), BF16),
            pltpu.VMEM((block_edges // 2, LANES), BF16),
            pltpu.VMEM((block_edges, wide), BF16),
            pltpu.VMEM((block_atoms, wide), F32),
            pltpu.VMEM((2 * block_atoms, wide + 2 * channels), BF16),
            pltpu.VMEM((ext + WINDOW, wide), F32),
            pltpu.VMEM((mid_width + 16, last_width), F32),
            pltpu.VMEM((channels + 16, mid_width), F32),
            pltpu.VMEM((LANES, 2 * channels), F32),
            pltpu.VMEM((3 * channels, channels), F32),
            *net_scratch,
            pltpu.SemaphoreType.DMA((AHEAD, 3)),
        ],
        compiler_params=pltpu.CompilerParams(vmem_limit_bytes=vmem),
        name="main",
    )(
        windows, low, by_component, high, out_grad_by_component, edge_rows, *net_args,
        w_iso1, w_anti1, w_sym1, w_iso2, w_anti2, w_sym2, *net0,
    )

    kept = {}

    def send_rims():
        kept["above"] = lax.ppermute(rim_low, AXES, down)
        kept["below"] = lax.ppermute(rim_high, AXES, up)
        return kept["above"], kept["below"]

    def finish():
        grad_atoms = pl.pallas_call(
            final_kernel,
            out_shape=shape_of((9, rows, channels), F32),
            compiler_params=pltpu.CompilerParams(vmem_limit_bytes=vmem),
            name="final",
        )(
            own_grad, kept["above"], kept["below"], by_component, out_grad_by_component,
            w_iso1, w_anti1, w_sym1,
        )
        kept["outs"] = jnp.swapaxes(updated, 0, 1), jnp.swapaxes(grad_atoms, 0, 1)
        return kept["outs"]

    summed = reduce_everywhere(grads, AXES, (lambda: (), send_rims, finish))
    square_shape = (channels, channels)
    shapes = [square_shape] * 6 + [w_rad1.shape, (1, channels), w_rad2.shape, (1, mid_width)]
    shapes += [w_rad3.shape, (1, last_width)]
    out = pl.pallas_call(
        unpack_kernel,
        out_shape=[shape_of(shape, F32) for shape in shapes],
        compiler_params=pltpu.CompilerParams(vmem_limit_bytes=16 * 1024 * 1024),
        name="unpack",
    )(summed)
    return (
        *kept["outs"],
        *out[:3],
        *(v if n % 2 == 0 else v[0] for n, v in enumerate(out[6:])),
        *out[3:6],
    )


def solution(mesh):
    split3 = P(AXES, None, None)
    split2 = P(AXES, None)
    return jax.shard_map(
        local,
        mesh=mesh,
        in_specs=(split3, split2, split2, split2) + (P(),) * 12 + (split3,),
        out_specs=(split3, split3) + (P(),) * 12,
        check_vma=False,
    )
```

```python
import functools
import math

import jax
import jax.numpy as jnp
from jax import lax
from jax.experimental import pallas as pl
from jax.experimental.pallas import tpu as pltpu
from jax.sharding import PartitionSpec as P

MOL_MOST = 256
CUTOFF = 5.0
LANES = 128
GROUP = 8
BASES = 32
UNROLL = 2
PAIRS = ((0, 1), (2, 3), (4, 5), (6, 7), (8,))
SCHEDULE = "0H0T0D000a01040G0b0J030c0W0d0p0E0e0F0x0V0y020U0z1H1T1D101a111b121G1J131c141d1p1E1e1F1y1x1V1U1z1W"
WINDOW = 256
KIND = (0, 1, 1, 1, 2, 2, 2, 2, 2)
AXES = ("edge", "grp")
F32 = jnp.float32
BF16 = jnp.bfloat16


def col(c):
    return slice(c * LANES, (c + 1) * LANES)


def to_matrix(coords):
    t, a01, a02, a12, s01, s02, s12, s00, s11 = coords
    return [
        [t + s00, s01 + a01, s02 + a02],
        [s01 - a01, t + s11, s12 + a12],
        [s02 - a02, s12 - a12, t - s00 - s11],
    ]


def primal(m):
    t = (m[0][0] + m[1][1] + m[2][2]) * (1.0 / 3.0)
    return [
        t,
        0.5 * (m[0][1] - m[1][0]),
        0.5 * (m[0][2] - m[2][0]),
        0.5 * (m[1][2] - m[2][1]),
        0.5 * (m[0][1] + m[1][0]),
        0.5 * (m[0][2] + m[2][0]),
        0.5 * (m[1][2] + m[2][1]),
        m[0][0] - t,
        m[1][1] - t,
    ]


def dual(m):
    return [
        m[0][0] + m[1][1] + m[2][2],
        m[0][1] - m[1][0],
        m[0][2] - m[2][0],
        m[1][2] - m[2][1],
        m[0][1] + m[1][0],
        m[0][2] + m[2][0],
        m[1][2] + m[2][1],
        m[0][0] - m[2][2],
        m[1][1] - m[2][2],
    ]


def primal_of_dual(d):
    third = 1.0 / 3.0
    return (
        [d[0] * third]
        + [0.5 * v for v in d[1:7]]
        + [(2.0 * d[7] - d[8]) * third, (2.0 * d[8] - d[7]) * third]
    )


def product(a, b):
    return [
        [a[p][0] * b[0][q] + a[p][1] * b[1][q] + a[p][2] * b[2][q] for q in range(3)]
        for p in range(3)
    ]


def add(a, b):
    return [[a[p][q] + b[p][q] for q in range(3)] for p in range(3)]


def both_ways(a, b):
    return add(product(a, b), product(b, a))


def flip(m):
    return [[m[q][p] for q in range(3)] for p in range(3)]


def flat(m):
    return [m[p][q] for p in range(3) for q in range(3)]


def square(parts):
    return [list(parts[0:3]), list(parts[3:6]), list(parts[6:9])]


def total(values):
    out = values[0]
    for v in values[1:]:
        out = out + v
    return out


def dot(a, b):
    return jnp.dot(a, b, preferred_element_type=F32)


def dot_first(a, b):
    return lax.dot_general(a, b, (((0,), (0,)), ((), ())), preferred_element_type=F32)


def dot_last(a, b):
    return lax.dot_general(a, b, (((1,), (1,)), ((), ())), preferred_element_type=F32)


def stack(values):
    return jnp.concatenate([v.astype(BF16) for v in values], axis=0)


def pieces_of(value, rows):
    return [value[n * rows : (n + 1) * rows] for n in range(value.shape[0] // rows)]


def rounded_parts(m):
    coords = primal(m)
    return [v.astype(BF16) for v in coords + [-coords[7] - coords[8]]]


def parts_in(atoms_ref, at):
    values = [atoms_ref[c, at : at + 64, :].astype(F32) for c in range(9)]
    scale = 1.0 / (1.0 + total([v * v for v in values]))
    return rounded_parts(square([v * scale for v in values]))


def mix_parts(parts, weights):
    rows = parts[0].shape[0]
    t, a01, a02, a12, s01, s02, s12, s00, s11, s22 = (
        pieces_of(dot(parts[0], weights[0]), rows)
        + pieces_of(dot(stack(parts[1:4]), weights[1]), rows)
        + pieces_of(dot(stack(parts[4:10]), weights[2]), rows)
    )
    return [
        [t + s00, s01 + a01, s02 + a02],
        [s01 - a01, t + s11, s12 + a12],
        [s02 - a02, s12 - a12, t + s22],
    ]


def seen_by_kind(grad):
    diagonal = [grad[0][0], grad[1][1], grad[2][2]]
    skew = [grad[0][1], grad[1][0], grad[0][2], grad[2][0], grad[1][2], grad[2][1]]
    return [stack(v) for v in (diagonal, skew, skew + diagonal)]


def back_parts(grad, weights):
    rows = grad[0][0].shape[0]
    seen = seen_by_kind(grad)
    iso, anti, sym = (pieces_of(dot_last(v, w), rows) for v, w in zip(seen, weights))
    coords = [
        iso[0] + iso[1] + iso[2],
        anti[0] - anti[1], anti[2] - anti[3], anti[4] - anti[5],
        sym[0] + sym[1], sym[2] + sym[3], sym[4] + sym[5],
        sym[6] - sym[8], sym[7] - sym[8],
    ]
    return seen, coords


def weight_grads(parts, seen):
    p = parts
    lefts = (
        [p[0]] * 3,
        [p[1], -p[1], p[2], -p[2], p[3], -p[3]],
        [p[4], p[4], p[5], p[5], p[6], p[6], p[7], p[8], p[9]],
    )
    return [dot_first(stack(left), right) for left, right in zip(lefts, seen)]


def half_silu(u):
    t = jnp.tanh(u)
    p = 1.0 + t
    act = u * p
    return act, p + act * (1.0 - t)


SLOPE3, ACT2, SLOPE2 = slice(0, 384), slice(384, 640), slice(640, 896)
ACT1, SLOPE1 = slice(896, 1024), slice(1024, 1152)
KEPT = 1152
HALF = 64
AHEAD = 6

ORDER = ((0, 1), (1, 0), (0, 2), (2, 0), (1, 2), (2, 1), (0, 0), (1, 1), (2, 2))


def over_lanes(block, slots, lanes=LANES):
    return jnp.concatenate(
        [jnp.broadcast_to(block[:, s : s + 1], (block.shape[0], lanes)) for s in slots], axis=0
    )


class Network:
    def __init__(self, dist, gate, out, factors, basis, at, refs):
        self.dist, self.gate8 = dist, gate
        self.out, self.factors, self.basis, self.refs = out, factors, basis, refs
        edges = dist.shape[0] * dist.shape[1]
        self.here = pl.ds(pl.multiple_of(at * edges, edges), edges)
        self.half = pl.ds(pl.multiple_of(at * (edges // 2), edges // 2), edges // 2)

    def run(self):
        self.layer1()
        self.active1()
        self.layer2()
        self.active2(0)
        self.active2(1)
        self.layer3()
        for kind in range(3):
            self.active3(kind)

    def layer1(self):
        slots = self.dist.shape[1]
        self.gate = over_lanes(self.gate8, range(slots))
        low = over_lanes(self.dist, range(slots // 2))
        lane = lax.broadcasted_iota(jnp.int32, low.shape, 1)
        dist = jnp.where(lane < HALF, low, over_lanes(self.dist, range(slots // 2, slots)))
        lane = lane % HALF
        off = dist - lane.astype(F32) * (CUTOFF / 31.0)
        basis = jnp.exp(off * off * (-0.5 * (31.0 / CUTOFF) ** 2))
        last = jnp.where(lane == BASES, 1.0, 0.0)
        basis = jnp.where(lane < BASES, basis, last).astype(BF16)
        self.basis[self.half, :] = basis
        inner = dot(basis, self.refs[0][...])
        self.inner = jnp.concatenate([inner[:, :LANES], inner[:, LANES:]], axis=0)

    def active1(self):
        act, slope = half_silu(self.inner)
        self.act = act.astype(BF16)
        self.out[self.here, ACT1] = self.act
        self.out[self.here, SLOPE1] = slope.astype(BF16)

    def layer2(self):
        one = lax.broadcasted_iota(jnp.int32, self.act.shape, 1) == 0
        one = jnp.where(one, 1.0, 0.0).astype(BF16)
        self.inner = dot(jnp.concatenate([self.act, one], axis=1), self.refs[1][...])

    def active2(self, n):
        act, slope = half_silu(self.inner[:, col(n)])
        act = act.astype(BF16)
        self.act = jnp.concatenate([self.act, act], axis=1) if n else act
        self.out[self.here, col(ACT2.start // LANES + n)] = act
        self.out[self.here, col(SLOPE2.start // LANES + n)] = slope.astype(BF16)

    def layer3(self):
        self.inner = dot(self.act, self.refs[2][...])

    def active3(self, kind):
        act, slope = half_silu(self.inner[:, col(kind)] + self.refs[3][:, col(kind)])
        self.factors[self.here, col(kind)] = act * self.gate
        self.out[self.here, col(kind)] = (slope * (0.5 * self.gate)).astype(BF16)


def halve_weights(w1_ref, w2_ref, w3_ref, bias_ref, w1_s, w2_s, w3_s, b3_s):
    half = 0.5 * bias_ref[...].astype(F32)

    def biased(weights, bias, rows):
        below = lax.broadcasted_iota(jnp.int32, (rows - weights.shape[0], bias.shape[1]), 0)
        bias = jnp.where(below == 0, bias, 0.0)
        return jnp.concatenate([0.5 * weights.astype(F32), bias], axis=0).astype(BF16)

    w1_s[...] = jnp.zeros_like(w1_s)
    first = biased(w1_ref[...], half[0:1], HALF)
    w1_s[:HALF, :LANES] = first
    w1_s[HALF:, LANES:] = first
    wide2 = jnp.concatenate([half[1:2], half[2:3]], axis=1)
    w2_s[...] = biased(w2_ref[...], wide2, w2_s.shape[0])
    w3_s[...] = (0.5 * w3_ref[...].astype(F32)).astype(BF16)
    b3_s[...] = jnp.concatenate([half[3:4], half[4:5], half[5:6]], axis=1)


def by_atom(ref):
    return jnp.transpose(ref[...].astype(F32))


def gating(dist, live):
    return 0.5 * (jnp.cos(math.pi * dist / CUTOFF) + 1.0) * live


def network_kernel(
    dist_ref, live_ref, w1_raw, w2_raw, w3_raw, bias_ref, out_ref, fac_ref, basis_ref, dist_s, gate_s, w1_s, w2_s,
    w3_s, b3_s,
):
    net_refs = (w1_s, w2_s, w3_s, b3_s)

    @pl.when(pl.program_id(0) == 0)
    def _():
        halve_weights(w1_raw, w2_raw, w3_raw, bias_ref, *net_refs)
        dist_s[...] = by_atom(dist_ref)
        gate_s[...] = gating(dist_s[...], by_atom(live_ref))

    mine = pl.ds(pl.multiple_of(pl.program_id(0) * GROUP, GROUP), GROUP)
    Network(dist_s[mine, :], gate_s[mine, :], out_ref, fac_ref, basis_ref, 0, net_refs).run()


def window_key(link, first, w):
    start = first + w * WINDOW
    base = pl.multiple_of(first // 16 * 16 + w * WINDOW, 16)
    off = first % 16
    rel = link - start.astype(F32)
    key = rel + off.astype(F32)
    key = jnp.where(key >= WINDOW, key - WINDOW, key)
    key = jnp.where(jnp.logical_and(rel >= 0, rel < WINDOW), key, -1.0)
    return key, base, off


def main_kernel(
    win_ref, near_ref, own_ref, far_ref, outgrad_ref, dist_ref, live_ref, link_ref,
    w1_raw, w2_raw, w3_raw, bias_ref,
    iso1_ref, anti1_ref, sym1_ref, iso2_ref, anti2_ref, sym2_ref, net_first, fac_first, basis_first,
    upd_ref, rim_near_ref, own_out_ref, rim_far_ref, grads_ref,
    table, net_a, net_b, fac_a, fac_b, basis_a, basis_b, x_s, msg_s, gm_s, spread,
    d3_ref, d2_ref, d1_ref, dw2_ref, w1_ref, w2_ref, w3_ref, b3_ref,
    dist_s, gate_s, link_s, sems,
):
    step = pl.program_id(0)
    steps = pl.num_programs(0)
    edges = GROUP * link_ref.shape[0]
    halo = near_ref.shape[1]
    odd = win_ref[win_ref.shape[0] - 1, 0]
    far_side = halo + own_ref.shape[1]
    near_at = pl.multiple_of((1 - odd) * far_side, 64)
    far_at = pl.multiple_of(odd * far_side, 64)
    atoms = upd_ref.shape[1]
    chunks = atoms // GROUP
    slots = edges // GROUP
    pairs = edges // 16
    wide = 9 * LANES
    radial = (w1_ref, w2_ref, w3_ref, b3_ref)

    def chunk_atoms(index):
        return pl.ds(pl.multiple_of(index * GROUP, GROUP), GROUP)

    def fetches(j):
        here = pl.ds(pl.multiple_of(j * edges, edges), edges)
        half = pl.ds(pl.multiple_of(j * (edges // 2), edges // 2), edges // 2)
        return (
            pltpu.make_async_copy(net_first.at[here], net_a.at[here], sems.at[j, 0]),
            pltpu.make_async_copy(fac_first.at[here], fac_a.at[here], sems.at[j, 1]),
            pltpu.make_async_copy(basis_first.at[half], basis_a.at[half], sems.at[j, 2]),
        )

    @pl.when(step == 0)
    def _():
        for j in range(AHEAD):
            for copy in fetches(j):
                copy.start()
        halve_weights(w1_raw, w2_raw, w3_raw, bias_ref, *radial)
        dist_s[...] = by_atom(dist_ref)
        gate_s[...] = gating(dist_s[...], by_atom(live_ref))
        link_s[...] = by_atom(link_ref)
        weights = (iso1_ref[...], anti1_ref[...], sym1_ref[...])
        for ref, place in ((near_ref, near_at), (own_ref, halo), (far_ref, far_at)):
            for at in range(0, ref.shape[1], 64):
                mixed = mix_parts(parts_in(ref, at), weights)
                for n, (p, q) in enumerate(ORDER):
                    table[pl.ds(place + at, 64), col(n)] = mixed[p][q].astype(BF16)
        place = far_side + halo
        table[place:, :] = jnp.zeros((table.shape[0] - place, wide), BF16)
        d3_ref[...] = jnp.zeros_like(d3_ref)
        d2_ref[...] = jnp.zeros_like(d2_ref)
        d1_ref[...] = jnp.zeros_like(d1_ref)
        dw2_ref[...] = jnp.zeros_like(dw2_ref)
        spread[...] = jnp.zeros_like(spread)

        @pl.loop(AHEAD, chunks)
        def _(j):
            mine = chunk_atoms(j)
            Network(dist_s[mine, :], gate_s[mine, :], net_a, fac_a, basis_a, j, radial).run()

    def gather(fac, j, w, more):
        here = pl.ds(pl.multiple_of(j * edges, edges), edges)
        index = step * chunks + j
        key, base, off = window_key(link_s[chunk_atoms(index), :], win_ref[index, 0], w)
        near = lax.broadcasted_iota(jnp.int32, (edges, WINDOW), 1).astype(F32)
        hot = (over_lanes(key, range(slots), WINDOW) == near).astype(BF16)
        kept = lax.broadcasted_iota(jnp.int32, (16, LANES), 0) >= off
        kept = jnp.where(kept, 1.0, 0.0).astype(BF16)[:, 0:1]
        factors = [fac[here, col(k)] for k in range(3)]
        to = pl.ds(pl.multiple_of(j * GROUP, GROUP), GROUP)

        def rows_of(lanes):
            top = table[pl.ds(base, 16), lanes] * kept
            top += table[pl.ds(base + WINDOW, 16), lanes] * (1.0 - kept)
            rest = table[pl.ds(base + 16, WINDOW - 16), lanes]
            got = dot(hot, jnp.concatenate([top, rest], axis=0))
            return [got[:, col(n)] for n in range(got.shape[1] // LANES)]

        def use(c, x):
            rounded = x.astype(BF16)
            message = factors[KIND[c]] * x
            message = jnp.sum(message.reshape(slots, GROUP, LANES), axis=0)
            x_s[here, col(c)] = x_s[here, col(c)] + rounded if more else rounded
            msg_s[to, col(c)] = msg_s[to, col(c)] + message if more else message

        for n in range(3):
            one, other = rows_of(slice(2 * n * LANES, 2 * (n + 1) * LANES))
            use(1 + n, one - other)
            use(4 + n, one + other)
        x00, x11 = rows_of(slice(6 * LANES, 8 * LANES))
        (x22,) = rows_of(slice(8 * LANES, 9 * LANES))
        trace = x00 + x11 + x22
        third = trace * (1.0 / 3.0)
        use(0, trace)
        use(7, x00 - third)
        use(8, x11 - third)

    even = step % 2 == 0

    def collect(fac):
        @pl.loop(0, chunks // UNROLL)
        def _(pair):
            if fac is fac_a:

                @pl.when(jnp.logical_and(step == 0, pair < AHEAD // UNROLL))
                def _():
                    for n in range(UNROLL):
                        for copy in fetches(pair * UNROLL + n):
                            copy.wait()

            for n in range(UNROLL):
                gather(fac, pair * UNROLL + n, 0, False)

        @pl.loop(0, chunks)
        def _(j):
            @pl.loop(1, win_ref[step * chunks + j, 1])
            def _(w):
                gather(fac, j, w, True)

    @pl.when(even)
    def _():
        collect(fac_a)

    @pl.when(jnp.logical_not(even))
    def _():
        collect(fac_b)

    weights2 = (iso2_ref[...], anti2_ref[...], sym2_ref[...])
    put = pl.ds(pl.multiple_of(halo + step * atoms, 16), atoms)
    mixed = [[None] * 3 for _ in range(3)]
    for n, (p, q) in enumerate(ORDER):
        mixed[p][q] = table[put, col(n)].astype(F32)
    sums = [msg_s[:, col(c)] for c in range(9)]
    messages = to_matrix([sums[0] * (1.0 / 3.0)] + [0.5 * v for v in sums[1:7]] + sums[7:])
    paired = both_ways(mixed, messages)
    inverse = 1.0 / (1.0 + total([v * v for v in flat(paired)]))
    pair_coords = primal(paired)
    mid = [(v * inverse).astype(BF16) for v in pair_coords]
    mid.append(((-pair_coords[7] - pair_coords[8]) * inverse).astype(BF16))
    update = mix_parts(mid, weights2)
    at = pl.ds(pl.multiple_of(step * atoms, 16), atoms)
    values = [own_ref[c, at, :].astype(F32) for c in range(9)]
    inverse_in = 1.0 / (1.0 + total([v * v for v in values]))
    squared = flat(product(update, update))
    for c, (v, u, s) in enumerate(zip(values, flat(update), squared)):
        upd_ref[c] = (v * inverse_in + u + s).astype(BF16)
    out_grad = square([outgrad_ref[c].astype(F32) for c in range(9)])
    grad_update = add(out_grad, both_ways(out_grad, flip(update)))
    seen, mid_dual = back_parts(grad_update, weights2)
    for kind, grad in enumerate(weight_grads(mid, seen)):
        dw2_ref[kind * LANES : (kind + 1) * LANES, :] += grad
    projected = total([a * b for a, b in zip(mid_dual, pair_coords)]) * (2.0 * inverse * inverse)
    grad_paired = to_matrix([v * inverse for v in primal_of_dual(mid_dual)])
    grad_paired = [
        [grad_paired[p][q] - paired[p][q] * projected for q in range(3)] for p in range(3)
    ]
    from_pair = primal(both_ways(grad_paired, flip(messages)))
    for c in range(9):
        spread[put, col(c)] += from_pair[c]
    grad_messages = [
        [v.astype(BF16).astype(F32) for v in row] for row in both_ways(flip(mixed), grad_paired)
    ]
    for c, v in enumerate(primal(grad_messages) + dual(grad_messages)[7:]):
        twice = v.reshape(chunks, 1, GROUP, LANES)
        twice = jnp.concatenate([twice, twice], axis=1).reshape(2 * atoms, LANES)
        gm_s[:, col(c)] = twice.astype(BF16)

    def chunk_places(j):
        here = pl.ds(pl.multiple_of(j * edges, edges), edges)
        two = pl.ds(pl.multiple_of(j * 2 * GROUP, 2 * GROUP), 2 * GROUP)
        return here, two

    def scatter_hot(j, w):
        index = step * chunks + j
        key, base, off = window_key(link_s[chunk_atoms(index), :], win_ref[index, 0], w)
        lane = lax.broadcasted_iota(jnp.int32, (slots, edges), 1)
        own_slot = lax.broadcasted_iota(jnp.int32, (slots, edges), 0) == lane // GROUP
        copies = dot(key.astype(BF16), jnp.where(own_slot, 1.0, 0.0).astype(BF16))
        lane = lax.broadcasted_iota(jnp.int32, (GROUP, edges), 1)
        own_atom = lax.broadcasted_iota(jnp.int32, (GROUP, edges), 0) == lane % GROUP
        key = jnp.sum(jnp.where(own_atom, copies, 0.0), axis=0, keepdims=True)
        near = lax.broadcasted_iota(jnp.int32, (WINDOW, edges), 0).astype(F32)
        kept = lax.broadcasted_iota(jnp.int32, (16, LANES), 0) >= off
        return (key == near).astype(BF16), base, kept

    def scatter(fac, j, hot_base_kept, cs):
        here, two = chunk_places(j)
        hot, base, kept = hot_base_kept
        terms = [
            (fac[here, col(KIND[c])].astype(BF16).reshape(pairs, 16, LANES) * gm_s[two, col(c)]).reshape(
                edges, LANES
            )
            for c in cs
        ]
        sums = dot(hot, jnp.concatenate(terms, axis=1))
        for n, c in enumerate(cs):
            top = sums[:16, col(n)]
            spread[pl.ds(base, 16), col(c)] += jnp.where(kept, top, 0.0)
            spread[pl.ds(base + WINDOW, 16), col(c)] += jnp.where(kept, 0.0, top)
            spread[pl.ds(base + 16, WINDOW - 16), col(c)] += sums[16:, col(n)]

    class Backward:
        def __init__(self, j, now, after):
            self.j, self.now = j, now
            self.net, self.fac, self.basis = now
            self.here, self.two = chunk_places(j)
            self.half = pl.ds(pl.multiple_of(j * (edges // 2), edges // 2), edges // 2)
            self.ahead = None
            if after is not None:
                mine = chunk_atoms((step + 1) * chunks + j)
                self.ahead = Network(dist_s[mine, :], gate_s[mine, :], *after, j, radial)

        def hot(self):
            self.key = scatter_hot(self.j, 0)

        def spread(self, n):
            scatter(self.fac, self.j, self.key, PAIRS[n])

        def terms(self):
            here, two = self.here, self.two
            terms = [
                x_s[here, col(c)].reshape(pairs, 16, LANES) * gm_s[two, col(c if c < 7 else c + 2)]
                for c in range(9)
            ]
            grads = [terms[0], total(terms[1:4]), total(terms[4:9])]
            grad3 = jnp.concatenate([v.reshape(edges, LANES) for v in grads], axis=1)
            self.grad3 = grad3 * self.net[here, SLOPE3]

        def back3(self):
            self.inner2 = dot_last(self.grad3, w3_ref[...])

        def grads2(self, n):
            slope = self.net[self.here, col(SLOPE2.start // LANES + n)].astype(F32)
            grad2 = (self.inner2[:, col(n)] * slope).astype(BF16)
            self.grad2 = jnp.concatenate([self.grad2, grad2], axis=1) if n else grad2

        def back2(self):
            self.inner1 = dot_last(self.grad2, w2_ref[:LANES, :])

        def grads1(self):
            slope = self.net[self.here, SLOPE1].astype(F32)
            grad1 = (self.inner1 * slope).astype(BF16)
            self.grad1 = jnp.concatenate([grad1[: edges // 2], grad1[edges // 2 :]], axis=1)

        def weights3(self):
            ones = jnp.ones((16, edges), BF16)
            act2 = jnp.concatenate([jnp.transpose(self.net[self.here, ACT2]), ones], axis=0)
            d3_ref[...] += dot(act2, self.grad3)

        def weights2(self):
            ones = jnp.ones((16, edges), BF16)
            act1 = jnp.concatenate([jnp.transpose(self.net[self.here, ACT1]), ones], axis=0)
            d2_ref[...] += dot(act1, self.grad2)

        def weights1(self):
            d1_ref[...] += dot(jnp.transpose(self.basis[self.half, :]), self.grad1)

    def sweep(now, after):
        steps_of = {
            "H": lambda b: b.hot(), "T": lambda b: b.terms(),
            "0": lambda b: b.spread(0), "1": lambda b: b.spread(1), "2": lambda b: b.spread(2),
            "3": lambda b: b.spread(3), "4": lambda b: b.spread(4),
            "D": lambda b: b.back3(), "G": lambda b: b.grads2(0), "J": lambda b: b.grads2(1),
            "E": lambda b: b.back2(), "F": lambda b: b.grads1(),
            "W": lambda b: b.weights3(), "V": lambda b: b.weights2(), "U": lambda b: b.weights1(),
            "a": lambda b: b.ahead.layer1(), "b": lambda b: b.ahead.active1(),
            "c": lambda b: b.ahead.layer2(), "d": lambda b: b.ahead.active2(0), "p": lambda b: b.ahead.active2(1),
            "e": lambda b: b.ahead.layer3(), "x": lambda b: b.ahead.active3(0),
            "y": lambda b: b.ahead.active3(1), "z": lambda b: b.ahead.active3(2),
        }

        @pl.loop(0, chunks // UNROLL)
        def _(pair):
            both = [Backward(pair * UNROLL + n, now, after) for n in range(UNROLL)]
            for which, name in zip(SCHEDULE[::2], SCHEDULE[1::2]):
                if after is not None or not name.islower():
                    steps_of[name](both[int(which)])

        @pl.loop(0, chunks)
        def _(j):
            @pl.loop(1, win_ref[step * chunks + j, 1])
            def _(w):
                more = scatter_hot(j, w)
                for cs in PAIRS:
                    scatter(now[1], j, more, cs)

    last = step == steps - 1

    @pl.when(jnp.logical_and(even, jnp.logical_not(last)))
    def _():
        sweep((net_a, fac_a, basis_a), (net_b, fac_b, basis_b))

    @pl.when(jnp.logical_not(jnp.logical_or(even, last)))
    def _():
        sweep((net_b, fac_b, basis_b), (net_a, fac_a, basis_a))

    @pl.when(last)
    def _():
        sweep((net_b, fac_b, basis_b), None)
        grads = [None] * 3
        for ref, out, place in (
            (near_ref, rim_near_ref, near_at),
            (own_ref, own_out_ref, halo),
            (far_ref, rim_far_ref, far_at),
        ):
            for at in range(0, out.shape[0], 64):
                coords = [spread[pl.ds(place + at, 64), col(c)] for c in range(9)]
                for c in range(9):
                    out[at : at + 64, col(c)] = coords[c].astype(out.dtype)
                seen = seen_by_kind(to_matrix(coords))
                fresh = weight_grads(parts_in(ref, at), seen)
                grads = [n if o is None else o + n for o, n in zip(grads, fresh)]
        first = d1_ref[:HALF, :LANES] + d1_ref[HALF:, LANES:]
        place = 0
        for value in (*grads, dw2_ref[...], first[:BASES]):
            grads_ref[place : place + value.shape[0], :] = value.astype(BF16)
            place += value.shape[0]
        biases = [first[BASES : BASES + 1]]
        for ref in (d2_ref, d3_ref):
            deep = ref.shape[0] - 16
            for n in range(ref.shape[1] // LANES):
                grads_ref[place : place + deep, :] = ref[:deep, col(n)].astype(BF16)
                biases.append(ref[deep : deep + 1, col(n)])
                place += deep
        biases.append(jnp.zeros((grads_ref.shape[0] - place - len(biases), LANES), F32))
        grads_ref[place:, :] = jnp.concatenate(biases, axis=0).astype(BF16)


def unpack_kernel(grads_ref, *out_refs):
    small, g_w1, g_w2, g_w3 = out_refs[:6], out_refs[6], out_refs[8], out_refs[10]
    place = 0
    for ref in (*small, g_w1):
        ref[...] = grads_ref[place : place + ref.shape[0], :].astype(F32)
        place += ref.shape[0]
    for ref in (g_w2, g_w3):
        for n in range(ref.shape[1] // LANES):
            ref[:, col(n)] = grads_ref[place : place + ref.shape[0], :].astype(F32)
            place += ref.shape[0]
    biases = grads_ref[place : place + 16, :].astype(F32)
    row = 0
    for ref in (out_refs[7], out_refs[9], out_refs[11]):
        for n in range(ref.shape[1] // LANES):
            ref[:, col(n)] = biases[row : row + 1, :]
            row += 1


def final_kernel(
    own_ref, near_ref, far_ref, atoms_ref, outgrad_ref, iso1_ref, anti1_ref, sym1_ref, out_ref
):
    weights = (iso1_ref[...], anti1_ref[...], sym1_ref[...])
    grad_mixed = [
        own_ref[:, col(c)] + near_ref[:, col(c)].astype(F32) + far_ref[:, col(c)].astype(F32)
        for c in range(9)
    ]
    back = flat(to_matrix(primal_of_dual(back_parts(to_matrix(grad_mixed), weights)[1])))
    values = [atoms_ref[c].astype(F32) for c in range(9)]
    inverse = 1.0 / (1.0 + total([v * v for v in values]))
    grad = [outgrad_ref[c].astype(F32) + back[c] for c in range(9)]
    along = total([g * v for g, v in zip(grad, values)]) * (2.0 * inverse)
    for c in range(9):
        out_ref[c] = (grad[c] - values[c] * along) * inverse


def whole(shape):
    return pl.BlockSpec(shape, lambda *_: (0,) * len(shape), pipeline_mode=pl.Buffered(1))


def block(shape):
    return pl.BlockSpec(shape, lambda i, *_: (i,) + (0,) * (len(shape) - 1))


def shape_of(shape, kind):
    return jax.ShapeDtypeStruct(shape, kind)


def part(value, index):
    return lax.dynamic_index_in_dim(value, index, 0, keepdims=False)


def reduce_everywhere(value, axes, beside):
    beside = list(beside)

    def between(v):
        return beside.pop(0)(v) if beside else v

    peers = math.prod(lax.axis_size(a) for a in axes)
    me = lax.axis_index(axes)
    runs, at = [], 1
    while at < peers:
        size = min(2 if at == 1 else 4, peers // at)
        runs.append((at, size))
        at *= size

    def swapped(v, by):
        return lax.ppermute(v, axes, [(i, i ^ by) for i in range(peers)])

    for at, size in runs[:-1]:
        shares = value.reshape(size, value.shape[0] // size, value.shape[1])
        mine = me // at % size
        kept = part(shares, mine).astype(F32)
        for k in range(1, size):
            kept = kept + swapped(part(shares, mine ^ k), k * at).astype(F32)
        value = between(kept.astype(BF16))
    at, size = runs[-1]
    kept = value.astype(F32)
    for k in range(1, size):
        kept = kept + swapped(value, k * at).astype(F32)
    value = between(kept.astype(BF16))
    for at, size in runs[-2::-1]:
        mine = me // at % size
        full = jnp.zeros((size,) + value.shape, value.dtype)
        full = lax.dynamic_update_index_in_dim(full, value, mine, 0)
        for k in range(1, size):
            full = lax.dynamic_update_index_in_dim(full, swapped(value, k * at), mine ^ k, 0)
        value = between(full.reshape(size * value.shape[0], value.shape[1]))
    return value


def local(
    atoms, neighbours, live_mask, distances,
    w_iso1, w_anti1, w_sym1, w_rad1, b_rad1, w_rad2, b_rad2, w_rad3, b_rad3,
    w_iso2, w_anti2, w_sym2, out_grad,
):
    rows, _, channels = atoms.shape
    slots = neighbours.shape[1]
    halo = MOL_MOST
    wide = 9 * channels
    ext = rows + 2 * halo
    edges = GROUP * slots
    chunk_count = rows // GROUP
    steps = 4
    chunks = chunk_count // steps
    block_atoms = rows // steps
    block_edges = block_atoms * slots
    vmem = 62 * 1024 * 1024
    me = lax.axis_index(AXES)
    peers = math.prod(lax.axis_size(a) for a in AXES)
    near_pairs = [(i, i ^ 1) for i in range(peers) if i ^ 1 < peers]
    far_pairs = [(i, i + 1 - 2 * (1 - i % 2)) for i in range(1, peers - 1)]

    by_component = jnp.swapaxes(atoms, 0, 1)
    out_grad_by_component = jnp.swapaxes(out_grad, 0, 1)
    near = lax.ppermute(by_component, AXES, near_pairs)
    far = lax.ppermute(by_component, AXES, far_pairs)

    links = neighbours - (me * rows - halo)
    edge_args = [jnp.swapaxes(v, 0, 1) for v in (distances, live_mask, links)]
    edge_specs = [whole(v.shape) for v in edge_args]
    edge_scratch = [pltpu.VMEM((rows, slots), F32)] * 3
    first = jnp.min(jnp.min(links, axis=1).reshape(chunk_count, GROUP), axis=1)
    last = jnp.max(jnp.max(links, axis=1).reshape(chunk_count, GROUP), axis=1)
    count = (last - first) // WINDOW + 1
    windows = jnp.stack([jnp.append(first, me % 2), jnp.append(count, 0)], axis=1)

    biases = jnp.concatenate([b_rad1, b_rad2, b_rad3]).reshape(-1, LANES)
    mid_width, last_width = w_rad2.shape[1], w_rad3.shape[1]
    small = whole((channels, channels))
    components = pl.BlockSpec((9, block_atoms, channels), lambda i: (0, i, 0))
    smem = pl.BlockSpec(memory_space=pltpu.SMEM)
    net_args = (w_rad1, w_rad2, w_rad3, biases)
    net_specs = [whole(v.shape) for v in net_args]
    net_scratch = [
        pltpu.VMEM((LANES, 2 * channels), BF16),
        pltpu.VMEM((2 * channels, mid_width), BF16),
        pltpu.VMEM((mid_width, last_width), BF16), pltpu.VMEM((1, last_width), F32),
    ]
    net0 = pl.pallas_call(
        network_kernel,
        grid=(AHEAD,),
        in_specs=edge_specs[:2] + net_specs,
        out_specs=[
            block((edges, KEPT)), block((edges, last_width)), block((edges // 2, LANES))
        ],
        out_shape=[
            shape_of((AHEAD * edges, KEPT), BF16), shape_of((AHEAD * edges, last_width), F32),
            shape_of((AHEAD * edges // 2, LANES), BF16),
        ],
        scratch_shapes=edge_scratch[:2] + net_scratch,
        compiler_params=pltpu.CompilerParams(vmem_limit_bytes=vmem),
        cost_estimate=pl.CostEstimate(
            flops=2 * block_edges * 135168, bytes_accessed=block_edges * KEPT * 2, transcendentals=0
        ),
        name="network",
    )(*edge_args[:2], *net_args)

    grad_rows = 6 * channels + BASES + mid_width // LANES * channels
    grad_rows += last_width // LANES * mid_width + 16
    grad_rows = -(-grad_rows // 128) * 128
    updated, rim_near, own_grad, rim_far, grads = pl.pallas_call(
        main_kernel,
        grid=(steps,),
        in_specs=[
            smem, whole(near.shape), whole(by_component.shape), whole(far.shape),
            components, *edge_specs, *net_specs,
            small, small, small, small, small, small,
            *[pl.BlockSpec(memory_space=pl.ANY)] * 3,
        ],
        out_specs=[
            components, whole((halo, wide)), whole((rows, wide)), whole((halo, wide)),
            whole((grad_rows, channels)),
        ],
        out_shape=[
            shape_of((9, rows, channels), BF16),
            shape_of((halo, wide), BF16), shape_of((rows, wide), F32),
            shape_of((halo, wide), BF16), shape_of((grad_rows, channels), BF16),
        ],
        scratch_shapes=[
            pltpu.VMEM((ext + WINDOW, wide), BF16),
            pltpu.VMEM((block_edges, KEPT), BF16),
            pltpu.VMEM((block_edges, KEPT), BF16),
            pltpu.VMEM((block_edges, last_width), F32),
            pltpu.VMEM((block_edges, last_width), F32),
            pltpu.VMEM((block_edges // 2, LANES), BF16),
            pltpu.VMEM((block_edges // 2, LANES), BF16),
            pltpu.VMEM((block_edges, wide), BF16),
            pltpu.VMEM((block_atoms, wide), F32),
            pltpu.VMEM((2 * block_atoms, wide + 2 * channels), BF16),
            pltpu.VMEM((ext + WINDOW, wide), F32),
            pltpu.VMEM((mid_width + 16, last_width), F32),
            pltpu.VMEM((channels + 16, mid_width), F32),
            pltpu.VMEM((LANES, 2 * channels), F32),
            pltpu.VMEM((3 * channels, channels), F32),
            *net_scratch,
            *edge_scratch,
            pltpu.SemaphoreType.DMA((AHEAD, 3)),
        ],
        compiler_params=pltpu.CompilerParams(vmem_limit_bytes=vmem),
        name="main",
    )(
        windows, near, by_component, far, out_grad_by_component, *edge_args, *net_args,
        w_iso1, w_anti1, w_sym1, w_iso2, w_anti2, w_sym2, *net0,
    )

    kept = {}

    def nothing(value):
        return value

    def send_rims(value):
        value, to_near, to_far = lax.optimization_barrier((value, rim_near, rim_far))
        kept["near"] = lax.ppermute(to_near, AXES, near_pairs)
        kept["far"] = lax.ppermute(to_far, AXES, far_pairs)
        return value

    def have_rims(value):
        value, kept["near"], kept["far"] = lax.optimization_barrier(
            (value, kept["near"], kept["far"])
        )
        return value

    def finish(value):
        grad_atoms = pl.pallas_call(
            final_kernel,
            out_shape=shape_of((9, rows, channels), F32),
            compiler_params=pltpu.CompilerParams(vmem_limit_bytes=vmem),
            name="final",
        )(
            own_grad, kept["near"], kept["far"], by_component, out_grad_by_component,
            w_iso1, w_anti1, w_sym1,
        )
        value, updated_out, grad_out = lax.optimization_barrier((value, updated, grad_atoms))
        kept["outs"] = jnp.swapaxes(updated_out, 0, 1), jnp.swapaxes(grad_out, 0, 1)
        return value

    summed = reduce_everywhere(grads, AXES, (nothing, send_rims, have_rims, finish))
    square_shape = (channels, channels)
    shapes = [square_shape] * 6 + [w_rad1.shape, (1, channels), w_rad2.shape, (1, mid_width)]
    shapes += [w_rad3.shape, (1, last_width)]
    out = pl.pallas_call(
        unpack_kernel,
        out_shape=[shape_of(shape, F32) for shape in shapes],
        compiler_params=pltpu.CompilerParams(vmem_limit_bytes=16 * 1024 * 1024),
        name="unpack",
    )(summed)
    return (
        *kept["outs"],
        *out[:3],
        *(v if n % 2 == 0 else v[0] for n, v in enumerate(out[6:])),
        *out[3:6],
    )


def solution(mesh):
    split3 = P(AXES, None, None)
    split2 = P(AXES, None)
    return jax.shard_map(
        local,
        mesh=mesh,
        in_specs=(split3, split2, split2, split2) + (P(),) * 12 + (split3,),
        out_specs=(split3, split3) + (P(),) * 12,
        check_vma=False,
    )
```

```python
import functools
import math

import jax
import jax.numpy as jnp
from jax import lax
from jax.experimental import pallas as pl
from jax.experimental.pallas import tpu as pltpu
from jax.sharding import PartitionSpec as P

MOL_MOST = 256
CUTOFF = 5.0
LANES = 128
GROUP = 8
BASES = 32
UNROLL = 2
PAIRS = ((0, 1), (2, 3), (4, 5), (6, 7), (8,))
GATHER = "0k0D0E0A0d0B0a0C0b1k0c1D1E1A1d1B1a1C1b1c"
SCHEDULE = "".join(n + s for n in "01" for s in "HaTDb0GJ1cWdp2E3eF4xVyUz")
WINDOW = 256
KIND = (0, 1, 1, 1, 2, 2, 2, 2, 2)
AXES = ("edge", "grp")
F32 = jnp.float32
BF16 = jnp.bfloat16


def col(c):
    return slice(c * LANES, (c + 1) * LANES)


def to_matrix(coords):
    t, a01, a02, a12, s01, s02, s12, s00, s11 = coords
    return [
        [t + s00, s01 + a01, s02 + a02],
        [s01 - a01, t + s11, s12 + a12],
        [s02 - a02, s12 - a12, t - s00 - s11],
    ]


def primal(m):
    t = (m[0][0] + m[1][1] + m[2][2]) * (1.0 / 3.0)
    return [
        t,
        0.5 * (m[0][1] - m[1][0]),
        0.5 * (m[0][2] - m[2][0]),
        0.5 * (m[1][2] - m[2][1]),
        0.5 * (m[0][1] + m[1][0]),
        0.5 * (m[0][2] + m[2][0]),
        0.5 * (m[1][2] + m[2][1]),
        m[0][0] - t,
        m[1][1] - t,
    ]


def dual(m):
    return [
        m[0][0] + m[1][1] + m[2][2],
        m[0][1] - m[1][0],
        m[0][2] - m[2][0],
        m[1][2] - m[2][1],
        m[0][1] + m[1][0],
        m[0][2] + m[2][0],
        m[1][2] + m[2][1],
        m[0][0] - m[2][2],
        m[1][1] - m[2][2],
    ]


def primal_of_dual(d):
    third = 1.0 / 3.0
    return (
        [d[0] * third]
        + [0.5 * v for v in d[1:7]]
        + [(2.0 * d[7] - d[8]) * third, (2.0 * d[8] - d[7]) * third]
    )


def product(a, b):
    return [
        [a[p][0] * b[0][q] + a[p][1] * b[1][q] + a[p][2] * b[2][q] for q in range(3)]
        for p in range(3)
    ]


def add(a, b):
    return [[a[p][q] + b[p][q] for q in range(3)] for p in range(3)]


def both_ways(a, b):
    return add(product(a, b), product(b, a))


def flip(m):
    return [[m[q][p] for q in range(3)] for p in range(3)]


def flat(m):
    return [m[p][q] for p in range(3) for q in range(3)]


def square(parts):
    return [list(parts[0:3]), list(parts[3:6]), list(parts[6:9])]


def total(values):
    out = values[0]
    for v in values[1:]:
        out = out + v
    return out


def dot(a, b):
    return jnp.dot(a, b, preferred_element_type=F32)


def dot_first(a, b):
    return lax.dot_general(a, b, (((0,), (0,)), ((), ())), preferred_element_type=F32)


def dot_last(a, b):
    return lax.dot_general(a, b, (((1,), (1,)), ((), ())), preferred_element_type=F32)


def stack(values):
    return jnp.concatenate([v.astype(BF16) for v in values], axis=0)


def pieces_of(value, rows):
    return [value[n * rows : (n + 1) * rows] for n in range(value.shape[0] // rows)]


def rounded_parts(m):
    coords = primal(m)
    return [v.astype(BF16) for v in coords + [-coords[7] - coords[8]]]


def parts_in(atoms_ref, at):
    values = [atoms_ref[c, at : at + BLOCK, :].astype(F32) for c in range(9)]
    scale = 1.0 / (1.0 + total([v * v for v in values]))
    return rounded_parts(square([v * scale for v in values]))


def mix_parts(parts, weights):
    rows = parts[0].shape[0]
    t, a01, a02, a12, s01, s02, s12, s00, s11, s22 = (
        pieces_of(dot(parts[0], weights[0]), rows)
        + pieces_of(dot(stack(parts[1:4]), weights[1]), rows)
        + pieces_of(dot(stack(parts[4:10]), weights[2]), rows)
    )
    return [
        [t + s00, s01 + a01, s02 + a02],
        [s01 - a01, t + s11, s12 + a12],
        [s02 - a02, s12 - a12, t + s22],
    ]


def seen_by_kind(grad):
    diagonal = [grad[0][0], grad[1][1], grad[2][2]]
    skew = [grad[0][1], grad[1][0], grad[0][2], grad[2][0], grad[1][2], grad[2][1]]
    return [stack(v) for v in (diagonal, skew, skew + diagonal)]


def back_parts(grad, weights):
    rows = grad[0][0].shape[0]
    seen = seen_by_kind(grad)
    iso, anti, sym = (pieces_of(dot_last(v, w), rows) for v, w in zip(seen, weights))
    coords = [
        iso[0] + iso[1] + iso[2],
        anti[0] - anti[1], anti[2] - anti[3], anti[4] - anti[5],
        sym[0] + sym[1], sym[2] + sym[3], sym[4] + sym[5],
        sym[6] - sym[8], sym[7] - sym[8],
    ]
    return seen, coords


def weight_grads(parts, seen):
    p = parts
    lefts = (
        [p[0]] * 3,
        [p[1], -p[1], p[2], -p[2], p[3], -p[3]],
        [p[4], p[4], p[5], p[5], p[6], p[6], p[7], p[8], p[9]],
    )
    return [dot_first(stack(left), right) for left, right in zip(lefts, seen)]


def half_silu(u):
    t = jnp.tanh(u)
    p = 1.0 + t
    act = u * p
    return act, p + act * (1.0 - t)


SLOPE3, ACT2, SLOPE2 = slice(0, 384), slice(384, 640), slice(640, 896)
ACT1, SLOPE1 = slice(896, 1024), slice(1024, 1152)
KEPT = 1152
BLOCK = 32
HALF = 64
AHEAD = 6

ORDER = ((0, 1), (1, 0), (0, 2), (2, 0), (1, 2), (2, 1), (0, 0), (1, 1), (2, 2))


def over_lanes(block, slots, lanes=LANES):
    return jnp.concatenate(
        [jnp.broadcast_to(block[:, s : s + 1], (block.shape[0], lanes)) for s in slots], axis=0
    )


class Network:
    def __init__(self, dist, gate, out, factors, basis, at, refs):
        self.dist, self.gate8 = dist, gate
        self.out, self.factors, self.basis, self.refs = out, factors, basis, refs
        edges = dist.shape[0] * dist.shape[1]
        self.here = pl.ds(pl.multiple_of(at * edges, edges), edges)
        self.half = pl.ds(pl.multiple_of(at * (edges // 2), edges // 2), edges // 2)

    def run(self):
        self.layer1()
        self.active1()
        self.layer2()
        self.active2(0)
        self.active2(1)
        self.layer3()
        for kind in range(3):
            self.active3(kind)

    def layer1(self):
        slots = self.dist.shape[1]
        self.gate = over_lanes(self.gate8, range(slots))
        low = over_lanes(self.dist, range(slots // 2))
        lane = lax.broadcasted_iota(jnp.int32, low.shape, 1)
        dist = jnp.where(lane < HALF, low, over_lanes(self.dist, range(slots // 2, slots)))
        lane = lane % HALF
        off = dist - lane.astype(F32) * (CUTOFF / 31.0)
        basis = jnp.exp(off * off * (-0.5 * (31.0 / CUTOFF) ** 2))
        last = jnp.where(lane == BASES, 1.0, 0.0)
        basis = jnp.where(lane < BASES, basis, last).astype(BF16)
        self.basis[self.half, :] = basis
        inner = dot(basis, self.refs[0][...])
        self.inner = jnp.concatenate([inner[:, :LANES], inner[:, LANES:]], axis=0)

    def active1(self):
        act, slope = half_silu(self.inner)
        self.act = act.astype(BF16)
        self.out[self.here, ACT1] = self.act
        self.out[self.here, SLOPE1] = slope.astype(BF16)

    def layer2(self):
        one = lax.broadcasted_iota(jnp.int32, self.act.shape, 1) == 0
        one = jnp.where(one, 1.0, 0.0).astype(BF16)
        self.inner = dot(jnp.concatenate([self.act, one], axis=1), self.refs[1][...])

    def active2(self, n):
        act, slope = half_silu(self.inner[:, col(n)])
        act = act.astype(BF16)
        self.act = jnp.concatenate([self.act, act], axis=1) if n else act
        self.out[self.here, col(ACT2.start // LANES + n)] = act
        self.out[self.here, col(SLOPE2.start // LANES + n)] = slope.astype(BF16)

    def layer3(self):
        self.inner = dot(self.act, self.refs[2][...])

    def active3(self, kind):
        act, slope = half_silu(self.inner[:, col(kind)] + self.refs[3][:, col(kind)])
        self.factors[self.here, col(kind)] = act * self.gate
        self.out[self.here, col(kind)] = (slope * (0.5 * self.gate)).astype(BF16)


def halve_weights(w1_ref, w2_ref, w3_ref, bias_ref, w1_s, w2_s, w3_s, b3_s):
    half = 0.5 * bias_ref[...].astype(F32)

    def biased(weights, bias, rows):
        below = lax.broadcasted_iota(jnp.int32, (rows - weights.shape[0], bias.shape[1]), 0)
        bias = jnp.where(below == 0, bias, 0.0)
        return jnp.concatenate([0.5 * weights.astype(F32), bias], axis=0).astype(BF16)

    w1_s[...] = jnp.zeros_like(w1_s)
    first = biased(w1_ref[...], half[0:1], HALF)
    w1_s[:HALF, :LANES] = first
    w1_s[HALF:, LANES:] = first
    wide2 = jnp.concatenate([half[1:2], half[2:3]], axis=1)
    w2_s[...] = biased(w2_ref[...], wide2, w2_s.shape[0])
    w3_s[...] = (0.5 * w3_ref[...].astype(F32)).astype(BF16)
    b3_s[...] = jnp.concatenate([half[3:4], half[4:5], half[5:6]], axis=1)


def by_atom(ref):
    return jnp.transpose(ref[...].astype(F32))


def gating(dist, live):
    return 0.5 * (jnp.cos(math.pi * dist / CUTOFF) + 1.0) * live


def network_kernel(
    dist_ref, live_ref, w1_raw, w2_raw, w3_raw, bias_ref, out_ref, fac_ref, basis_ref, dist_s, gate_s, w1_s, w2_s,
    w3_s, b3_s,
):
    net_refs = (w1_s, w2_s, w3_s, b3_s)

    @pl.when(pl.program_id(0) == 0)
    def _():
        halve_weights(w1_raw, w2_raw, w3_raw, bias_ref, *net_refs)
        dist_s[...] = by_atom(dist_ref)
        gate_s[...] = gating(dist_s[...], by_atom(live_ref))

    mine = pl.ds(pl.multiple_of(pl.program_id(0) * GROUP, GROUP), GROUP)
    Network(dist_s[mine, :], gate_s[mine, :], out_ref, fac_ref, basis_ref, 0, net_refs).run()


def window_key(link, first, w):
    start = first + w * WINDOW
    base = pl.multiple_of(first // 16 * 16 + w * WINDOW, 16)
    off = first % 16
    rel = link - start.astype(F32)
    key = rel + off.astype(F32)
    key = jnp.where(key >= WINDOW, key - WINDOW, key)
    key = jnp.where(jnp.logical_and(rel >= 0, rel < WINDOW), key, -1.0)
    return key, base, off


def main_kernel(
    win_ref, near_ref, own_ref, far_ref, outgrad_ref, dist_ref, live_ref, link_ref,
    w1_raw, w2_raw, w3_raw, bias_ref,
    iso1_ref, anti1_ref, sym1_ref, iso2_ref, anti2_ref, sym2_ref, net_first, fac_first, basis_first,
    upd_ref, rim_near_ref, own_out_ref, rim_far_ref, mine_ref, other_ref,
    table, parts_s, net_a, net_b, fac_a, fac_b, basis_a, basis_b, x_s, msg_s, gm_s, spread,
    d3_ref, d2_ref, d1_ref, dw2_ref, w1_ref, w2_ref, w3_ref, b3_ref,
    dist_s, gate_s, link_s, sems,
):
    step = pl.program_id(0)
    steps = pl.num_programs(0)
    edges = GROUP * link_ref.shape[0]
    halo = near_ref.shape[1]
    odd = win_ref[win_ref.shape[0] - 1, 0]
    far_side = halo + own_ref.shape[1]
    near_at = pl.multiple_of((1 - odd) * far_side, 64)
    far_at = pl.multiple_of(odd * far_side, 64)
    atoms = upd_ref.shape[1]
    chunks = atoms // GROUP
    slots = edges // GROUP
    pairs = edges // 16
    wide = 9 * LANES
    radial = (w1_ref, w2_ref, w3_ref, b3_ref)

    def chunk_atoms(index):
        return pl.ds(pl.multiple_of(index * GROUP, GROUP), GROUP)

    def fetches(j):
        here = pl.ds(pl.multiple_of(j * edges, edges), edges)
        half = pl.ds(pl.multiple_of(j * (edges // 2), edges // 2), edges // 2)
        return (
            pltpu.make_async_copy(net_first.at[here], net_a.at[here], sems.at[j, 0]),
            pltpu.make_async_copy(fac_first.at[here], fac_a.at[here], sems.at[j, 1]),
            pltpu.make_async_copy(basis_first.at[half], basis_a.at[half], sems.at[j, 2]),
        )

    @pl.when(step == 0)
    def _():
        for j in range(AHEAD):
            for copy in fetches(j):
                copy.start()
        halve_weights(w1_raw, w2_raw, w3_raw, bias_ref, *radial)
        dist_s[...] = by_atom(dist_ref)
        gate_s[...] = gating(dist_s[...], by_atom(live_ref))
        link_s[...] = by_atom(link_ref)
        weights = (iso1_ref[...], anti1_ref[...], sym1_ref[...])
        for ref, place in ((near_ref, near_at), (own_ref, halo), (far_ref, far_at)):
            for at in range(0, ref.shape[1], BLOCK):
                here = pl.ds(place + at, BLOCK)
                parts = parts_in(ref, at)
                for c, v in enumerate(parts):
                    parts_s[here, col(c)] = v
                mixed = mix_parts(parts, weights)
                for n, (p, q) in enumerate(ORDER):
                    table[here, col(n)] = mixed[p][q].astype(BF16)
        place = far_side + halo
        table[place:, :] = jnp.zeros((table.shape[0] - place, wide), BF16)
        d3_ref[...] = jnp.zeros_like(d3_ref)
        d2_ref[...] = jnp.zeros_like(d2_ref)
        d1_ref[...] = jnp.zeros_like(d1_ref)
        dw2_ref[...] = jnp.zeros_like(dw2_ref)
        spread[...] = jnp.zeros_like(spread)

        @pl.loop(AHEAD, chunks)
        def _(j):
            mine = chunk_atoms(j)
            Network(dist_s[mine, :], gate_s[mine, :], net_a, fac_a, basis_a, j, radial).run()

    class Gather:
        def __init__(self, fac, j, w, more):
            self.j, self.w, self.fac, self.more, self.got = j, w, fac, more, {}
            self.here = pl.ds(pl.multiple_of(j * edges, edges), edges)
            self.to = pl.ds(pl.multiple_of(j * GROUP, GROUP), GROUP)

        def hot(self):
            index = step * chunks + self.j
            key, self.base, off = window_key(
                link_s[chunk_atoms(index), :], win_ref[index, 0], self.w
            )
            near = lax.broadcasted_iota(jnp.int32, (edges, WINDOW), 1).astype(F32)
            self.key = (over_lanes(key, range(slots), WINDOW) == near).astype(BF16)
            kept = lax.broadcasted_iota(jnp.int32, (16, LANES), 0) >= off
            self.kept = jnp.where(kept, 1.0, 0.0).astype(BF16)[:, 0:1]

        def rows_of(self, first, past):
            lanes = slice(first * LANES, past * LANES)
            top = table[pl.ds(self.base, 16), lanes] * self.kept
            top += table[pl.ds(self.base + WINDOW, 16), lanes] * (1.0 - self.kept)
            rest = table[pl.ds(self.base + 16, WINDOW - 16), lanes]
            got = dot(self.key, jnp.concatenate([top, rest], axis=0))
            for n in range(past - first):
                self.got[first + n] = got[:, col(n)]

        def use(self, c, x):
            rounded = x.astype(BF16)
            message = self.fac[self.here, col(KIND[c])] * x
            message = jnp.sum(message.reshape(slots, GROUP, LANES), axis=0)
            if self.more:
                rounded += x_s[self.here, col(c)]
                message += msg_s[self.to, col(c)]
            x_s[self.here, col(c)] = rounded
            msg_s[self.to, col(c)] = message

        def pair(self, n):
            one, other = self.got.pop(2 * n), self.got.pop(2 * n + 1)
            self.use(1 + n, one - other)
            self.use(4 + n, one + other)

        def diagonal(self):
            x00, x11, x22 = (self.got.pop(n) for n in (6, 7, 8))
            trace = x00 + x11 + x22
            third = trace * (1.0 / 3.0)
            self.use(0, trace)
            self.use(7, x00 - third)
            self.use(8, x11 - third)

    def gather(fac, places, w, more, order):
        steps_of = {
            "k": lambda g: g.hot(),
            "A": lambda g: g.rows_of(0, 2), "B": lambda g: g.rows_of(2, 4),
            "C": lambda g: g.rows_of(4, 6), "D": lambda g: g.rows_of(6, 8),
            "E": lambda g: g.rows_of(8, 9), "a": lambda g: g.pair(0), "b": lambda g: g.pair(1),
            "c": lambda g: g.pair(2), "d": lambda g: g.diagonal(),
        }
        each = [Gather(fac, j, w, more) for j in places]
        for which, name in zip(order[::2], order[1::2]):
            if int(which) < len(each):
                steps_of[name](each[int(which)])

    even = step % 2 == 0

    def collect(fac):
        @pl.loop(0, chunks // UNROLL)
        def _(pair):
            if fac is fac_a:

                @pl.when(jnp.logical_and(step == 0, pair < AHEAD // UNROLL))
                def _():
                    for n in range(UNROLL):
                        for copy in fetches(pair * UNROLL + n):
                            copy.wait()

            gather(fac, [pair * UNROLL + n for n in range(UNROLL)], 0, False, GATHER)

        @pl.loop(0, chunks)
        def _(j):
            @pl.loop(1, win_ref[step * chunks + j, 1])
            def _(w):
                gather(fac, [j], w, True, GATHER)

    @pl.when(even)
    def _():
        collect(fac_a)

    @pl.when(jnp.logical_not(even))
    def _():
        collect(fac_b)

    weights2 = (iso2_ref[...], anti2_ref[...], sym2_ref[...])
    put = pl.ds(pl.multiple_of(halo + step * atoms, 16), atoms)
    mixed = [[None] * 3 for _ in range(3)]
    for n, (p, q) in enumerate(ORDER):
        mixed[p][q] = table[put, col(n)].astype(F32)
    sums = [msg_s[:, col(c)] for c in range(9)]
    messages = to_matrix([sums[0] * (1.0 / 3.0)] + [0.5 * v for v in sums[1:7]] + sums[7:])
    paired = both_ways(mixed, messages)
    inverse = 1.0 / (1.0 + total([v * v for v in flat(paired)]))
    pair_coords = primal(paired)
    mid = [(v * inverse).astype(BF16) for v in pair_coords]
    mid.append(((-pair_coords[7] - pair_coords[8]) * inverse).astype(BF16))
    update = mix_parts(mid, weights2)
    at = pl.ds(pl.multiple_of(step * atoms, 16), atoms)
    values = [own_ref[c, at, :].astype(F32) for c in range(9)]
    inverse_in = 1.0 / (1.0 + total([v * v for v in values]))
    squared = flat(product(update, update))
    for c, (v, u, s) in enumerate(zip(values, flat(update), squared)):
        upd_ref[c] = (v * inverse_in + u + s).astype(BF16)
    out_grad = square([outgrad_ref[c].astype(F32) for c in range(9)])
    grad_update = add(out_grad, both_ways(out_grad, flip(update)))
    seen, mid_dual = back_parts(grad_update, weights2)
    for kind, grad in enumerate(weight_grads(mid, seen)):
        dw2_ref[kind * LANES : (kind + 1) * LANES, :] += grad
    projected = total([a * b for a, b in zip(mid_dual, pair_coords)]) * (2.0 * inverse * inverse)
    grad_paired = to_matrix([v * inverse for v in primal_of_dual(mid_dual)])
    grad_paired = [
        [grad_paired[p][q] - paired[p][q] * projected for q in range(3)] for p in range(3)
    ]
    from_pair = primal(both_ways(grad_paired, flip(messages)))
    for c in range(9):
        spread[put, col(c)] += from_pair[c]
    grad_messages = [
        [v.astype(BF16).astype(F32) for v in row] for row in both_ways(flip(mixed), grad_paired)
    ]
    for c, v in enumerate(primal(grad_messages) + dual(grad_messages)[7:]):
        twice = v.reshape(chunks, 1, GROUP, LANES)
        twice = jnp.concatenate([twice, twice], axis=1).reshape(2 * atoms, LANES)
        gm_s[:, col(c)] = twice.astype(BF16)

    def chunk_places(j):
        here = pl.ds(pl.multiple_of(j * edges, edges), edges)
        two = pl.ds(pl.multiple_of(j * 2 * GROUP, 2 * GROUP), 2 * GROUP)
        return here, two

    def scatter_hot(j, w):
        index = step * chunks + j
        key, base, off = window_key(link_s[chunk_atoms(index), :], win_ref[index, 0], w)
        lane = lax.broadcasted_iota(jnp.int32, (slots, edges), 1)
        own_slot = lax.broadcasted_iota(jnp.int32, (slots, edges), 0) == lane // GROUP
        copies = dot(key.astype(BF16), jnp.where(own_slot, 1.0, 0.0).astype(BF16))
        lane = lax.broadcasted_iota(jnp.int32, (GROUP, edges), 1)
        own_atom = lax.broadcasted_iota(jnp.int32, (GROUP, edges), 0) == lane % GROUP
        key = jnp.sum(jnp.where(own_atom, copies, 0.0), axis=0, keepdims=True)
        near = lax.broadcasted_iota(jnp.int32, (WINDOW, edges), 0).astype(F32)
        kept = lax.broadcasted_iota(jnp.int32, (16, LANES), 0) >= off
        return (key == near).astype(BF16), base, kept

    def scatter(fac, j, hot_base_kept, cs):
        here, two = chunk_places(j)
        hot, base, kept = hot_base_kept
        terms = [
            (fac[here, col(KIND[c])].astype(BF16).reshape(pairs, 16, LANES) * gm_s[two, col(c)]).reshape(
                edges, LANES
            )
            for c in cs
        ]
        sums = dot(hot, jnp.concatenate(terms, axis=1))
        for n, c in enumerate(cs):
            top = sums[:16, col(n)]
            spread[pl.ds(base, 16), col(c)] += jnp.where(kept, top, 0.0)
            spread[pl.ds(base + WINDOW, 16), col(c)] += jnp.where(kept, 0.0, top)
            spread[pl.ds(base + 16, WINDOW - 16), col(c)] += sums[16:, col(n)]

    class Backward:
        def __init__(self, j, now, after):
            self.j, self.now = j, now
            self.net, self.fac, self.basis = now
            self.here, self.two = chunk_places(j)
            self.half = pl.ds(pl.multiple_of(j * (edges // 2), edges // 2), edges // 2)
            self.ahead = None
            if after is not None:
                mine = chunk_atoms((step + 1) * chunks + j)
                self.ahead = Network(dist_s[mine, :], gate_s[mine, :], *after, j, radial)

        def hot(self):
            self.key = scatter_hot(self.j, 0)

        def spread(self, n):
            scatter(self.fac, self.j, self.key, PAIRS[n])

        def terms(self):
            here, two = self.here, self.two
            terms = [
                x_s[here, col(c)].reshape(pairs, 16, LANES) * gm_s[two, col(c if c < 7 else c + 2)]
                for c in range(9)
            ]
            grads = [terms[0], total(terms[1:4]), total(terms[4:9])]
            grad3 = jnp.concatenate([v.reshape(edges, LANES) for v in grads], axis=1)
            self.grad3 = grad3 * self.net[here, SLOPE3]

        def back3(self):
            self.inner2 = dot_last(self.grad3, w3_ref[...])

        def grads2(self, n):
            slope = self.net[self.here, col(SLOPE2.start // LANES + n)].astype(F32)
            grad2 = (self.inner2[:, col(n)] * slope).astype(BF16)
            self.grad2 = jnp.concatenate([self.grad2, grad2], axis=1) if n else grad2

        def back2(self):
            self.inner1 = dot_last(self.grad2, w2_ref[:LANES, :])

        def grads1(self):
            slope = self.net[self.here, SLOPE1].astype(F32)
            grad1 = (self.inner1 * slope).astype(BF16)
            self.grad1 = jnp.concatenate([grad1[: edges // 2], grad1[edges // 2 :]], axis=1)

        def weights3(self):
            ones = jnp.ones((16, edges), BF16)
            act2 = jnp.concatenate([jnp.transpose(self.net[self.here, ACT2]), ones], axis=0)
            d3_ref[...] += dot(act2, self.grad3)

        def weights2(self):
            ones = jnp.ones((16, edges), BF16)
            act1 = jnp.concatenate([jnp.transpose(self.net[self.here, ACT1]), ones], axis=0)
            d2_ref[...] += dot(act1, self.grad2)

        def weights1(self):
            d1_ref[...] += dot(jnp.transpose(self.basis[self.half, :]), self.grad1)

    def sweep(now, after):
        steps_of = {
            "H": lambda b: b.hot(), "T": lambda b: b.terms(),
            "0": lambda b: b.spread(0), "1": lambda b: b.spread(1), "2": lambda b: b.spread(2),
            "3": lambda b: b.spread(3), "4": lambda b: b.spread(4),
            "D": lambda b: b.back3(), "G": lambda b: b.grads2(0), "J": lambda b: b.grads2(1),
            "E": lambda b: b.back2(), "F": lambda b: b.grads1(),
            "W": lambda b: b.weights3(), "V": lambda b: b.weights2(), "U": lambda b: b.weights1(),
            "a": lambda b: b.ahead.layer1(), "b": lambda b: b.ahead.active1(),
            "c": lambda b: b.ahead.layer2(), "d": lambda b: b.ahead.active2(0), "p": lambda b: b.ahead.active2(1),
            "e": lambda b: b.ahead.layer3(), "x": lambda b: b.ahead.active3(0),
            "y": lambda b: b.ahead.active3(1), "z": lambda b: b.ahead.active3(2),
        }

        @pl.loop(0, chunks // UNROLL)
        def _(pair):
            both = [Backward(pair * UNROLL + n, now, after) for n in range(UNROLL)]
            for which, name in zip(SCHEDULE[::2], SCHEDULE[1::2]):
                if after is not None or not name.islower():
                    steps_of[name](both[int(which)])

        @pl.loop(0, chunks)
        def _(j):
            @pl.loop(1, win_ref[step * chunks + j, 1])
            def _(w):
                more = scatter_hot(j, w)
                for cs in PAIRS:
                    scatter(now[1], j, more, cs)

    last = step == steps - 1

    @pl.when(jnp.logical_and(even, jnp.logical_not(last)))
    def _():
        sweep((net_a, fac_a, basis_a), (net_b, fac_b, basis_b))

    @pl.when(jnp.logical_not(jnp.logical_or(even, last)))
    def _():
        sweep((net_b, fac_b, basis_b), (net_a, fac_a, basis_a))

    @pl.when(last)
    def _():
        sweep((net_b, fac_b, basis_b), None)
        grads = [None] * 3
        for out, place in (
            (rim_near_ref, near_at), (own_out_ref, halo), (rim_far_ref, far_at)
        ):
            coords = []
            for c in range(9):
                value = spread[pl.ds(place, out.shape[0]), col(c)]
                out[:, col(c)] = value.astype(out.dtype)
                coords.append(value)
            t, s00, s11 = coords[0], coords[7], coords[8]
            right = [3.0 * t] + [2.0 * v for v in coords[1:7]] + [s00, s11, -s00 - s11]
            left = [parts_s[pl.ds(place, out.shape[0]), col(c)] for c in range(10)]
            fresh = [
                dot_first(stack(left[lo:hi]), stack(right[lo:hi]))
                for lo, hi in ((0, 1), (1, 4), (4, 10))
            ]
            grads = [n if o is None else o + n for o, n in zip(grads, fresh)]
        first = d1_ref[:HALF, :LANES] + d1_ref[HALF:, LANES:]
        deep = d3_ref.shape[0] - 16
        thirds = [d3_ref[:deep, col(n)] for n in range(3)]
        biases = [first[BASES : BASES + 1]]
        biases += [d2_ref[LANES : LANES + 1, col(n)] for n in range(2)]
        biases += [d3_ref[deep : deep + 1, col(n)] for n in range(3)]
        biases.append(jnp.zeros((16 - len(biases), LANES), F32))
        biases = jnp.concatenate(biases, axis=0)
        halves = (
            [*thirds, d2_ref[:LANES, col(0)], first[:BASES], biases],
            [*grads, dw2_ref[...], d2_ref[:LANES, col(1)]],
        )

        def put_half(out, values):
            place = 0
            for value in values:
                out[place : place + value.shape[0], :] = value.astype(out.dtype)
                place += value.shape[0]
            out[place:, :] = jnp.zeros((out.shape[0] - place, LANES), out.dtype)

        for side in range(2):

            @pl.when(odd == side)
            def _():
                put_half(mine_ref, halves[side])
                put_half(other_ref, halves[1 - side])


def unpack_kernel(shares, place_ref, mine_ref, other_ref, *out_refs):
    small, (g_w1, g_b1, g_w2, g_b2, g_w3, g_b3) = out_refs[:6], out_refs[6:12]
    mine_s, other_s = out_refs[12:]
    rows = mine_ref.shape[0] // shares
    for n in range(shares):
        to = pl.ds(pl.multiple_of((place_ref[1] ^ n) * rows, 16), rows)
        mine_s[to, :] = mine_ref[n * rows : (n + 1) * rows, :].astype(F32)
        other_s[to, :] = other_ref[n * rows : (n + 1) * rows, :].astype(F32)

    def unpack(one, two):
        deep = g_w3.shape[0]
        for n in range(3):
            g_w3[:, col(n)] = one[n * deep : (n + 1) * deep, :]
        place = 3 * deep
        g_w2[:, col(0)] = one[place : place + LANES, :]
        place += LANES
        g_w1[...] = one[place : place + BASES, :]
        place += BASES
        biases = one[place : place + 16, :]
        row = 0
        for ref in (g_b1, g_b2, g_b3):
            count = ref.shape[0] // LANES
            for n in range(count):
                ref[col(n)] = biases[row + n]
            row += count
        for n, ref in enumerate(small):
            ref[...] = two[n * LANES : (n + 1) * LANES, :]
        g_w2[:, col(1)] = two[6 * LANES : 7 * LANES, :]

    @pl.when(place_ref[0] == 0)
    def _():
        unpack(mine_s, other_s)

    @pl.when(place_ref[0] == 1)
    def _():
        unpack(other_s, mine_s)


def final_kernel(
    own_ref, near_ref, far_ref, atoms_ref, outgrad_ref, iso1_ref, anti1_ref, sym1_ref, out_ref
):
    weights = (iso1_ref[...], anti1_ref[...], sym1_ref[...])
    grad_mixed = [
        own_ref[:, col(c)] + near_ref[:, col(c)].astype(F32) + far_ref[:, col(c)].astype(F32)
        for c in range(9)
    ]
    back = flat(to_matrix(primal_of_dual(back_parts(to_matrix(grad_mixed), weights)[1])))
    values = [atoms_ref[c].astype(F32) for c in range(9)]
    inverse = 1.0 / (1.0 + total([v * v for v in values]))
    grad = [outgrad_ref[c].astype(F32) + back[c] for c in range(9)]
    along = total([g * v for g, v in zip(grad, values)]) * (2.0 * inverse)
    for c in range(9):
        out_ref[c] = (grad[c] - values[c] * along) * inverse


def whole(shape):
    return pl.BlockSpec(shape, lambda *_: (0,) * len(shape), pipeline_mode=pl.Buffered(1))


def block(shape):
    return pl.BlockSpec(shape, lambda i, *_: (i,) + (0,) * (len(shape) - 1))


def shape_of(shape, kind):
    return jax.ShapeDtypeStruct(shape, kind)


def part(value, index):
    return lax.dynamic_index_in_dim(value, index, 0, keepdims=False)


def reduce_everywhere(mine, other, axes, beside):
    beside = list(beside)

    def between(v):
        return beside.pop(0)(v) if beside else v

    peers = math.prod(lax.axis_size(a) for a in axes)
    me = lax.axis_index(axes)
    runs, at = [], 2
    while at < peers:
        runs.append((at, min(4, peers // at)))
        at *= runs[-1][1]
    runs = runs[1:] + runs[:1]

    def swapped(v, by):
        return lax.ppermute(v, axes, [(i, i ^ by) for i in range(peers)])

    value = between(mine + swapped(other, 1).astype(F32))
    for at, size in runs[:-1]:
        shares = value.reshape(size, value.shape[0] // size, value.shape[1])
        own = me // at % size
        kept = part(shares, own)
        for k in range(1, size):
            kept = kept + swapped(part(shares, own ^ k).astype(BF16), k * at).astype(F32)
        value = between(kept)
    at, size = runs[-1]
    value = value.astype(BF16)
    terms = [value] + [swapped(value, k * at) for k in range(1, size)]
    terms[1] = between(terms[1])
    terms = [v.astype(F32) for v in terms]
    while len(terms) > 1:
        terms = [a + b for a, b in zip(terms[::2], terms[1::2])]
    value = between(terms[0].astype(BF16))
    for at, size in runs[-2:0:-1]:
        own = me // at % size
        full = jnp.zeros((size,) + value.shape, value.dtype)
        full = lax.dynamic_update_index_in_dim(full, value, own, 0)
        for k in range(1, size):
            full = lax.dynamic_update_index_in_dim(full, swapped(value, k * at), own ^ k, 0)
        value = full.reshape(size * value.shape[0], value.shape[1])
    at, size = runs[0]
    value = [value] + [swapped(value, k * at) for k in range(1, size)]
    value = between(jnp.concatenate(value, axis=0))
    return value, swapped(value, 1), me // at % size, size


def local(
    atoms, neighbours, live_mask, distances,
    w_iso1, w_anti1, w_sym1, w_rad1, b_rad1, w_rad2, b_rad2, w_rad3, b_rad3,
    w_iso2, w_anti2, w_sym2, out_grad,
):
    rows, _, channels = atoms.shape
    slots = neighbours.shape[1]
    halo = MOL_MOST
    wide = 9 * channels
    ext = rows + 2 * halo
    edges = GROUP * slots
    chunk_count = rows // GROUP
    steps = 4
    chunks = chunk_count // steps
    block_atoms = rows // steps
    block_edges = block_atoms * slots
    vmem = 63 * 1024 * 1024
    me = lax.axis_index(AXES)
    peers = math.prod(lax.axis_size(a) for a in AXES)
    near_pairs = [(i, i ^ 1) for i in range(peers) if i ^ 1 < peers]
    far_pairs = [(i, i + 1 - 2 * (1 - i % 2)) for i in range(1, peers - 1)]

    by_component = jnp.swapaxes(atoms, 0, 1)
    out_grad_by_component = jnp.swapaxes(out_grad, 0, 1)
    near = lax.ppermute(by_component, AXES, near_pairs)
    far = lax.ppermute(by_component, AXES, far_pairs)

    links = neighbours - (me * rows - halo)
    edge_args = [jnp.swapaxes(v, 0, 1) for v in (distances, live_mask, links)]
    edge_specs = [whole(v.shape) for v in edge_args]
    edge_scratch = [pltpu.VMEM((rows, slots), F32)] * 3
    first = jnp.min(jnp.min(links, axis=1).reshape(chunk_count, GROUP), axis=1)
    last = jnp.max(jnp.max(links, axis=1).reshape(chunk_count, GROUP), axis=1)
    count = (last - first) // WINDOW + 1
    windows = jnp.stack([jnp.append(first, me % 2), jnp.append(count, 0)], axis=1)

    biases = jnp.concatenate([b_rad1, b_rad2, b_rad3]).reshape(-1, LANES)
    mid_width, last_width = w_rad2.shape[1], w_rad3.shape[1]
    small = whole((channels, channels))
    components = pl.BlockSpec((9, block_atoms, channels), lambda i: (0, i, 0))
    smem = pl.BlockSpec(memory_space=pltpu.SMEM)
    net_args = (w_rad1, w_rad2, w_rad3, biases)
    net_specs = [whole(v.shape) for v in net_args]
    net_scratch = [
        pltpu.VMEM((LANES, 2 * channels), BF16),
        pltpu.VMEM((2 * channels, mid_width), BF16),
        pltpu.VMEM((mid_width, last_width), BF16), pltpu.VMEM((1, last_width), F32),
    ]
    net0 = pl.pallas_call(
        network_kernel,
        grid=(AHEAD,),
        in_specs=edge_specs[:2] + net_specs,
        out_specs=[
            block((edges, KEPT)), block((edges, last_width)), block((edges // 2, LANES))
        ],
        out_shape=[
            shape_of((AHEAD * edges, KEPT), BF16), shape_of((AHEAD * edges, last_width), F32),
            shape_of((AHEAD * edges // 2, LANES), BF16),
        ],
        scratch_shapes=edge_scratch[:2] + net_scratch,
        compiler_params=pltpu.CompilerParams(vmem_limit_bytes=vmem),
        cost_estimate=pl.CostEstimate(
            flops=2 * block_edges * 135168, bytes_accessed=block_edges * KEPT * 2, transcendentals=0
        ),
        name="network",
    )(*edge_args[:2], *net_args)

    half_rows = max(3 * mid_width + channels + BASES + 16, 7 * channels)
    half_rows = -(-half_rows // 64) * 64
    updated, rim_near, own_grad, rim_far, mine, other = pl.pallas_call(
        main_kernel,
        grid=(steps,),
        in_specs=[
            smem, whole(near.shape), whole(by_component.shape), whole(far.shape),
            components, *edge_specs, *net_specs,
            small, small, small, small, small, small,
            *[pl.BlockSpec(memory_space=pl.ANY)] * 3,
        ],
        out_specs=[
            components, whole((halo, wide)), whole((rows, wide)), whole((halo, wide)),
            whole((half_rows, channels)), whole((half_rows, channels)),
        ],
        out_shape=[
            shape_of((9, rows, channels), BF16),
            shape_of((halo, wide), BF16), shape_of((rows, wide), F32),
            shape_of((halo, wide), BF16),
            shape_of((half_rows, channels), F32), shape_of((half_rows, channels), BF16),
        ],
        scratch_shapes=[
            pltpu.VMEM((ext + WINDOW, wide), BF16),
            pltpu.VMEM((ext, 10 * channels), BF16),
            pltpu.VMEM((block_edges, KEPT), BF16),
            pltpu.VMEM((block_edges, KEPT), BF16),
            pltpu.VMEM((block_edges, last_width), F32),
            pltpu.VMEM((block_edges, last_width), F32),
            pltpu.VMEM((block_edges // 2, LANES), BF16),
            pltpu.VMEM((block_edges // 2, LANES), BF16),
            pltpu.VMEM((block_edges, wide), BF16),
            pltpu.VMEM((block_atoms, wide), F32),
            pltpu.VMEM((2 * block_atoms, wide + 2 * channels), BF16),
            pltpu.VMEM((ext + WINDOW, wide), F32),
            pltpu.VMEM((mid_width + 16, last_width), F32),
            pltpu.VMEM((channels + 16, mid_width), F32),
            pltpu.VMEM((LANES, 2 * channels), F32),
            pltpu.VMEM((3 * channels, channels), F32),
            *net_scratch,
            *edge_scratch,
            pltpu.SemaphoreType.DMA((AHEAD, 3)),
        ],
        compiler_params=pltpu.CompilerParams(vmem_limit_bytes=vmem),
        name="main",
    )(
        windows, near, by_component, far, out_grad_by_component, *edge_args, *net_args,
        w_iso1, w_anti1, w_sym1, w_iso2, w_anti2, w_sym2, *net0,
    )

    kept = {}

    def nothing(value):
        return value

    def send_rims(value):
        to_near, to_far = rim_near, rim_far
        kept["near"] = lax.ppermute(to_near, AXES, near_pairs)
        kept["far"] = lax.ppermute(to_far, AXES, far_pairs)
        return value

    def have_rims(value):
        value, kept["near"], kept["far"] = lax.optimization_barrier(
            (value, kept["near"], kept["far"])
        )
        return value

    def finish(value):
        grad_atoms = pl.pallas_call(
            final_kernel,
            out_shape=shape_of((9, rows, channels), F32),
            compiler_params=pltpu.CompilerParams(vmem_limit_bytes=24 * 1024 * 1024),
            name="final",
        )(
            own_grad, kept["near"], kept["far"], by_component, out_grad_by_component,
            w_iso1, w_anti1, w_sym1,
        )
        value, updated_out, grad_out = lax.optimization_barrier((value, updated, grad_atoms))
        kept["outs"] = jnp.swapaxes(updated_out, 0, 1), jnp.swapaxes(grad_out, 0, 1)
        return value

    send_rims(mine)
    summed, partner, place, shares = reduce_everywhere(mine, other, AXES, (nothing, nothing, nothing, have_rims, finish))
    square_shape = (channels, channels)
    shapes = [square_shape] * 6 + [w_rad1.shape, (channels,), w_rad2.shape, (mid_width,)]
    shapes += [w_rad3.shape, (last_width,)]
    out = pl.pallas_call(
        functools.partial(unpack_kernel, shares),
        in_specs=[smem, whole(summed.shape), whole(partner.shape)],
        out_shape=[shape_of(shape, F32) for shape in shapes],
        compiler_params=pltpu.CompilerParams(vmem_limit_bytes=16 * 1024 * 1024),
        scratch_shapes=[pltpu.VMEM(summed.shape, F32)] * 2,
        name="unpack",
    )(jnp.stack([me % 2, place]), summed, partner)
    return (*kept["outs"], *out[:3], *out[6:], *out[3:6])


def solution(mesh):
    split3 = P(AXES, None, None)
    split2 = P(AXES, None)
    return jax.shard_map(
        local,
        mesh=mesh,
        in_specs=(split3, split2, split2, split2) + (P(),) * 12 + (split3,),
        out_specs=(split3, split3) + (P(),) * 12,
        check_vma=False,
    )
```

```python
import functools
import math

import jax
import jax.numpy as jnp
from jax import lax
from jax.experimental import pallas as pl
from jax.experimental.pallas import tpu as pltpu
from jax.sharding import PartitionSpec as P

MOL_MOST = 256
CUTOFF = 5.0
LANES = 128
GROUP = 8
BASES = 32
UNROLL = 4
PAIRS = ((0, 1), (2, 3), (4, 5), (6, 7), (8,))
GATHERED = 8
GATHER = "kDEAdBaCbc"
SCHEDULE = "".join(n + s for n in "0123" for s in "HaTDb0GJ1cWdp2E3eF4xVyUz")
WINDOW = 256
KIND = (0, 1, 1, 1, 2, 2, 2, 2, 2)
AXES = ("edge", "grp")
F32 = jnp.float32
BF16 = jnp.bfloat16


def col(c):
    return slice(c * LANES, (c + 1) * LANES)


def to_matrix(coords):
    t, a01, a02, a12, s01, s02, s12, s00, s11 = coords
    return [
        [t + s00, s01 + a01, s02 + a02],
        [s01 - a01, t + s11, s12 + a12],
        [s02 - a02, s12 - a12, t - s00 - s11],
    ]


def primal(m):
    t = (m[0][0] + m[1][1] + m[2][2]) * (1.0 / 3.0)
    return [
        t,
        0.5 * (m[0][1] - m[1][0]),
        0.5 * (m[0][2] - m[2][0]),
        0.5 * (m[1][2] - m[2][1]),
        0.5 * (m[0][1] + m[1][0]),
        0.5 * (m[0][2] + m[2][0]),
        0.5 * (m[1][2] + m[2][1]),
        m[0][0] - t,
        m[1][1] - t,
    ]


def dual(m):
    return [
        m[0][0] + m[1][1] + m[2][2],
        m[0][1] - m[1][0],
        m[0][2] - m[2][0],
        m[1][2] - m[2][1],
        m[0][1] + m[1][0],
        m[0][2] + m[2][0],
        m[1][2] + m[2][1],
        m[0][0] - m[2][2],
        m[1][1] - m[2][2],
    ]


def primal_of_dual(d):
    third = 1.0 / 3.0
    return (
        [d[0] * third]
        + [0.5 * v for v in d[1:7]]
        + [(2.0 * d[7] - d[8]) * third, (2.0 * d[8] - d[7]) * third]
    )


def product(a, b):
    return [
        [a[p][0] * b[0][q] + a[p][1] * b[1][q] + a[p][2] * b[2][q] for q in range(3)]
        for p in range(3)
    ]


def add(a, b):
    return [[a[p][q] + b[p][q] for q in range(3)] for p in range(3)]


def both_ways(a, b):
    return add(product(a, b), product(b, a))


def flip(m):
    return [[m[q][p] for q in range(3)] for p in range(3)]


def flat(m):
    return [m[p][q] for p in range(3) for q in range(3)]


def square(parts):
    return [list(parts[0:3]), list(parts[3:6]), list(parts[6:9])]


def total(values):
    out = values[0]
    for v in values[1:]:
        out = out + v
    return out


def dot(a, b):
    return jnp.dot(a, b, preferred_element_type=F32)


def dot_first(a, b):
    return lax.dot_general(a, b, (((0,), (0,)), ((), ())), preferred_element_type=F32)


def dot_last(a, b):
    return lax.dot_general(a, b, (((1,), (1,)), ((), ())), preferred_element_type=F32)


def stack(values):
    return jnp.concatenate([v.astype(BF16) for v in values], axis=0)


def pieces_of(value, rows):
    return [value[n * rows : (n + 1) * rows] for n in range(value.shape[0] // rows)]


def rounded_parts(m):
    coords = primal(m)
    return [v.astype(BF16) for v in coords + [-coords[7] - coords[8]]]


def parts_in(atoms_ref, at):
    values = [atoms_ref[c, at : at + BLOCK, :].astype(F32) for c in range(9)]
    scale = 1.0 / (1.0 + total([v * v for v in values]))
    return rounded_parts(square([v * scale for v in values]))


def mix_parts(parts, weights):
    rows = parts[0].shape[0]
    t, a01, a02, a12, s01, s02, s12, s00, s11, s22 = (
        pieces_of(dot(parts[0], weights[0]), rows)
        + pieces_of(dot(stack(parts[1:4]), weights[1]), rows)
        + pieces_of(dot(stack(parts[4:10]), weights[2]), rows)
    )
    return [
        [t + s00, s01 + a01, s02 + a02],
        [s01 - a01, t + s11, s12 + a12],
        [s02 - a02, s12 - a12, t + s22],
    ]


def seen_by_kind(grad):
    diagonal = [grad[0][0], grad[1][1], grad[2][2]]
    skew = [grad[0][1], grad[1][0], grad[0][2], grad[2][0], grad[1][2], grad[2][1]]
    return [stack(v) for v in (diagonal, skew, skew + diagonal)]


def back_parts(grad, weights):
    rows = grad[0][0].shape[0]
    seen = seen_by_kind(grad)
    iso, anti, sym = (pieces_of(dot_last(v, w), rows) for v, w in zip(seen, weights))
    coords = [
        iso[0] + iso[1] + iso[2],
        anti[0] - anti[1], anti[2] - anti[3], anti[4] - anti[5],
        sym[0] + sym[1], sym[2] + sym[3], sym[4] + sym[5],
        sym[6] - sym[8], sym[7] - sym[8],
    ]
    return seen, coords


def weight_grads(parts, seen):
    p = parts
    lefts = (
        [p[0]] * 3,
        [p[1], -p[1], p[2], -p[2], p[3], -p[3]],
        [p[4], p[4], p[5], p[5], p[6], p[6], p[7], p[8], p[9]],
    )
    return [dot_first(stack(left), right) for left, right in zip(lefts, seen)]


def half_silu(u):
    t = jnp.tanh(u)
    p = 1.0 + t
    act = u * p
    return act, p + act * (1.0 - t)


SLOPE3, ACT2, SLOPE2 = slice(0, 384), slice(384, 640), slice(640, 896)
ACT1, SLOPE1 = slice(896, 1024), slice(1024, 1152)
KEPT = 1152
BLOCK = 32
HALF = 64
AHEAD = 6

ORDER = ((0, 1), (1, 0), (0, 2), (2, 0), (1, 2), (2, 1), (0, 0), (1, 1), (2, 2))


def over_lanes(block, slots, lanes=LANES):
    return jnp.concatenate(
        [jnp.broadcast_to(block[:, s : s + 1], (block.shape[0], lanes)) for s in slots], axis=0
    )


class Network:
    def __init__(self, dist, gate, out, factors, basis, at, refs):
        self.dist, self.gate8 = dist, gate
        self.out, self.factors, self.basis, self.refs = out, factors, basis, refs
        edges = dist.shape[0] * dist.shape[1]
        self.here = pl.ds(pl.multiple_of(at * edges, edges), edges)
        self.half = pl.ds(pl.multiple_of(at * (edges // 2), edges // 2), edges // 2)

    def run(self):
        self.layer1()
        self.active1()
        self.layer2()
        self.active2(0)
        self.active2(1)
        self.layer3()
        for kind in range(3):
            self.active3(kind)

    def layer1(self):
        slots = self.dist.shape[1]
        self.gate = over_lanes(self.gate8, range(slots))
        low = over_lanes(self.dist, range(slots // 2))
        lane = lax.broadcasted_iota(jnp.int32, low.shape, 1)
        dist = jnp.where(lane < HALF, low, over_lanes(self.dist, range(slots // 2, slots)))
        lane = lane % HALF
        off = dist - lane.astype(F32) * (CUTOFF / 31.0)
        basis = jnp.exp(off * off * (-0.5 * (31.0 / CUTOFF) ** 2))
        last = jnp.where(lane == BASES, 1.0, 0.0)
        basis = jnp.where(lane < BASES, basis, last).astype(BF16)
        self.basis[self.half, :] = basis
        inner = dot(basis, self.refs[0][...])
        self.inner = jnp.concatenate([inner[:, :LANES], inner[:, LANES:]], axis=0)

    def active1(self):
        act, slope = half_silu(self.inner)
        self.act = act.astype(BF16)
        self.out[self.here, ACT1] = self.act
        self.out[self.here, SLOPE1] = slope.astype(BF16)

    def layer2(self):
        one = lax.broadcasted_iota(jnp.int32, self.act.shape, 1) == 0
        one = jnp.where(one, 1.0, 0.0).astype(BF16)
        self.inner = dot(jnp.concatenate([self.act, one], axis=1), self.refs[1][...])

    def active2(self, n):
        act, slope = half_silu(self.inner[:, col(n)])
        act = act.astype(BF16)
        self.act = jnp.concatenate([self.act, act], axis=1) if n else act
        self.out[self.here, col(ACT2.start // LANES + n)] = act
        self.out[self.here, col(SLOPE2.start // LANES + n)] = slope.astype(BF16)

    def layer3(self):
        self.inner = dot(self.act, self.refs[2][...])

    def active3(self, kind):
        act, slope = half_silu(self.inner[:, col(kind)] + self.refs[3][:, col(kind)])
        self.factors[self.here, col(kind)] = act * self.gate
        self.out[self.here, col(kind)] = (slope * (0.5 * self.gate)).astype(BF16)


def halve_weights(w1_ref, w2_ref, w3_ref, bias_ref, w1_s, w2_s, w3_s, b3_s):
    half = 0.5 * bias_ref[...].astype(F32)

    def biased(weights, bias, rows):
        below = lax.broadcasted_iota(jnp.int32, (rows - weights.shape[0], bias.shape[1]), 0)
        bias = jnp.where(below == 0, bias, 0.0)
        return jnp.concatenate([0.5 * weights.astype(F32), bias], axis=0).astype(BF16)

    w1_s[...] = jnp.zeros_like(w1_s)
    first = biased(w1_ref[...], half[0:1], HALF)
    w1_s[:HALF, :LANES] = first
    w1_s[HALF:, LANES:] = first
    wide2 = jnp.concatenate([half[1:2], half[2:3]], axis=1)
    w2_s[...] = biased(w2_ref[...], wide2, w2_s.shape[0])
    w3_s[...] = (0.5 * w3_ref[...].astype(F32)).astype(BF16)
    b3_s[...] = jnp.concatenate([half[3:4], half[4:5], half[5:6]], axis=1)


def by_atom(ref):
    return jnp.transpose(ref[...].astype(F32))


def gating(dist, live):
    return 0.5 * (jnp.cos(math.pi * dist / CUTOFF) + 1.0) * live


def network_kernel(
    dist_ref, live_ref, w1_raw, w2_raw, w3_raw, bias_ref, out_ref, fac_ref, basis_ref, dist_s, gate_s, w1_s, w2_s,
    w3_s, b3_s,
):
    net_refs = (w1_s, w2_s, w3_s, b3_s)

    @pl.when(pl.program_id(0) == 0)
    def _():
        halve_weights(w1_raw, w2_raw, w3_raw, bias_ref, *net_refs)
        dist_s[...] = by_atom(dist_ref)
        gate_s[...] = gating(dist_s[...], by_atom(live_ref))

    mine = pl.ds(pl.multiple_of(pl.program_id(0) * GROUP, GROUP), GROUP)
    Network(dist_s[mine, :], gate_s[mine, :], out_ref, fac_ref, basis_ref, 0, net_refs).run()


def window_key(link, first, w):
    start = first + w * WINDOW
    base = pl.multiple_of(first // 16 * 16 + w * WINDOW, 16)
    off = first % 16
    rel = link - start.astype(F32)
    key = rel + off.astype(F32)
    key = jnp.where(key >= WINDOW, key - WINDOW, key)
    key = jnp.where(jnp.logical_and(rel >= 0, rel < WINDOW), key, -1.0)
    return key, base, off


def main_kernel(
    win_ref, near_ref, own_ref, far_ref, outgrad_ref, dist_ref, live_ref, link_ref,
    w1_raw, w2_raw, w3_raw, bias_ref,
    iso1_ref, anti1_ref, sym1_ref, iso2_ref, anti2_ref, sym2_ref, net_first, fac_first, basis_first,
    upd_ref, rim_near_ref, own_out_ref, rim_far_ref, mine_ref, other_ref,
    table, parts_s, net_a, net_b, fac_a, fac_b, basis_a, basis_b, x_s, msg_s, gm_s, spread,
    d3_ref, d2_ref, d1_ref, dw2_ref, w1_ref, w2_ref, w3_ref, b3_ref,
    dist_s, gate_s, link_s, sems,
):
    step = pl.program_id(0)
    steps = pl.num_programs(0)
    edges = GROUP * link_ref.shape[0]
    halo = near_ref.shape[1]
    odd = win_ref[win_ref.shape[0] - 1, 0]
    far_side = halo + own_ref.shape[1]
    near_at = pl.multiple_of((1 - odd) * far_side, 64)
    far_at = pl.multiple_of(odd * far_side, 64)
    atoms = upd_ref.shape[1]
    chunks = atoms // GROUP
    slots = edges // GROUP
    pairs = edges // 16
    wide = 9 * LANES
    radial = (w1_ref, w2_ref, w3_ref, b3_ref)

    def chunk_atoms(index):
        return pl.ds(pl.multiple_of(index * GROUP, GROUP), GROUP)

    def fetch_factors(j):
        here = pl.ds(pl.multiple_of(j * edges, edges), edges)
        return pltpu.make_async_copy(fac_first.at[here], fac_a.at[here], sems.at[j, 0])

    def fetch_rest(j):
        here = pl.ds(pl.multiple_of(j * edges, edges), edges)
        half = pl.ds(pl.multiple_of(j * (edges // 2), edges // 2), edges // 2)
        return (
            pltpu.make_async_copy(net_first.at[here], net_a.at[here], sems.at[j, 1]),
            pltpu.make_async_copy(basis_first.at[half], basis_a.at[half], sems.at[j, 2]),
        )

    @pl.when(step == 0)
    def _():
        for j in range(AHEAD):
            fetch_factors(j).start()
        halve_weights(w1_raw, w2_raw, w3_raw, bias_ref, *radial)
        dist_s[...] = by_atom(dist_ref)
        gate_s[...] = gating(dist_s[...], by_atom(live_ref))
        link_s[...] = by_atom(link_ref)
        weights = (iso1_ref[...], anti1_ref[...], sym1_ref[...])
        for ref, place in ((near_ref, near_at), (own_ref, halo), (far_ref, far_at)):
            for at in range(0, ref.shape[1], BLOCK):
                here = pl.ds(place + at, BLOCK)
                parts = parts_in(ref, at)
                for c, v in enumerate(parts):
                    parts_s[here, col(c)] = v
                mixed = mix_parts(parts, weights)
                for n, (p, q) in enumerate(ORDER):
                    table[here, col(n)] = mixed[p][q].astype(BF16)
        place = far_side + halo
        table[place:, :] = jnp.zeros((table.shape[0] - place, wide), BF16)
        d3_ref[...] = jnp.zeros_like(d3_ref)
        d2_ref[...] = jnp.zeros_like(d2_ref)
        d1_ref[...] = jnp.zeros_like(d1_ref)
        dw2_ref[...] = jnp.zeros_like(dw2_ref)
        spread[...] = jnp.zeros_like(spread)

        @pl.loop(AHEAD, chunks)
        def _(j):
            mine = chunk_atoms(j)
            Network(dist_s[mine, :], gate_s[mine, :], net_a, fac_a, basis_a, j, radial).run()

    @pl.when(step == 0)
    def _():
        for j in range(AHEAD):
            for copy in fetch_rest(j):
                copy.start()

    class Gather:
        def __init__(self, fac, j, w, more):
            self.j, self.w, self.fac, self.more, self.got = j, w, fac, more, {}
            self.here = pl.ds(pl.multiple_of(j * edges, edges), edges)
            self.to = pl.ds(pl.multiple_of(j * GROUP, GROUP), GROUP)

        def hot(self):
            index = step * chunks + self.j
            key, self.base, off = window_key(
                link_s[chunk_atoms(index), :], win_ref[index, 0], self.w
            )
            near = lax.broadcasted_iota(jnp.int32, (edges, WINDOW), 1).astype(F32)
            self.key = (over_lanes(key, range(slots), WINDOW) == near).astype(BF16)
            kept = lax.broadcasted_iota(jnp.int32, (16, LANES), 0) >= off
            self.kept = jnp.where(kept, 1.0, 0.0).astype(BF16)[:, 0:1]

        def rows_of(self, first, past):
            lanes = slice(first * LANES, past * LANES)
            top = table[pl.ds(self.base, 16), lanes] * self.kept
            top += table[pl.ds(self.base + WINDOW, 16), lanes] * (1.0 - self.kept)
            rest = table[pl.ds(self.base + 16, WINDOW - 16), lanes]
            got = dot(self.key, jnp.concatenate([top, rest], axis=0))
            for n in range(past - first):
                self.got[first + n] = got[:, col(n)]

        def use(self, c, x):
            rounded = x.astype(BF16)
            message = self.fac[self.here, col(KIND[c])] * x
            message = jnp.sum(message.reshape(slots, GROUP, LANES), axis=0)
            if self.more:
                rounded += x_s[self.here, col(c)]
                message += msg_s[self.to, col(c)]
            x_s[self.here, col(c)] = rounded
            msg_s[self.to, col(c)] = message

        def pair(self, n):
            one, other = self.got.pop(2 * n), self.got.pop(2 * n + 1)
            self.use(1 + n, one - other)
            self.use(4 + n, one + other)

        def diagonal(self):
            x00, x11, x22 = (self.got.pop(n) for n in (6, 7, 8))
            trace = x00 + x11 + x22
            third = trace * (1.0 / 3.0)
            self.use(0, trace)
            self.use(7, x00 - third)
            self.use(8, x11 - third)

    def gather(fac, places, w, more, order):
        steps_of = {
            "k": lambda g: g.hot(),
            "A": lambda g: g.rows_of(0, 2), "B": lambda g: g.rows_of(2, 4),
            "C": lambda g: g.rows_of(4, 6), "D": lambda g: g.rows_of(6, 8),
            "E": lambda g: g.rows_of(8, 9), "a": lambda g: g.pair(0), "b": lambda g: g.pair(1),
            "c": lambda g: g.pair(2), "d": lambda g: g.diagonal(),
        }
        for each in [Gather(fac, j, w, more) for j in places]:
            for name in order:
                steps_of[name](each)

    even = step % 2 == 0

    def collect(fac):
        @pl.loop(0, chunks // GATHERED)
        def _(turn):
            places = [turn * GATHERED + n for n in range(GATHERED)]
            if fac is fac_a:
                for j in places:

                    @pl.when(jnp.logical_and(step == 0, j < AHEAD))
                    def _():
                        fetch_factors(j).wait()

            gather(fac, places, 0, False, GATHER)

        @pl.loop(0, chunks)
        def _(j):
            @pl.loop(1, win_ref[step * chunks + j, 1])
            def _(w):
                gather(fac, [j], w, True, GATHER)

    @pl.when(even)
    def _():
        collect(fac_a)

    @pl.when(jnp.logical_not(even))
    def _():
        collect(fac_b)

    weights2 = (iso2_ref[...], anti2_ref[...], sym2_ref[...])
    put = pl.ds(pl.multiple_of(halo + step * atoms, 16), atoms)
    mixed = [[None] * 3 for _ in range(3)]
    for n, (p, q) in enumerate(ORDER):
        mixed[p][q] = table[put, col(n)].astype(F32)
    sums = [msg_s[:, col(c)] for c in range(9)]
    messages = to_matrix([sums[0] * (1.0 / 3.0)] + [0.5 * v for v in sums[1:7]] + sums[7:])
    paired = both_ways(mixed, messages)
    inverse = 1.0 / (1.0 + total([v * v for v in flat(paired)]))
    pair_coords = primal(paired)
    mid = [(v * inverse).astype(BF16) for v in pair_coords]
    mid.append(((-pair_coords[7] - pair_coords[8]) * inverse).astype(BF16))
    update = mix_parts(mid, weights2)
    at = pl.ds(pl.multiple_of(step * atoms, 16), atoms)
    values = [own_ref[c, at, :].astype(F32) for c in range(9)]
    inverse_in = 1.0 / (1.0 + total([v * v for v in values]))
    squared = flat(product(update, update))
    for c, (v, u, s) in enumerate(zip(values, flat(update), squared)):
        upd_ref[c] = (v * inverse_in + u + s).astype(BF16)
    out_grad = square([outgrad_ref[c].astype(F32) for c in range(9)])
    grad_update = add(out_grad, both_ways(out_grad, flip(update)))
    seen, mid_dual = back_parts(grad_update, weights2)
    for kind, grad in enumerate(weight_grads(mid, seen)):
        dw2_ref[kind * LANES : (kind + 1) * LANES, :] += grad
    projected = total([a * b for a, b in zip(mid_dual, pair_coords)]) * (2.0 * inverse * inverse)
    grad_paired = to_matrix([v * inverse for v in primal_of_dual(mid_dual)])
    grad_paired = [
        [grad_paired[p][q] - paired[p][q] * projected for q in range(3)] for p in range(3)
    ]
    from_pair = primal(both_ways(grad_paired, flip(messages)))
    for c in range(9):
        spread[put, col(c)] += from_pair[c]
    grad_messages = [
        [v.astype(BF16).astype(F32) for v in row] for row in both_ways(flip(mixed), grad_paired)
    ]
    for c, v in enumerate(primal(grad_messages) + dual(grad_messages)[7:]):
        twice = v.reshape(chunks, 1, GROUP, LANES)
        twice = jnp.concatenate([twice, twice], axis=1).reshape(2 * atoms, LANES)
        gm_s[:, col(c)] = twice.astype(BF16)

    def chunk_places(j):
        here = pl.ds(pl.multiple_of(j * edges, edges), edges)
        two = pl.ds(pl.multiple_of(j * 2 * GROUP, 2 * GROUP), 2 * GROUP)
        return here, two

    def scatter_hot(j, w):
        index = step * chunks + j
        key, base, off = window_key(link_s[chunk_atoms(index), :], win_ref[index, 0], w)
        lane = lax.broadcasted_iota(jnp.int32, (slots, edges), 1)
        own_slot = lax.broadcasted_iota(jnp.int32, (slots, edges), 0) == lane // GROUP
        copies = dot(key.astype(BF16), jnp.where(own_slot, 1.0, 0.0).astype(BF16))
        lane = lax.broadcasted_iota(jnp.int32, (GROUP, edges), 1)
        own_atom = lax.broadcasted_iota(jnp.int32, (GROUP, edges), 0) == lane % GROUP
        key = jnp.sum(jnp.where(own_atom, copies, 0.0), axis=0, keepdims=True)
        near = lax.broadcasted_iota(jnp.int32, (WINDOW, edges), 0).astype(F32)
        kept = lax.broadcasted_iota(jnp.int32, (16, LANES), 0) >= off
        return (key == near).astype(BF16), base, kept

    def scatter(fac, j, hot_base_kept, cs):
        here, two = chunk_places(j)
        hot, base, kept = hot_base_kept
        terms = [
            (fac[here, col(KIND[c])].astype(BF16).reshape(pairs, 16, LANES) * gm_s[two, col(c)]).reshape(
                edges, LANES
            )
            for c in cs
        ]
        sums = dot(hot, jnp.concatenate(terms, axis=1))
        for n, c in enumerate(cs):
            top = sums[:16, col(n)]
            spread[pl.ds(base, 16), col(c)] += jnp.where(kept, top, 0.0)
            spread[pl.ds(base + WINDOW, 16), col(c)] += jnp.where(kept, 0.0, top)
            spread[pl.ds(base + 16, WINDOW - 16), col(c)] += sums[16:, col(n)]

    class Backward:
        def __init__(self, j, now, after):
            self.j, self.now = j, now
            self.net, self.fac, self.basis = now
            self.here, self.two = chunk_places(j)
            self.half = pl.ds(pl.multiple_of(j * (edges // 2), edges // 2), edges // 2)
            self.ahead = None
            if after is not None:
                mine = chunk_atoms((step + 1) * chunks + j)
                self.ahead = Network(dist_s[mine, :], gate_s[mine, :], *after, j, radial)

        def hot(self):
            self.key = scatter_hot(self.j, 0)

        def spread(self, n):
            scatter(self.fac, self.j, self.key, PAIRS[n])

        def terms(self):
            here, two = self.here, self.two
            terms = [
                x_s[here, col(c)].reshape(pairs, 16, LANES) * gm_s[two, col(c if c < 7 else c + 2)]
                for c in range(9)
            ]
            grads = [terms[0], total(terms[1:4]), total(terms[4:9])]
            grad3 = jnp.concatenate([v.reshape(edges, LANES) for v in grads], axis=1)
            self.grad3 = grad3 * self.net[here, SLOPE3]

        def back3(self):
            self.inner2 = dot_last(self.grad3, w3_ref[...])

        def grads2(self, n):
            slope = self.net[self.here, col(SLOPE2.start // LANES + n)].astype(F32)
            grad2 = (self.inner2[:, col(n)] * slope).astype(BF16)
            self.grad2 = jnp.concatenate([self.grad2, grad2], axis=1) if n else grad2

        def back2(self):
            self.inner1 = dot_last(self.grad2, w2_ref[:LANES, :])

        def grads1(self):
            slope = self.net[self.here, SLOPE1].astype(F32)
            grad1 = (self.inner1 * slope).astype(BF16)
            self.grad1 = jnp.concatenate([grad1[: edges // 2], grad1[edges // 2 :]], axis=1)

        def weights3(self):
            ones = jnp.ones((16, edges), BF16)
            act2 = jnp.concatenate([jnp.transpose(self.net[self.here, ACT2]), ones], axis=0)
            d3_ref[...] += dot(act2, self.grad3)

        def weights2(self):
            ones = jnp.ones((16, edges), BF16)
            act1 = jnp.concatenate([jnp.transpose(self.net[self.here, ACT1]), ones], axis=0)
            d2_ref[...] += dot(act1, self.grad2)

        def weights1(self):
            d1_ref[...] += dot(jnp.transpose(self.basis[self.half, :]), self.grad1)

    def sweep(now, after):
        steps_of = {
            "H": lambda b: b.hot(), "T": lambda b: b.terms(),
            "0": lambda b: b.spread(0), "1": lambda b: b.spread(1), "2": lambda b: b.spread(2),
            "3": lambda b: b.spread(3), "4": lambda b: b.spread(4),
            "D": lambda b: b.back3(), "G": lambda b: b.grads2(0), "J": lambda b: b.grads2(1),
            "E": lambda b: b.back2(), "F": lambda b: b.grads1(),
            "W": lambda b: b.weights3(), "V": lambda b: b.weights2(), "U": lambda b: b.weights1(),
            "a": lambda b: b.ahead.layer1(), "b": lambda b: b.ahead.active1(),
            "c": lambda b: b.ahead.layer2(), "d": lambda b: b.ahead.active2(0), "p": lambda b: b.ahead.active2(1),
            "e": lambda b: b.ahead.layer3(), "x": lambda b: b.ahead.active3(0),
            "y": lambda b: b.ahead.active3(1), "z": lambda b: b.ahead.active3(2),
        }

        @pl.loop(0, chunks // UNROLL)
        def _(pair):
            if now[0] is net_a:

                for n in range(UNROLL):

                    @pl.when(jnp.logical_and(step == 0, pair * UNROLL + n < AHEAD))
                    def _():
                        for copy in fetch_rest(pair * UNROLL + n):
                            copy.wait()

            both = [Backward(pair * UNROLL + n, now, after) for n in range(UNROLL)]
            for which, name in zip(SCHEDULE[::2], SCHEDULE[1::2]):
                if after is not None or not name.islower():
                    steps_of[name](both[int(which)])

        @pl.loop(0, chunks)
        def _(j):
            @pl.loop(1, win_ref[step * chunks + j, 1])
            def _(w):
                more = scatter_hot(j, w)
                for cs in PAIRS:
                    scatter(now[1], j, more, cs)

    last = step == steps - 1

    @pl.when(jnp.logical_and(even, jnp.logical_not(last)))
    def _():
        sweep((net_a, fac_a, basis_a), (net_b, fac_b, basis_b))

    @pl.when(jnp.logical_not(jnp.logical_or(even, last)))
    def _():
        sweep((net_b, fac_b, basis_b), (net_a, fac_a, basis_a))

    @pl.when(last)
    def _():
        sweep((net_b, fac_b, basis_b), None)
        grads = [None] * 3
        for out, place in (
            (rim_near_ref, near_at), (own_out_ref, halo), (rim_far_ref, far_at)
        ):
            coords = []
            for c in range(9):
                value = spread[pl.ds(place, out.shape[0]), col(c)]
                out[:, col(c)] = value.astype(out.dtype)
                coords.append(value)
            t, s00, s11 = coords[0], coords[7], coords[8]
            right = [3.0 * t] + [2.0 * v for v in coords[1:7]] + [s00, s11, -s00 - s11]
            left = [parts_s[pl.ds(place, out.shape[0]), col(c)] for c in range(10)]
            fresh = [
                dot_first(stack(left[lo:hi]), stack(right[lo:hi]))
                for lo, hi in ((0, 1), (1, 4), (4, 10))
            ]
            grads = [n if o is None else o + n for o, n in zip(grads, fresh)]
        first = d1_ref[:HALF, :LANES] + d1_ref[HALF:, LANES:]
        deep = d3_ref.shape[0] - 16
        thirds = [d3_ref[:deep, col(n)] for n in range(3)]
        biases = [first[BASES : BASES + 1]]
        biases += [d2_ref[LANES : LANES + 1, col(n)] for n in range(2)]
        biases += [d3_ref[deep : deep + 1, col(n)] for n in range(3)]
        biases.append(jnp.zeros((16 - len(biases), LANES), F32))
        biases = jnp.concatenate(biases, axis=0)
        halves = (
            [*thirds, d2_ref[:LANES, col(0)], first[:BASES], biases],
            [*grads, dw2_ref[...], d2_ref[:LANES, col(1)]],
        )

        def put_half(out, values):
            place = 0
            for value in values:
                out[place : place + value.shape[0], :] = value.astype(out.dtype)
                place += value.shape[0]
            out[place:, :] = jnp.zeros((out.shape[0] - place, LANES), out.dtype)

        for side in range(2):

            @pl.when(odd == side)
            def _():
                put_half(mine_ref, halves[side])
                put_half(other_ref, halves[1 - side])


def unpack_kernel(shares, place_ref, mine_ref, other_ref, *out_refs):
    small, (g_w1, g_b1, g_w2, g_b2, g_w3, g_b3) = out_refs[:6], out_refs[6:12]
    mine_s, other_s = out_refs[12:]
    rows = mine_ref.shape[0] // shares
    for n in range(shares):
        to = pl.ds(pl.multiple_of((place_ref[1] ^ n) * rows, 16), rows)
        mine_s[to, :] = mine_ref[n * rows : (n + 1) * rows, :].astype(F32)
        other_s[to, :] = other_ref[n * rows : (n + 1) * rows, :].astype(F32)

    def unpack(one, two):
        deep = g_w3.shape[0]
        for n in range(3):
            g_w3[:, col(n)] = one[n * deep : (n + 1) * deep, :]
        place = 3 * deep
        g_w2[:, col(0)] = one[place : place + LANES, :]
        place += LANES
        g_w1[...] = one[place : place + BASES, :]
        place += BASES
        biases = one[place : place + 16, :]
        row = 0
        for ref in (g_b1, g_b2, g_b3):
            count = ref.shape[0] // LANES
            for n in range(count):
                ref[col(n)] = biases[row + n]
            row += count
        for n, ref in enumerate(small):
            ref[...] = two[n * LANES : (n + 1) * LANES, :]
        g_w2[:, col(1)] = two[6 * LANES : 7 * LANES, :]

    @pl.when(place_ref[0] == 0)
    def _():
        unpack(mine_s, other_s)

    @pl.when(place_ref[0] == 1)
    def _():
        unpack(other_s, mine_s)


def final_kernel(
    own_ref, near_ref, far_ref, atoms_ref, outgrad_ref, iso1_ref, anti1_ref, sym1_ref, out_ref
):
    weights = (iso1_ref[...], anti1_ref[...], sym1_ref[...])
    grad_mixed = [
        own_ref[:, col(c)] + near_ref[:, col(c)].astype(F32) + far_ref[:, col(c)].astype(F32)
        for c in range(9)
    ]
    back = flat(to_matrix(primal_of_dual(back_parts(to_matrix(grad_mixed), weights)[1])))
    values = [atoms_ref[c].astype(F32) for c in range(9)]
    inverse = 1.0 / (1.0 + total([v * v for v in values]))
    grad = [outgrad_ref[c].astype(F32) + back[c] for c in range(9)]
    along = total([g * v for g, v in zip(grad, values)]) * (2.0 * inverse)
    for c in range(9):
        out_ref[c] = (grad[c] - values[c] * along) * inverse


def whole(shape):
    return pl.BlockSpec(shape, lambda *_: (0,) * len(shape), pipeline_mode=pl.Buffered(1))


def block(shape):
    return pl.BlockSpec(shape, lambda i, *_: (i,) + (0,) * (len(shape) - 1))


def shape_of(shape, kind):
    return jax.ShapeDtypeStruct(shape, kind)


def part(value, index):
    return lax.dynamic_index_in_dim(value, index, 0, keepdims=False)


def reduce_everywhere(mine, other, axes, beside):
    beside = list(beside)

    def between(v):
        return beside.pop(0)(v) if beside else v

    peers = math.prod(lax.axis_size(a) for a in axes)
    me = lax.axis_index(axes)
    runs, at = [], 2
    while at < peers:
        runs.append((at, min(4, peers // at)))
        at *= runs[-1][1]
    runs = runs[1:] + runs[:1]

    def swapped(v, by):
        return lax.ppermute(v, axes, [(i, i ^ by) for i in range(peers)])

    value = between(mine + swapped(other, 1).astype(F32))
    for at, size in runs[:-1]:
        shares = value.reshape(size, value.shape[0] // size, value.shape[1])
        own = me // at % size
        kept = part(shares, own)
        for k in range(1, size):
            kept = kept + swapped(part(shares, own ^ k).astype(BF16), k * at).astype(F32)
        value = between(kept)
    at, size = runs[-1]
    value = value.astype(BF16)
    terms = [value] + [swapped(value, k * at) for k in range(1, size)]
    terms[1] = between(terms[1])
    terms = [v.astype(F32) for v in terms]
    while len(terms) > 1:
        terms = [a + b for a, b in zip(terms[::2], terms[1::2])]
    value = between(terms[0].astype(BF16))
    for at, size in runs[-2:0:-1]:
        own = me // at % size
        full = jnp.zeros((size,) + value.shape, value.dtype)
        full = lax.dynamic_update_index_in_dim(full, value, own, 0)
        for k in range(1, size):
            full = lax.dynamic_update_index_in_dim(full, swapped(value, k * at), own ^ k, 0)
        value = full.reshape(size * value.shape[0], value.shape[1])
    at, size = runs[0]
    value = [value] + [swapped(value, k * at) for k in range(1, size)]
    value = between(jnp.concatenate(value, axis=0))
    return value, swapped(value, 1), me // at % size, size


def local(
    atoms, neighbours, live_mask, distances,
    w_iso1, w_anti1, w_sym1, w_rad1, b_rad1, w_rad2, b_rad2, w_rad3, b_rad3,
    w_iso2, w_anti2, w_sym2, out_grad,
):
    rows, _, channels = atoms.shape
    slots = neighbours.shape[1]
    halo = MOL_MOST
    wide = 9 * channels
    ext = rows + 2 * halo
    edges = GROUP * slots
    chunk_count = rows // GROUP
    steps = 4
    chunks = chunk_count // steps
    block_atoms = rows // steps
    block_edges = block_atoms * slots
    vmem = 63 * 1024 * 1024
    me = lax.axis_index(AXES)
    peers = math.prod(lax.axis_size(a) for a in AXES)
    near_pairs = [(i, i ^ 1) for i in range(peers) if i ^ 1 < peers]
    far_pairs = [(i, i + 1 - 2 * (1 - i % 2)) for i in range(1, peers - 1)]

    by_component = jnp.swapaxes(atoms, 0, 1)
    out_grad_by_component = jnp.swapaxes(out_grad, 0, 1)
    near = lax.ppermute(by_component, AXES, near_pairs)
    far = lax.ppermute(by_component, AXES, far_pairs)

    links = neighbours - (me * rows - halo)
    edge_args = [jnp.swapaxes(v, 0, 1) for v in (distances, live_mask, links)]
    edge_specs = [whole(v.shape) for v in edge_args]
    edge_scratch = [pltpu.VMEM((rows, slots), F32)] * 3
    first = jnp.min(jnp.min(links, axis=1).reshape(chunk_count, GROUP), axis=1)
    last = jnp.max(jnp.max(links, axis=1).reshape(chunk_count, GROUP), axis=1)
    count = (last - first) // WINDOW + 1
    windows = jnp.stack([jnp.append(first, me % 2), jnp.append(count, 0)], axis=1)

    biases = jnp.concatenate([b_rad1, b_rad2, b_rad3]).reshape(-1, LANES)
    mid_width, last_width = w_rad2.shape[1], w_rad3.shape[1]
    small = whole((channels, channels))
    components = pl.BlockSpec((9, block_atoms, channels), lambda i: (0, i, 0))
    smem = pl.BlockSpec(memory_space=pltpu.SMEM)
    net_args = (w_rad1, w_rad2, w_rad3, biases)
    net_specs = [whole(v.shape) for v in net_args]
    net_scratch = [
        pltpu.VMEM((LANES, 2 * channels), BF16),
        pltpu.VMEM((2 * channels, mid_width), BF16),
        pltpu.VMEM((mid_width, last_width), BF16), pltpu.VMEM((1, last_width), F32),
    ]
    net0 = pl.pallas_call(
        network_kernel,
        grid=(AHEAD,),
        in_specs=edge_specs[:2] + net_specs,
        out_specs=[
            block((edges, KEPT)), block((edges, last_width)), block((edges // 2, LANES))
        ],
        out_shape=[
            shape_of((AHEAD * edges, KEPT), BF16), shape_of((AHEAD * edges, last_width), F32),
            shape_of((AHEAD * edges // 2, LANES), BF16),
        ],
        scratch_shapes=edge_scratch[:2] + net_scratch,
        compiler_params=pltpu.CompilerParams(vmem_limit_bytes=vmem),
        cost_estimate=pl.CostEstimate(
            flops=2 * block_edges * 135168, bytes_accessed=block_edges * KEPT * 2, transcendentals=0
        ),
        name="network",
    )(*edge_args[:2], *net_args)

    half_rows = max(3 * mid_width + channels + BASES + 16, 7 * channels)
    half_rows = -(-half_rows // 64) * 64
    updated, rim_near, own_grad, rim_far, mine, other = pl.pallas_call(
        main_kernel,
        grid=(steps,),
        in_specs=[
            smem, whole(near.shape), whole(by_component.shape), whole(far.shape),
            components, *edge_specs, *net_specs,
            small, small, small, small, small, small,
            *[pl.BlockSpec(memory_space=pl.ANY)] * 3,
        ],
        out_specs=[
            components, whole((halo, wide)), whole((rows, wide)), whole((halo, wide)),
            whole((half_rows, channels)), whole((half_rows, channels)),
        ],
        out_shape=[
            shape_of((9, rows, channels), BF16),
            shape_of((halo, wide), BF16), shape_of((rows, wide), F32),
            shape_of((halo, wide), BF16),
            shape_of((half_rows, channels), F32), shape_of((half_rows, channels), BF16),
        ],
        scratch_shapes=[
            pltpu.VMEM((ext + WINDOW, wide), BF16),
            pltpu.VMEM((ext, 10 * channels), BF16),
            pltpu.VMEM((block_edges, KEPT), BF16),
            pltpu.VMEM((block_edges, KEPT), BF16),
            pltpu.VMEM((block_edges, last_width), F32),
            pltpu.VMEM((block_edges, last_width), F32),
            pltpu.VMEM((block_edges // 2, LANES), BF16),
            pltpu.VMEM((block_edges // 2, LANES), BF16),
            pltpu.VMEM((block_edges, wide), BF16),
            pltpu.VMEM((block_atoms, wide), F32),
            pltpu.VMEM((2 * block_atoms, wide + 2 * channels), BF16),
            pltpu.VMEM((ext + WINDOW, wide), F32),
            pltpu.VMEM((mid_width + 16, last_width), F32),
            pltpu.VMEM((channels + 16, mid_width), F32),
            pltpu.VMEM((LANES, 2 * channels), F32),
            pltpu.VMEM((3 * channels, channels), F32),
            *net_scratch,
            *edge_scratch,
            pltpu.SemaphoreType.DMA((AHEAD, 3)),
        ],
        compiler_params=pltpu.CompilerParams(vmem_limit_bytes=vmem),
        name="main",
    )(
        windows, near, by_component, far, out_grad_by_component, *edge_args, *net_args,
        w_iso1, w_anti1, w_sym1, w_iso2, w_anti2, w_sym2, *net0,
    )

    kept = {}

    def nothing(value):
        return value

    def send_rims(value):
        to_near, to_far = rim_near, rim_far
        kept["near"] = lax.ppermute(to_near, AXES, near_pairs)
        kept["far"] = lax.ppermute(to_far, AXES, far_pairs)
        return value

    def have_rims(value):
        value, kept["near"], kept["far"] = lax.optimization_barrier(
            (value, kept["near"], kept["far"])
        )
        return value

    def finish(value):
        grad_atoms = pl.pallas_call(
            final_kernel,
            out_shape=shape_of((9, rows, channels), F32),
            compiler_params=pltpu.CompilerParams(vmem_limit_bytes=24 * 1024 * 1024),
            name="final",
        )(
            own_grad, kept["near"], kept["far"], by_component, out_grad_by_component,
            w_iso1, w_anti1, w_sym1,
        )
        value, updated_out, grad_out = lax.optimization_barrier((value, updated, grad_atoms))
        kept["outs"] = jnp.swapaxes(updated_out, 0, 1), jnp.swapaxes(grad_out, 0, 1)
        return value

    send_rims(mine)
    summed, partner, place, shares = reduce_everywhere(mine, other, AXES, (nothing, nothing, nothing, have_rims, finish))
    square_shape = (channels, channels)
    shapes = [square_shape] * 6 + [w_rad1.shape, (channels,), w_rad2.shape, (mid_width,)]
    shapes += [w_rad3.shape, (last_width,)]
    out = pl.pallas_call(
        functools.partial(unpack_kernel, shares),
        in_specs=[smem, whole(summed.shape), whole(partner.shape)],
        out_shape=[shape_of(shape, F32) for shape in shapes],
        compiler_params=pltpu.CompilerParams(vmem_limit_bytes=16 * 1024 * 1024),
        scratch_shapes=[pltpu.VMEM(summed.shape, F32)] * 2,
        name="unpack",
    )(jnp.stack([me % 2, place]), summed, partner)
    return (*kept["outs"], *out[:3], *out[6:], *out[3:6])


def solution(mesh):
    split3 = P(AXES, None, None)
    split2 = P(AXES, None)
    return jax.shard_map(
        local,
        mesh=mesh,
        in_specs=(split3, split2, split2, split2) + (P(),) * 12 + (split3,),
        out_specs=(split3, split3) + (P(),) * 12,
        check_vma=False,
    )
```

```python
import functools
import math

import jax
import jax.numpy as jnp
from jax import lax
from jax.experimental import pallas as pl
from jax.experimental.pallas import tpu as pltpu
from jax.sharding import PartitionSpec as P

MOL_MOST = 256
CUTOFF = 5.0
LANES = 128
GROUP = 8
BASES = 32
UNROLL = 4
PAIRS = ((0, 1), (2, 3), (4, 5), (6, 7), (8,))
GATHERED = 8
GATHER = "kDEAdBaCbc"
SCHEDULE = "".join(n + s for n in "0123" for s in "HaTDb0GJ1cWdp2E3eF4xVyUz")
WINDOW = 256
KIND = (0, 1, 1, 1, 2, 2, 2, 2, 2)
AXES = ("edge", "grp")
F32 = jnp.float32
BF16 = jnp.bfloat16


def col(c):
    return slice(c * LANES, (c + 1) * LANES)


def to_matrix(coords):
    t, a01, a02, a12, s01, s02, s12, s00, s11 = coords
    return [
        [t + s00, s01 + a01, s02 + a02],
        [s01 - a01, t + s11, s12 + a12],
        [s02 - a02, s12 - a12, t - s00 - s11],
    ]


def primal(m):
    t = (m[0][0] + m[1][1] + m[2][2]) * (1.0 / 3.0)
    return [
        t,
        0.5 * (m[0][1] - m[1][0]),
        0.5 * (m[0][2] - m[2][0]),
        0.5 * (m[1][2] - m[2][1]),
        0.5 * (m[0][1] + m[1][0]),
        0.5 * (m[0][2] + m[2][0]),
        0.5 * (m[1][2] + m[2][1]),
        m[0][0] - t,
        m[1][1] - t,
    ]


def dual(m):
    return [
        m[0][0] + m[1][1] + m[2][2],
        m[0][1] - m[1][0],
        m[0][2] - m[2][0],
        m[1][2] - m[2][1],
        m[0][1] + m[1][0],
        m[0][2] + m[2][0],
        m[1][2] + m[2][1],
        m[0][0] - m[2][2],
        m[1][1] - m[2][2],
    ]


def primal_of_dual(d):
    third = 1.0 / 3.0
    return (
        [d[0] * third]
        + [0.5 * v for v in d[1:7]]
        + [(2.0 * d[7] - d[8]) * third, (2.0 * d[8] - d[7]) * third]
    )


def product(a, b):
    return [
        [a[p][0] * b[0][q] + a[p][1] * b[1][q] + a[p][2] * b[2][q] for q in range(3)]
        for p in range(3)
    ]


def add(a, b):
    return [[a[p][q] + b[p][q] for q in range(3)] for p in range(3)]


def both_ways(a, b):
    return add(product(a, b), product(b, a))


def flip(m):
    return [[m[q][p] for q in range(3)] for p in range(3)]


def flat(m):
    return [m[p][q] for p in range(3) for q in range(3)]


def square(parts):
    return [list(parts[0:3]), list(parts[3:6]), list(parts[6:9])]


def total(values):
    out = values[0]
    for v in values[1:]:
        out = out + v
    return out


def dot(a, b):
    return jnp.dot(a, b, preferred_element_type=F32)


def dot_first(a, b):
    return lax.dot_general(a, b, (((0,), (0,)), ((), ())), preferred_element_type=F32)


def dot_last(a, b):
    return lax.dot_general(a, b, (((1,), (1,)), ((), ())), preferred_element_type=F32)


def stack(values):
    return jnp.concatenate([v.astype(BF16) for v in values], axis=0)


def pieces_of(value, rows):
    return [value[n * rows : (n + 1) * rows] for n in range(value.shape[0] // rows)]


def rounded_parts(m):
    coords = primal(m)
    return [v.astype(BF16) for v in coords + [-coords[7] - coords[8]]]


def parts_in(atoms_ref, at):
    values = [atoms_ref[c, at : at + BLOCK, :].astype(F32) for c in range(9)]
    scale = 1.0 / (1.0 + total([v * v for v in values]))
    return rounded_parts(square([v * scale for v in values]))


def mix_parts(parts, weights):
    rows = parts[0].shape[0]
    t, a01, a02, a12, s01, s02, s12, s00, s11, s22 = (
        pieces_of(dot(parts[0], weights[0]), rows)
        + pieces_of(dot(stack(parts[1:4]), weights[1]), rows)
        + pieces_of(dot(stack(parts[4:10]), weights[2]), rows)
    )
    return [
        [t + s00, s01 + a01, s02 + a02],
        [s01 - a01, t + s11, s12 + a12],
        [s02 - a02, s12 - a12, t + s22],
    ]


def seen_by_kind(grad):
    diagonal = [grad[0][0], grad[1][1], grad[2][2]]
    skew = [grad[0][1], grad[1][0], grad[0][2], grad[2][0], grad[1][2], grad[2][1]]
    return [stack(v) for v in (diagonal, skew, skew + diagonal)]


def back_parts(grad, weights):
    rows = grad[0][0].shape[0]
    seen = seen_by_kind(grad)
    iso, anti, sym = (pieces_of(dot_last(v, w), rows) for v, w in zip(seen, weights))
    coords = [
        iso[0] + iso[1] + iso[2],
        anti[0] - anti[1], anti[2] - anti[3], anti[4] - anti[5],
        sym[0] + sym[1], sym[2] + sym[3], sym[4] + sym[5],
        sym[6] - sym[8], sym[7] - sym[8],
    ]
    return seen, coords


def weight_grads(parts, seen):
    p = parts
    lefts = (
        [p[0]] * 3,
        [p[1], -p[1], p[2], -p[2], p[3], -p[3]],
        [p[4], p[4], p[5], p[5], p[6], p[6], p[7], p[8], p[9]],
    )
    return [dot_first(stack(left), right) for left, right in zip(lefts, seen)]


def half_silu(u):
    t = jnp.tanh(u)
    p = 1.0 + t
    act = u * p
    return act, p + act * (1.0 - t)


SLOPE3, ACT2, SLOPE2 = slice(0, 384), slice(384, 640), slice(640, 896)
ACT1, SLOPE1 = slice(896, 1024), slice(1024, 1152)
KEPT = 1152
BLOCK = 32
HALF = 64
AHEAD = 6

ORDER = ((0, 1), (1, 0), (0, 2), (2, 0), (1, 2), (2, 1), (0, 0), (1, 1), (2, 2))


def over_lanes(block, slots, lanes=LANES):
    return jnp.concatenate(
        [jnp.broadcast_to(block[:, s : s + 1], (block.shape[0], lanes)) for s in slots], axis=0
    )


class Network:
    def __init__(self, dist, gate, out, factors, basis, at, refs):
        self.dist, self.gate8 = dist, gate
        self.out, self.factors, self.basis, self.refs = out, factors, basis, refs
        edges = dist.shape[0] * dist.shape[1]
        self.here = pl.ds(pl.multiple_of(at * edges, edges), edges)
        self.half = pl.ds(pl.multiple_of(at * (edges // 2), edges // 2), edges // 2)

    def run(self):
        self.layer1()
        self.active1()
        self.layer2()
        self.active2(0)
        self.active2(1)
        self.layer3()
        for kind in range(3):
            self.active3(kind)

    def layer1(self):
        slots = self.dist.shape[1]
        self.gate = over_lanes(self.gate8, range(slots))
        low = over_lanes(self.dist, range(slots // 2))
        lane = lax.broadcasted_iota(jnp.int32, low.shape, 1)
        dist = jnp.where(lane < HALF, low, over_lanes(self.dist, range(slots // 2, slots)))
        lane = lane % HALF
        off = dist - lane.astype(F32) * (CUTOFF / 31.0)
        basis = jnp.exp(off * off * (-0.5 * (31.0 / CUTOFF) ** 2))
        last = jnp.where(lane == BASES, 1.0, 0.0)
        basis = jnp.where(lane < BASES, basis, last).astype(BF16)
        self.basis[self.half, :] = basis
        inner = dot(basis, self.refs[0][...])
        self.inner = jnp.concatenate([inner[:, :LANES], inner[:, LANES:]], axis=0)

    def active1(self):
        act, slope = half_silu(self.inner)
        self.act = act.astype(BF16)
        self.out[self.here, ACT1] = self.act
        self.out[self.here, SLOPE1] = slope.astype(BF16)

    def layer2(self):
        one = lax.broadcasted_iota(jnp.int32, self.act.shape, 1) == 0
        one = jnp.where(one, 1.0, 0.0).astype(BF16)
        self.inner = dot(jnp.concatenate([self.act, one], axis=1), self.refs[1][...])

    def active2(self, n):
        act, slope = half_silu(self.inner[:, col(n)])
        act = act.astype(BF16)
        self.act = jnp.concatenate([self.act, act], axis=1) if n else act
        self.out[self.here, col(ACT2.start // LANES + n)] = act
        self.out[self.here, col(SLOPE2.start // LANES + n)] = slope.astype(BF16)

    def layer3(self):
        self.inner = dot(self.act, self.refs[2][...])

    def active3(self, kind):
        act, slope = half_silu(self.inner[:, col(kind)] + self.refs[3][:, col(kind)])
        self.factors[self.here, col(kind)] = act * self.gate
        self.out[self.here, col(kind)] = (slope * (0.5 * self.gate)).astype(BF16)


def halve_weights(w1_ref, w2_ref, w3_ref, b1_ref, b2_ref, b3_ref, w1_s, w2_s, w3_s, b3_s):
    half = [0.5 * ref[...].astype(F32).reshape(1, -1) for ref in (b1_ref, b2_ref, b3_ref)]

    def biased(weights, bias, rows):
        below = lax.broadcasted_iota(jnp.int32, (rows - weights.shape[0], bias.shape[1]), 0)
        bias = jnp.where(below == 0, bias, 0.0)
        return jnp.concatenate([0.5 * weights.astype(F32), bias], axis=0).astype(BF16)

    w1_s[...] = jnp.zeros_like(w1_s)
    first = biased(w1_ref[...], half[0], HALF)
    w1_s[:HALF, :LANES] = first
    w1_s[HALF:, LANES:] = first
    w2_s[...] = biased(w2_ref[...], half[1], w2_s.shape[0])
    w3_s[...] = (0.5 * w3_ref[...].astype(F32)).astype(BF16)
    b3_s[...] = half[2]


def by_atom(ref):
    return jnp.transpose(ref[...].astype(F32))


def gating(dist, live):
    return 0.5 * (jnp.cos(math.pi * dist / CUTOFF) + 1.0) * live


def network_kernel(
    dist_ref, live_ref, w1_raw, w2_raw, w3_raw, b1_raw, b2_raw, b3_raw, out_ref, fac_ref, basis_ref, dist_s, gate_s, w1_s, w2_s,
    w3_s, b3_s,
):
    net_refs = (w1_s, w2_s, w3_s, b3_s)

    @pl.when(pl.program_id(0) == 0)
    def _():
        halve_weights(w1_raw, w2_raw, w3_raw, b1_raw, b2_raw, b3_raw, *net_refs)
        dist_s[...] = by_atom(dist_ref)
        gate_s[...] = gating(dist_s[...], by_atom(live_ref))

    mine = pl.ds(pl.multiple_of(pl.program_id(0) * GROUP, GROUP), GROUP)
    Network(dist_s[mine, :], gate_s[mine, :], out_ref, fac_ref, basis_ref, 0, net_refs).run()


def window_key(link, first, w):
    start = first + w * WINDOW
    base = pl.multiple_of(first // 16 * 16 + w * WINDOW, 16)
    off = first % 16
    rel = link - start.astype(F32)
    key = rel + off.astype(F32)
    key = jnp.where(key >= WINDOW, key - WINDOW, key)
    key = jnp.where(jnp.logical_and(rel >= 0, rel < WINDOW), key, -1.0)
    return key, base, off


def main_kernel(
    win_ref, near_ref, own_ref, far_ref, outgrad_ref, dist_ref, live_ref, link_ref,
    w1_raw, w2_raw, w3_raw, b1_raw, b2_raw, b3_raw,
    iso1_ref, anti1_ref, sym1_ref, iso2_ref, anti2_ref, sym2_ref, net_first, fac_first, basis_first,
    upd_ref, rim_near_ref, own_out_ref, rim_far_ref, mine_ref, other_ref,
    table, parts_s, net_a, net_b, fac_a, fac_b, basis_a, basis_b, x_s, msg_s, gm_s, spread,
    d3_ref, d2_ref, d1_ref, dw2_ref, w1_ref, w2_ref, w3_ref, b3_ref,
    dist_s, gate_s, link_s, sems,
):
    step = pl.program_id(0)
    steps = pl.num_programs(0)
    edges = GROUP * link_ref.shape[0]
    halo = near_ref.shape[1]
    odd = win_ref[win_ref.shape[0] - 1, 0]
    far_side = halo + own_ref.shape[1]
    near_at = pl.multiple_of((1 - odd) * far_side, 64)
    far_at = pl.multiple_of(odd * far_side, 64)
    atoms = upd_ref.shape[1]
    chunks = atoms // GROUP
    slots = edges // GROUP
    pairs = edges // 16
    wide = 9 * LANES
    radial = (w1_ref, w2_ref, w3_ref, b3_ref)

    def chunk_atoms(index):
        return pl.ds(pl.multiple_of(index * GROUP, GROUP), GROUP)

    def fetch_factors(j):
        here = pl.ds(pl.multiple_of(j * edges, edges), edges)
        return pltpu.make_async_copy(fac_first.at[here], fac_a.at[here], sems.at[j, 0])

    def fetch_rest(j):
        here = pl.ds(pl.multiple_of(j * edges, edges), edges)
        half = pl.ds(pl.multiple_of(j * (edges // 2), edges // 2), edges // 2)
        return (
            pltpu.make_async_copy(net_first.at[here], net_a.at[here], sems.at[j, 1]),
            pltpu.make_async_copy(basis_first.at[half], basis_a.at[half], sems.at[j, 2]),
        )

    @pl.when(step == 0)
    def _():
        for j in range(AHEAD):
            fetch_factors(j).start()
        halve_weights(w1_raw, w2_raw, w3_raw, b1_raw, b2_raw, b3_raw, *radial)
        dist_s[...] = by_atom(dist_ref)
        gate_s[...] = gating(dist_s[...], by_atom(live_ref))
        link_s[...] = by_atom(link_ref)
        weights = (iso1_ref[...], anti1_ref[...], sym1_ref[...])
        for ref, place in ((near_ref, near_at), (own_ref, halo), (far_ref, far_at)):
            for at in range(0, ref.shape[1], BLOCK):
                here = pl.ds(place + at, BLOCK)
                parts = parts_in(ref, at)
                for c, v in enumerate(parts):
                    parts_s[here, col(c)] = v
                mixed = mix_parts(parts, weights)
                for n, (p, q) in enumerate(ORDER):
                    table[here, col(n)] = mixed[p][q].astype(BF16)
        place = far_side + halo
        table[place:, :] = jnp.zeros((table.shape[0] - place, wide), BF16)
        d3_ref[...] = jnp.zeros_like(d3_ref)
        d2_ref[...] = jnp.zeros_like(d2_ref)
        d1_ref[...] = jnp.zeros_like(d1_ref)
        dw2_ref[...] = jnp.zeros_like(dw2_ref)
        spread[...] = jnp.zeros_like(spread)

        @pl.loop(AHEAD, chunks, unroll=2)
        def _(j):
            mine = chunk_atoms(j)
            Network(dist_s[mine, :], gate_s[mine, :], net_a, fac_a, basis_a, j, radial).run()

    @pl.when(step == 0)
    def _():
        for j in range(AHEAD):
            for copy in fetch_rest(j):
                copy.start()

    class Gather:
        def __init__(self, fac, j, w, more):
            self.j, self.w, self.fac, self.more, self.got = j, w, fac, more, {}
            self.here = pl.ds(pl.multiple_of(j * edges, edges), edges)
            self.to = pl.ds(pl.multiple_of(j * GROUP, GROUP), GROUP)

        def hot(self):
            index = step * chunks + self.j
            key, self.base, off = window_key(
                link_s[chunk_atoms(index), :], win_ref[index, 0], self.w
            )
            near = lax.broadcasted_iota(jnp.int32, (edges, WINDOW), 1).astype(F32)
            self.key = (over_lanes(key, range(slots), WINDOW) == near).astype(BF16)
            kept = lax.broadcasted_iota(jnp.int32, (16, LANES), 0) >= off
            self.kept = jnp.where(kept, 1.0, 0.0).astype(BF16)[:, 0:1]

        def rows_of(self, first, past):
            lanes = slice(first * LANES, past * LANES)
            top = table[pl.ds(self.base, 16), lanes] * self.kept
            top += table[pl.ds(self.base + WINDOW, 16), lanes] * (1.0 - self.kept)
            rest = table[pl.ds(self.base + 16, WINDOW - 16), lanes]
            got = dot(self.key, jnp.concatenate([top, rest], axis=0))
            for n in range(past - first):
                self.got[first + n] = got[:, col(n)]

        def use(self, c, x):
            rounded = x.astype(BF16)
            message = self.fac[self.here, col(KIND[c])] * x
            message = jnp.sum(message.reshape(slots, GROUP, LANES), axis=0)
            if self.more:
                rounded += x_s[self.here, col(c)]
                message += msg_s[self.to, col(c)]
            x_s[self.here, col(c)] = rounded
            msg_s[self.to, col(c)] = message

        def pair(self, n):
            one, other = self.got.pop(2 * n), self.got.pop(2 * n + 1)
            self.use(1 + n, one - other)
            self.use(4 + n, one + other)

        def diagonal(self):
            x00, x11, x22 = (self.got.pop(n) for n in (6, 7, 8))
            trace = x00 + x11 + x22
            third = trace * (1.0 / 3.0)
            self.use(0, trace)
            self.use(7, x00 - third)
            self.use(8, x11 - third)

    def gather(fac, places, w, more, order):
        steps_of = {
            "k": lambda g: g.hot(),
            "A": lambda g: g.rows_of(0, 2), "B": lambda g: g.rows_of(2, 4),
            "C": lambda g: g.rows_of(4, 6), "D": lambda g: g.rows_of(6, 8),
            "E": lambda g: g.rows_of(8, 9), "a": lambda g: g.pair(0), "b": lambda g: g.pair(1),
            "c": lambda g: g.pair(2), "d": lambda g: g.diagonal(),
        }
        for each in [Gather(fac, j, w, more) for j in places]:
            for name in order:
                steps_of[name](each)

    even = step % 2 == 0

    def collect(fac):
        @pl.loop(0, chunks // GATHERED)
        def _(turn):
            places = [turn * GATHERED + n for n in range(GATHERED)]
            if fac is fac_a:
                for j in places:

                    @pl.when(jnp.logical_and(step == 0, j < AHEAD))
                    def _():
                        fetch_factors(j).wait()

            gather(fac, places, 0, False, GATHER)

        @pl.loop(0, chunks)
        def _(j):
            @pl.loop(1, win_ref[step * chunks + j, 1])
            def _(w):
                gather(fac, [j], w, True, GATHER)

    @pl.when(even)
    def _():
        collect(fac_a)

    @pl.when(jnp.logical_not(even))
    def _():
        collect(fac_b)

    weights2 = (iso2_ref[...], anti2_ref[...], sym2_ref[...])
    put = pl.ds(pl.multiple_of(halo + step * atoms, 16), atoms)
    mixed = [[None] * 3 for _ in range(3)]
    for n, (p, q) in enumerate(ORDER):
        mixed[p][q] = table[put, col(n)].astype(F32)
    sums = [msg_s[:, col(c)] for c in range(9)]
    messages = to_matrix([sums[0] * (1.0 / 3.0)] + [0.5 * v for v in sums[1:7]] + sums[7:])
    paired = both_ways(mixed, messages)
    inverse = 1.0 / (1.0 + total([v * v for v in flat(paired)]))
    pair_coords = primal(paired)
    mid = [(v * inverse).astype(BF16) for v in pair_coords]
    mid.append(((-pair_coords[7] - pair_coords[8]) * inverse).astype(BF16))
    update = mix_parts(mid, weights2)
    at = pl.ds(pl.multiple_of(step * atoms, 16), atoms)
    values = [own_ref[c, at, :].astype(F32) for c in range(9)]
    inverse_in = 1.0 / (1.0 + total([v * v for v in values]))
    squared = flat(product(update, update))
    for c, (v, u, s) in enumerate(zip(values, flat(update), squared)):
        upd_ref[c] = (v * inverse_in + u + s).astype(BF16)
    out_grad = square([outgrad_ref[c].astype(F32) for c in range(9)])
    grad_update = add(out_grad, both_ways(out_grad, flip(update)))
    seen, mid_dual = back_parts(grad_update, weights2)
    for kind, grad in enumerate(weight_grads(mid, seen)):
        dw2_ref[kind * LANES : (kind + 1) * LANES, :] += grad
    projected = total([a * b for a, b in zip(mid_dual, pair_coords)]) * (2.0 * inverse * inverse)
    grad_paired = to_matrix([v * inverse for v in primal_of_dual(mid_dual)])
    grad_paired = [
        [grad_paired[p][q] - paired[p][q] * projected for q in range(3)] for p in range(3)
    ]
    from_pair = primal(both_ways(grad_paired, flip(messages)))
    for c in range(9):
        spread[put, col(c)] += from_pair[c]
    grad_messages = [
        [v.astype(BF16).astype(F32) for v in row] for row in both_ways(flip(mixed), grad_paired)
    ]
    for c, v in enumerate(primal(grad_messages) + dual(grad_messages)[7:]):
        twice = v.reshape(chunks, 1, GROUP, LANES)
        twice = jnp.concatenate([twice, twice], axis=1).reshape(2 * atoms, LANES)
        gm_s[:, col(c)] = twice.astype(BF16)

    def chunk_places(j):
        here = pl.ds(pl.multiple_of(j * edges, edges), edges)
        two = pl.ds(pl.multiple_of(j * 2 * GROUP, 2 * GROUP), 2 * GROUP)
        return here, two

    def scatter_hot(j, w):
        index = step * chunks + j
        key, base, off = window_key(link_s[chunk_atoms(index), :], win_ref[index, 0], w)
        lane = lax.broadcasted_iota(jnp.int32, (slots, edges), 1)
        own_slot = lax.broadcasted_iota(jnp.int32, (slots, edges), 0) == lane // GROUP
        copies = dot(key.astype(BF16), jnp.where(own_slot, 1.0, 0.0).astype(BF16))
        lane = lax.broadcasted_iota(jnp.int32, (GROUP, edges), 1)
        own_atom = lax.broadcasted_iota(jnp.int32, (GROUP, edges), 0) == lane % GROUP
        key = jnp.sum(jnp.where(own_atom, copies, 0.0), axis=0, keepdims=True)
        near = lax.broadcasted_iota(jnp.int32, (WINDOW, edges), 0).astype(F32)
        kept = lax.broadcasted_iota(jnp.int32, (16, LANES), 0) >= off
        return (key == near).astype(BF16), base, kept

    def scatter(fac, j, hot_base_kept, cs):
        here, two = chunk_places(j)
        hot, base, kept = hot_base_kept
        terms = [
            (fac[here, col(KIND[c])].astype(BF16).reshape(pairs, 16, LANES) * gm_s[two, col(c)]).reshape(
                edges, LANES
            )
            for c in cs
        ]
        sums = dot(hot, jnp.concatenate(terms, axis=1))
        for n, c in enumerate(cs):
            top = sums[:16, col(n)]
            spread[pl.ds(base, 16), col(c)] += jnp.where(kept, top, 0.0)
            spread[pl.ds(base + WINDOW, 16), col(c)] += jnp.where(kept, 0.0, top)
            spread[pl.ds(base + 16, WINDOW - 16), col(c)] += sums[16:, col(n)]

    class Backward:
        def __init__(self, j, now, after):
            self.j, self.now = j, now
            self.net, self.fac, self.basis = now
            self.here, self.two = chunk_places(j)
            self.half = pl.ds(pl.multiple_of(j * (edges // 2), edges // 2), edges // 2)
            self.ahead = None
            if after is not None:
                mine = chunk_atoms((step + 1) * chunks + j)
                self.ahead = Network(dist_s[mine, :], gate_s[mine, :], *after, j, radial)

        def hot(self):
            self.key = scatter_hot(self.j, 0)

        def spread(self, n):
            scatter(self.fac, self.j, self.key, PAIRS[n])

        def terms(self):
            here, two = self.here, self.two
            terms = [
                x_s[here, col(c)].reshape(pairs, 16, LANES) * gm_s[two, col(c if c < 7 else c + 2)]
                for c in range(9)
            ]
            grads = [terms[0], total(terms[1:4]), total(terms[4:9])]
            grad3 = jnp.concatenate([v.reshape(edges, LANES) for v in grads], axis=1)
            self.grad3 = grad3 * self.net[here, SLOPE3]

        def back3(self):
            self.inner2 = dot_last(self.grad3, w3_ref[...])

        def grads2(self, n):
            slope = self.net[self.here, col(SLOPE2.start // LANES + n)].astype(F32)
            grad2 = (self.inner2[:, col(n)] * slope).astype(BF16)
            self.grad2 = jnp.concatenate([self.grad2, grad2], axis=1) if n else grad2

        def back2(self):
            self.inner1 = dot_last(self.grad2, w2_ref[:LANES, :])

        def grads1(self):
            slope = self.net[self.here, SLOPE1].astype(F32)
            grad1 = (self.inner1 * slope).astype(BF16)
            self.grad1 = jnp.concatenate([grad1[: edges // 2], grad1[edges // 2 :]], axis=1)

        def weights3(self):
            ones = jnp.ones((16, edges), BF16)
            act2 = jnp.concatenate([jnp.transpose(self.net[self.here, ACT2]), ones], axis=0)
            d3_ref[...] += dot(act2, self.grad3)

        def weights2(self):
            ones = jnp.ones((16, edges), BF16)
            act1 = jnp.concatenate([jnp.transpose(self.net[self.here, ACT1]), ones], axis=0)
            d2_ref[...] += dot(act1, self.grad2)

        def weights1(self):
            d1_ref[...] += dot(jnp.transpose(self.basis[self.half, :]), self.grad1)

    def sweep(now, after):
        steps_of = {
            "H": lambda b: b.hot(), "T": lambda b: b.terms(),
            "0": lambda b: b.spread(0), "1": lambda b: b.spread(1), "2": lambda b: b.spread(2),
            "3": lambda b: b.spread(3), "4": lambda b: b.spread(4),
            "D": lambda b: b.back3(), "G": lambda b: b.grads2(0), "J": lambda b: b.grads2(1),
            "E": lambda b: b.back2(), "F": lambda b: b.grads1(),
            "W": lambda b: b.weights3(), "V": lambda b: b.weights2(), "U": lambda b: b.weights1(),
            "a": lambda b: b.ahead.layer1(), "b": lambda b: b.ahead.active1(),
            "c": lambda b: b.ahead.layer2(), "d": lambda b: b.ahead.active2(0), "p": lambda b: b.ahead.active2(1),
            "e": lambda b: b.ahead.layer3(), "x": lambda b: b.ahead.active3(0),
            "y": lambda b: b.ahead.active3(1), "z": lambda b: b.ahead.active3(2),
        }

        @pl.loop(0, chunks // UNROLL)
        def _(pair):
            if now[0] is net_a:

                for n in range(UNROLL):

                    @pl.when(jnp.logical_and(step == 0, pair * UNROLL + n < AHEAD))
                    def _():
                        for copy in fetch_rest(pair * UNROLL + n):
                            copy.wait()

            both = [Backward(pair * UNROLL + n, now, after) for n in range(UNROLL)]
            for which, name in zip(SCHEDULE[::2], SCHEDULE[1::2]):
                if after is not None or not name.islower():
                    steps_of[name](both[int(which)])

        @pl.loop(0, chunks)
        def _(j):
            @pl.loop(1, win_ref[step * chunks + j, 1])
            def _(w):
                more = scatter_hot(j, w)
                for cs in PAIRS:
                    scatter(now[1], j, more, cs)

    last = step == steps - 1

    @pl.when(jnp.logical_and(even, jnp.logical_not(last)))
    def _():
        sweep((net_a, fac_a, basis_a), (net_b, fac_b, basis_b))

    @pl.when(jnp.logical_not(jnp.logical_or(even, last)))
    def _():
        sweep((net_b, fac_b, basis_b), (net_a, fac_a, basis_a))

    @pl.when(last)
    def _():
        sweep((net_b, fac_b, basis_b), None)
        grads = [None] * 3
        for out, place in (
            (rim_near_ref, near_at), (own_out_ref, halo), (rim_far_ref, far_at)
        ):
            coords = []
            for c in range(9):
                value = spread[pl.ds(place, out.shape[0]), col(c)]
                out[:, col(c)] = value.astype(out.dtype)
                coords.append(value)
            t, s00, s11 = coords[0], coords[7], coords[8]
            right = [3.0 * t] + [2.0 * v for v in coords[1:7]] + [s00, s11, -s00 - s11]
            left = [parts_s[pl.ds(place, out.shape[0]), col(c)] for c in range(10)]
            fresh = [
                dot_first(stack(left[lo:hi]), stack(right[lo:hi]))
                for lo, hi in ((0, 1), (1, 4), (4, 10))
            ]
            grads = [n if o is None else o + n for o, n in zip(grads, fresh)]
        first = d1_ref[:HALF, :LANES] + d1_ref[HALF:, LANES:]
        deep = d3_ref.shape[0] - 16
        thirds = [d3_ref[:deep, col(n)] for n in range(3)]
        biases = [first[BASES : BASES + 1]]
        biases += [d2_ref[LANES : LANES + 1, col(n)] for n in range(2)]
        biases += [d3_ref[deep : deep + 1, col(n)] for n in range(3)]
        biases.append(jnp.zeros((16 - len(biases), LANES), F32))
        biases = jnp.concatenate(biases, axis=0)
        halves = (
            [*thirds, d2_ref[:LANES, col(0)], first[:BASES], biases],
            [*grads, dw2_ref[...], d2_ref[:LANES, col(1)]],
        )

        def put_half(out, values):
            place = 0
            for value in values:
                out[place : place + value.shape[0], :] = value.astype(out.dtype)
                place += value.shape[0]
            out[place:, :] = jnp.zeros((out.shape[0] - place, LANES), out.dtype)

        for side in range(2):

            @pl.when(odd == side)
            def _():
                put_half(mine_ref, halves[side])
                put_half(other_ref, halves[1 - side])


def unpack_kernel(shares, place_ref, mine_ref, other_ref, *out_refs):
    small, (g_w1, g_b1, g_w2, g_b2, g_w3, g_b3) = out_refs[:6], out_refs[6:12]
    mine_s, other_s = out_refs[12:]
    rows = mine_ref.shape[0] // shares
    for n in range(shares):
        to = pl.ds(pl.multiple_of((place_ref[1] ^ n) * rows, 16), rows)
        mine_s[to, :] = mine_ref[n * rows : (n + 1) * rows, :].astype(F32)
        other_s[to, :] = other_ref[n * rows : (n + 1) * rows, :].astype(F32)

    def unpack(one, two):
        deep = g_w3.shape[0]
        for n in range(3):
            g_w3[:, col(n)] = one[n * deep : (n + 1) * deep, :]
        place = 3 * deep
        g_w2[:, col(0)] = one[place : place + LANES, :]
        place += LANES
        g_w1[...] = one[place : place + BASES, :]
        place += BASES
        biases = one[place : place + 16, :]
        row = 0
        for ref in (g_b1, g_b2, g_b3):
            count = ref.shape[0] // LANES
            for n in range(count):
                ref[col(n)] = biases[row + n]
            row += count
        for n, ref in enumerate(small):
            ref[...] = two[n * LANES : (n + 1) * LANES, :]
        g_w2[:, col(1)] = two[6 * LANES : 7 * LANES, :]

    @pl.when(place_ref[0] == 0)
    def _():
        unpack(mine_s, other_s)

    @pl.when(place_ref[0] == 1)
    def _():
        unpack(other_s, mine_s)


def final_kernel(
    own_ref, near_ref, far_ref, atoms_ref, outgrad_ref, iso1_ref, anti1_ref, sym1_ref, out_ref
):
    weights = (iso1_ref[...], anti1_ref[...], sym1_ref[...])
    grad_mixed = [
        own_ref[:, col(c)] + near_ref[:, col(c)].astype(F32) + far_ref[:, col(c)].astype(F32)
        for c in range(9)
    ]
    back = flat(to_matrix(primal_of_dual(back_parts(to_matrix(grad_mixed), weights)[1])))
    values = [atoms_ref[c].astype(F32) for c in range(9)]
    inverse = 1.0 / (1.0 + total([v * v for v in values]))
    grad = [outgrad_ref[c].astype(F32) + back[c] for c in range(9)]
    along = total([g * v for g, v in zip(grad, values)]) * (2.0 * inverse)
    for c in range(9):
        out_ref[c] = (grad[c] - values[c] * along) * inverse


def whole(shape):
    return pl.BlockSpec(shape, lambda *_: (0,) * len(shape), pipeline_mode=pl.Buffered(1))


def block(shape):
    return pl.BlockSpec(shape, lambda i, *_: (i,) + (0,) * (len(shape) - 1))


def shape_of(shape, kind):
    return jax.ShapeDtypeStruct(shape, kind)


def part(value, index):
    return lax.dynamic_index_in_dim(value, index, 0, keepdims=False)


def reduce_everywhere(mine, other, axes, beside):
    beside = list(beside)

    def between(v):
        return beside.pop(0)(v) if beside else v

    peers = math.prod(lax.axis_size(a) for a in axes)
    me = lax.axis_index(axes)
    runs, at = [], 2
    while at < peers:
        runs.append((at, min(4, peers // at)))
        at *= runs[-1][1]
    runs = runs[1:] + runs[:1]

    def swapped(v, by):
        return lax.ppermute(v, axes, [(i, i ^ by) for i in range(peers)])

    value = between(mine + swapped(other, 1).astype(F32))
    for at, size in runs[:-1]:
        shares = value.reshape(size, value.shape[0] // size, value.shape[1])
        own = me // at % size
        kept = part(shares, own)
        for k in range(1, size):
            kept = kept + swapped(part(shares, own ^ k).astype(BF16), k * at).astype(F32)
        value = between(kept)
    at, size = runs[-1]
    value = value.astype(BF16)
    terms = [value] + [swapped(value, k * at) for k in range(1, size)]
    terms[1] = between(terms[1])
    terms = [v.astype(F32) for v in terms]
    while len(terms) > 1:
        terms = [a + b for a, b in zip(terms[::2], terms[1::2])]
    value = between(terms[0].astype(BF16))
    for at, size in runs[-2:0:-1]:
        own = me // at % size
        full = jnp.zeros((size,) + value.shape, value.dtype)
        full = lax.dynamic_update_index_in_dim(full, value, own, 0)
        for k in range(1, size):
            full = lax.dynamic_update_index_in_dim(full, swapped(value, k * at), own ^ k, 0)
        value = full.reshape(size * value.shape[0], value.shape[1])
    at, size = runs[0]
    value = [value] + [swapped(value, k * at) for k in range(1, size)]
    value = between(jnp.concatenate(value, axis=0))
    return value, swapped(value, 1), me // at % size, size


def local(
    atoms, neighbours, live_mask, distances,
    w_iso1, w_anti1, w_sym1, w_rad1, b_rad1, w_rad2, b_rad2, w_rad3, b_rad3,
    w_iso2, w_anti2, w_sym2, out_grad,
):
    rows, _, channels = atoms.shape
    slots = neighbours.shape[1]
    halo = MOL_MOST
    wide = 9 * channels
    ext = rows + 2 * halo
    edges = GROUP * slots
    chunk_count = rows // GROUP
    steps = 4
    chunks = chunk_count // steps
    block_atoms = rows // steps
    block_edges = block_atoms * slots
    vmem = 63 * 1024 * 1024
    me = lax.axis_index(AXES)
    peers = math.prod(lax.axis_size(a) for a in AXES)
    near_pairs = [(i, i ^ 1) for i in range(peers) if i ^ 1 < peers]
    far_pairs = [(i, i + 1 - 2 * (1 - i % 2)) for i in range(1, peers - 1)]

    by_component = jnp.swapaxes(atoms, 0, 1)
    out_grad_by_component = jnp.swapaxes(out_grad, 0, 1)
    near = lax.ppermute(by_component, AXES, near_pairs)
    far = lax.ppermute(by_component, AXES, far_pairs)

    links = neighbours - (me * rows - halo)
    edge_args = [jnp.swapaxes(v, 0, 1) for v in (distances, live_mask, links)]
    edge_specs = [whole(v.shape) for v in edge_args]
    edge_scratch = [pltpu.VMEM((rows, slots), F32)] * 3
    first = jnp.min(jnp.min(links, axis=1).reshape(chunk_count, GROUP), axis=1)
    last = jnp.max(jnp.max(links, axis=1).reshape(chunk_count, GROUP), axis=1)
    count = (last - first) // WINDOW + 1
    windows = jnp.stack([jnp.append(first, me % 2), jnp.append(count, 0)], axis=1)

    mid_width, last_width = w_rad2.shape[1], w_rad3.shape[1]
    small = whole((channels, channels))
    components = pl.BlockSpec((9, block_atoms, channels), lambda i: (0, i, 0))
    smem = pl.BlockSpec(memory_space=pltpu.SMEM)
    net_args = (w_rad1, w_rad2, w_rad3, b_rad1, b_rad2, b_rad3)
    net_specs = [whole(v.shape) for v in net_args]
    net_scratch = [
        pltpu.VMEM((LANES, 2 * channels), BF16),
        pltpu.VMEM((2 * channels, mid_width), BF16),
        pltpu.VMEM((mid_width, last_width), BF16), pltpu.VMEM((1, last_width), F32),
    ]
    net0 = pl.pallas_call(
        network_kernel,
        grid=(AHEAD,),
        in_specs=edge_specs[:2] + net_specs,
        out_specs=[
            block((edges, KEPT)), block((edges, last_width)), block((edges // 2, LANES))
        ],
        out_shape=[
            shape_of((AHEAD * edges, KEPT), BF16), shape_of((AHEAD * edges, last_width), F32),
            shape_of((AHEAD * edges // 2, LANES), BF16),
        ],
        scratch_shapes=edge_scratch[:2] + net_scratch,
        compiler_params=pltpu.CompilerParams(vmem_limit_bytes=vmem),
        cost_estimate=pl.CostEstimate(
            flops=2 * block_edges * 135168, bytes_accessed=block_edges * KEPT * 2, transcendentals=0
        ),
        name="network",
    )(*edge_args[:2], *net_args)

    half_rows = max(3 * mid_width + channels + BASES + 16, 7 * channels)
    half_rows = -(-half_rows // 64) * 64
    updated, rim_near, own_grad, rim_far, mine, other = pl.pallas_call(
        main_kernel,
        grid=(steps,),
        in_specs=[
            smem, whole(near.shape), whole(by_component.shape), whole(far.shape),
            components, *edge_specs, *net_specs,
            small, small, small, small, small, small,
            *[pl.BlockSpec(memory_space=pl.ANY)] * 3,
        ],
        out_specs=[
            components, whole((halo, wide)), whole((rows, wide)), whole((halo, wide)),
            whole((half_rows, channels)), whole((half_rows, channels)),
        ],
        out_shape=[
            shape_of((9, rows, channels), BF16),
            shape_of((halo, wide), BF16), shape_of((rows, wide), F32),
            shape_of((halo, wide), BF16),
            shape_of((half_rows, channels), F32), shape_of((half_rows, channels), BF16),
        ],
        scratch_shapes=[
            pltpu.VMEM((ext + WINDOW, wide), BF16),
            pltpu.VMEM((ext, 10 * channels), BF16),
            pltpu.VMEM((block_edges, KEPT), BF16),
            pltpu.VMEM((block_edges, KEPT), BF16),
            pltpu.VMEM((block_edges, last_width), F32),
            pltpu.VMEM((block_edges, last_width), F32),
            pltpu.VMEM((block_edges // 2, LANES), BF16),
            pltpu.VMEM((block_edges // 2, LANES), BF16),
            pltpu.VMEM((block_edges, wide), BF16),
            pltpu.VMEM((block_atoms, wide), F32),
            pltpu.VMEM((2 * block_atoms, wide + 2 * channels), BF16),
            pltpu.VMEM((ext + WINDOW, wide), F32),
            pltpu.VMEM((mid_width + 16, last_width), F32),
            pltpu.VMEM((channels + 16, mid_width), F32),
            pltpu.VMEM((LANES, 2 * channels), F32),
            pltpu.VMEM((3 * channels, channels), F32),
            *net_scratch,
            *edge_scratch,
            pltpu.SemaphoreType.DMA((AHEAD, 3)),
        ],
        compiler_params=pltpu.CompilerParams(vmem_limit_bytes=vmem),
        name="main",
    )(
        windows, near, by_component, far, out_grad_by_component, *edge_args, *net_args,
        w_iso1, w_anti1, w_sym1, w_iso2, w_anti2, w_sym2, *net0,
    )

    kept = {}

    def nothing(value):
        return value

    def send_rims(value):
        to_near, to_far = rim_near, rim_far
        kept["near"] = lax.ppermute(to_near, AXES, near_pairs)
        kept["far"] = lax.ppermute(to_far, AXES, far_pairs)
        return value

    def have_rims(value):
        value, kept["near"], kept["far"] = lax.optimization_barrier(
            (value, kept["near"], kept["far"])
        )
        return value

    def finish(value):
        grad_atoms = pl.pallas_call(
            final_kernel,
            out_shape=shape_of((9, rows, channels), F32),
            compiler_params=pltpu.CompilerParams(vmem_limit_bytes=24 * 1024 * 1024),
            name="final",
        )(
            own_grad, kept["near"], kept["far"], by_component, out_grad_by_component,
            w_iso1, w_anti1, w_sym1,
        )
        value, updated_out, grad_out = lax.optimization_barrier((value, updated, grad_atoms))
        kept["outs"] = jnp.swapaxes(updated_out, 0, 1), jnp.swapaxes(grad_out, 0, 1)
        return value

    send_rims(mine)
    summed, partner, place, shares = reduce_everywhere(mine, other, AXES, (nothing, nothing, nothing, have_rims, finish))
    square_shape = (channels, channels)
    shapes = [square_shape] * 6 + [w_rad1.shape, (channels,), w_rad2.shape, (mid_width,)]
    shapes += [w_rad3.shape, (last_width,)]
    out = pl.pallas_call(
        functools.partial(unpack_kernel, shares),
        in_specs=[smem, whole(summed.shape), whole(partner.shape)],
        out_shape=[shape_of(shape, F32) for shape in shapes],
        compiler_params=pltpu.CompilerParams(vmem_limit_bytes=16 * 1024 * 1024),
        scratch_shapes=[pltpu.VMEM(summed.shape, F32)] * 2,
        name="unpack",
    )(jnp.stack([me % 2, place]), summed, partner)
    return (*kept["outs"], *out[:3], *out[6:], *out[3:6])


def solution(mesh):
    split3 = P(AXES, None, None)
    split2 = P(AXES, None)
    return jax.shard_map(
        local,
        mesh=mesh,
        in_specs=(split3, split2, split2, split2) + (P(),) * 12 + (split3,),
        out_specs=(split3, split3) + (P(),) * 12,
        check_vma=False,
    )
```
